32 devices in a mesh: batch: 2 (over y), res: 16 (over z, x, core), head: 1.
Axes of the slice: x: 2, y: 2, z: 4, core: 2. Of those that a mesh axis runs over, the one named last changes fastest.
Arguments:
- single: bfloat16 [768, 384], P(('batch', 'res')), parts along dimension 0, may hold values from -50 to 50
- pair: bfloat16 [768, 384, 128], P(('batch', 'res'), 'head'), parts along dimension 0, may hold values from -6 to 6
- rotations: float32 [3, 3, 768], P(None, None, 'batch'), parts along dimension 2, may hold values from -1 to 1, as said below
- translations: float32 [3, 768], P(None, 'batch'), parts along dimension 1, may hold values from -4 to 4
- residue_chain_index: int32 [384], replicated, may hold values from 0 to 3, never falling along the last dimension, each value on 1 to 192 neighbouring positions
- residue_move_mask: int32 [768], P('batch'), parts along dimension 0, may hold values 0 or 1
- timestep: int32 [1], replicated, may hold values from 0 to 6
- single_projection_weight: bfloat16 [384, 16, 132], P(None, 'head'), may hold values from -1 to 1, as said below
- head_bias_weight: bfloat16 [128, 16], replicated, may hold values from -0.5 to 0.5
- head_distance_weight: float32 [16], P('head'), may hold values from 0.1 to 1
- chain_logit_offset: float32 [16], P('head'), may hold values from -2 to 2
- local_output_weight: bfloat16 [16, 64, 384], P('head'), may hold values from -0.109375 to 0.109375
- pair_output_weight: bfloat16 [16, 128, 384], replicated, may hold values from -0.109375 to 0.109375
- single_norm_gain: float32 [384], replicated, may hold values from 0.5 to 1.5
- frame_velocity_weight: bfloat16 [384, 6], replicated, may hold values from -0.3125 to 0.3125
- left_pair_weight: bfloat16 [384, 128], replicated, may hold values from -0.3125 to 0.3125
- right_pair_weight: bfloat16 [384, 128], replicated, may hold values from -0.3125 to 0.3125
- pair_norm_gain: float32 [128], replicated, may hold values from 0.5 to 1.5
- transition_hidden_weight: bfloat16 [128, 256], replicated, may hold values from -0.5 to 0.5
- transition_middle_weight: bfloat16 [256, 256], replicated, may hold values from -0.375 to 0.375
- transition_back_weight: bfloat16 [256, 128], replicated, may hold values from -0.375 to 0.375
Outputs:
- single_out: bfloat16 [768, 384], P(('batch', 'res')), parts along dimension 0
- rot_out: float32 [3, 3, 768], P(None, None, ('batch', 'res')), parts along dimension 2
- trans_out: float32 [3, 768], P(None, ('batch', 'res')), parts along dimension 1
- pair_out: bfloat16 [768, 384, 128], P(('batch', 'res'), 'head'), parts along dimension 0
The draws below stay inside these ranges and needn't reach their ends.
There are 2 independent parts, one for each index of `batch`. The reference program is written for one: setup_inputs(seed, part) draws one part's arguments, and reference() takes and returns one part's arrays. A program takes and returns all parts, laid end to end along the dimension named above; an argument that names none is the same for every part. Nothing has to cross between parts.
Inputs may be any that keep to these rules, and one draw needn't show every extreme that they name: Each residue's 3 x 3 block rotations[:, :, i] is a rotation matrix. `single_projection_weight`: mean zero entries of deviation about 1 / sqrt(384).
All inputs are finite; a program needn't handle non-finite values.
Results may differ from the reference program's by a relative error of at most 0.0044.
The reference program's roundings to bfloat16 on the way count: a program that leaves them out, or rounds other values in their place, can miss the bound.
Values may be sent and summed in bfloat16 or wider, within the bound.
No kernel may reach another device: no remote copies, remote signals or barrier semaphores. Data moves between devices by JAX's collectives and lax.ppermute only.
A program may use at most 64 MiB of HBM per device.

```python
import math
import jax
import jax.numpy as jnp
import numpy as np
from jax import lax

D = 384
HEAD_TOTAL = 16
HEAD_FEATURES = 16
PQ = 8
PV = 12
C_Z = 128
HID = 256
STEPS = 8
RESIDUES = 384
PROJ_FEAT = 132
OUT_FEAT = 64


def draw_single(key, part):
    base = jnp.clip(jax.random.normal(jax.random.fold_in(key, 11), (RESIDUES, D), jnp.float32), -4.0, 4.0)
    return base.astype(jnp.bfloat16)


def axis_turn(angles, axis_name):
    cosine = jnp.cos(angles)
    sine = jnp.sin(angles)
    zeros_row = jnp.zeros_like(angles)
    ones_row = jnp.ones_like(angles)
    if axis_name == 'zaxis':
        return jnp.stack([jnp.stack([cosine, -sine, zeros_row]), jnp.stack([sine, cosine, zeros_row]), jnp.stack([zeros_row, zeros_row, ones_row])])
    return jnp.stack([jnp.stack([cosine, zeros_row, sine]), jnp.stack([zeros_row, ones_row, zeros_row]), jnp.stack([-sine, zeros_row, cosine])])


def draw_rotations(key, part):
    angles = jax.random.uniform(jax.random.fold_in(key, 21), (3, RESIDUES), jnp.float32, -math.pi, math.pi)
    first_turn = axis_turn(angles[0], 'zaxis')
    second_turn = axis_turn(angles[1], 'yaxis')
    third_turn = axis_turn(angles[2], 'zaxis')
    joined = jnp.einsum('abn,bcn->acn', first_turn, second_turn)
    joined = jnp.einsum('abn,bcn->acn', joined, third_turn)
    return jnp.clip(joined, -1.0, 1.0).astype(jnp.float32)


def draw_translations(key, part):
    shifts = jnp.clip(jax.random.normal(jax.random.fold_in(key, 31), (3, RESIDUES), jnp.float32), -4.0, 4.0)
    return shifts.astype(jnp.float32)


def draw_single_projection_weight(key, part):
    span = math.sqrt(3.0 / D)
    weights = jax.random.uniform(jax.random.fold_in(key, 41), (D, HEAD_TOTAL, PROJ_FEAT), jnp.float32, -span, span)
    return weights.astype(jnp.bfloat16)


def with_ends(result, own_key, smallest, high):
    index_at = [jax.random.randint(jax.random.fold_in(own_key, axis), (), 0, length) for axis, length in enumerate(result.shape)]
    longest = result.shape.index(max(result.shape))
    next_to = index_at[:longest] + [(index_at[longest] + 1) % result.shape[longest]] + index_at[longest + 1:]
    return result.at[tuple(index_at)].set(smallest).at[tuple(next_to)].set(high)


def block_levels(rng, shape, split, least, high):
    level = 1.0
    for dim, parts in split:
        draws = jax.random.uniform(jax.random.fold_in(jax.random.fold_in(rng, 6), dim), (parts,), jnp.float32, least / len(split), high / len(split))
        level = level * jnp.repeat(jnp.exp(draws), shape[dim] // parts).reshape((-1,) + (1,) * (len(shape) - 1 - dim))
    return level


def profile(amount, total, limit, lean):
    loads = [(1 << 20) // math.isqrt(grade ** lean) + 1 for grade in range(2, amount + 1)]
    spare, given = total - limit - (amount - 1), [1] * (amount - 1)
    while spare > 0:
        candidates = [i for i in range(amount - 1) if given[i] < limit]
        whole, remaining = sum([loads[i] for i in candidates]), spare
        for i in candidates:
            more = min(limit - given[i], max(1, remaining * loads[i] // whole), spare)
            given[i] = given[i] + more
            spare = spare - more
    return np.array([limit] + given)


def uneven(stream_key, count, total, reach, lean):
    if count == 2:
        one = jax.random.randint(stream_key, (), max(1, total - reach), min(reach, total - 1) + 1)
        return jnp.stack([one, total - one])
    lengths = jnp.asarray(profile(count, total, reach, lean), jnp.int32)
    twos = (count - 1) // 2
    donor, receiver = lengths[1:1 + 2 * twos:2], lengths[2:2 + 2 * twos:2]
    room = jnp.minimum(donor - 1, reach - receiver)
    shifted = jax.random.randint(jax.random.fold_in(stream_key, 1), (twos,), 0, 1 << 20) % (room + 1)
    lengths = lengths.at[1:1 + 2 * twos:2].set(donor - shifted).at[2:2 + 2 * twos:2].set(receiver + shifted)
    return lengths[jax.random.permutation(jax.random.fold_in(stream_key, 2), count)]


def normal_values(own_key, shape, deviation, bound, pieces=(), kind=jnp.bfloat16):
    level = block_levels(own_key, shape, pieces, -0.22, 0.18) if pieces else 1.0
    values = jax.random.normal(own_key, shape, jnp.float32) * deviation * level
    return jnp.minimum(jnp.maximum(values, -bound), bound).astype(kind)


def setup_inputs(seed: int = 0, part: int = 0) -> dict:
    key_of = jax.random.split(jax.random.key(seed), 22)
    part_splits = jax.random.split(jax.random.fold_in(key_of[21], part), 22)
    single = draw_single(jax.random.fold_in(jax.random.fold_in(key_of[21], part), 71), part)
    pair = normal_values(part_splits[1], (RESIDUES, RESIDUES, C_Z), 1.0, 6.0, ((0, 16),))
    rotations = draw_rotations(jax.random.fold_in(jax.random.fold_in(key_of[21], part), 71), part)
    translations = draw_translations(jax.random.fold_in(jax.random.fold_in(key_of[21], part), 71), part)
    residue_chain_index = jnp.searchsorted(jnp.cumsum(uneven(key_of[4], 4, RESIDUES, RESIDUES // 2, 0)), jnp.arange(RESIDUES), side="right").astype(jnp.int32)
    residue_move_mask = with_ends((jax.random.randint(part_splits[5], (RESIDUES,), 0, 8) < 7).astype(jnp.int32), jax.random.fold_in(part_splits[5], 1), 0, 1)
    timestep = jax.random.randint(key_of[6], (1,), 0, STEPS - 1).astype(jnp.int32)
    single_projection_weight = draw_single_projection_weight(jax.random.fold_in(key_of[21], 71), part)
    head_bias_weight = normal_values(key_of[8], (C_Z, HEAD_TOTAL), C_Z ** -0.5, 0.5)
    head_distance_weight = jnp.clip(jnp.exp(jax.random.uniform(key_of[9], (HEAD_TOTAL,), jnp.float32, math.log(0.1), math.log(1.0))), 0.1, 1.0)
    chain_logit_offset = jnp.clip(jax.random.uniform(key_of[10], (HEAD_TOTAL,), jnp.float32, -2.0, 2.0), -2.0, 2.0)
    local_output_weight = normal_values(key_of[11], (HEAD_TOTAL, OUT_FEAT, D), (HEAD_TOTAL * (OUT_FEAT + C_Z)) ** -0.5, 0.109375)
    pair_output_weight = normal_values(key_of[12], (HEAD_TOTAL, C_Z, D), (HEAD_TOTAL * (OUT_FEAT + C_Z)) ** -0.5, 0.109375)
    single_norm_gain = jnp.clip(1.0 + 0.1 * jax.random.normal(key_of[13], (D,), jnp.float32), 0.5, 1.5)
    frame_velocity_weight = normal_values(key_of[14], (D, 6), D ** -0.5, 0.3125)
    left_pair_weight = normal_values(key_of[15], (D, C_Z), D ** -0.5, 0.3125)
    right_pair_weight = normal_values(key_of[16], (D, C_Z), D ** -0.5, 0.3125)
    pair_norm_gain = jnp.clip(1.0 + 0.1 * jax.random.normal(key_of[17], (C_Z,), jnp.float32), 0.5, 1.5)
    transition_hidden_weight = normal_values(key_of[18], (C_Z, HID), C_Z ** -0.5, 0.5)
    transition_middle_weight = normal_values(key_of[19], (HID, HID), HID ** -0.5, 0.375)
    transition_back_weight = normal_values(key_of[20], (HID, C_Z), HID ** -0.5, 0.375)
    return {"single": single, "pair": pair, "rotations": rotations, "translations": translations, "residue_chain_index": residue_chain_index, "residue_move_mask": residue_move_mask, "timestep": timestep, "single_projection_weight": single_projection_weight, "head_bias_weight": head_bias_weight, "head_distance_weight": head_distance_weight, "chain_logit_offset": chain_logit_offset, "local_output_weight": local_output_weight, "pair_output_weight": pair_output_weight, "single_norm_gain": single_norm_gain, "frame_velocity_weight": frame_velocity_weight, "left_pair_weight": left_pair_weight, "right_pair_weight": right_pair_weight, "pair_norm_gain": pair_norm_gain, "transition_hidden_weight": transition_hidden_weight, "transition_middle_weight": transition_middle_weight, "transition_back_weight": transition_back_weight}


LOGIT_FACTOR = math.sqrt(1.0 / 3.0)
HIGHEST = lax.Precision.HIGHEST

def rounded(values):
    return lax.optimization_barrier(values.astype(jnp.bfloat16))

def layer_norm(values, gain):
    centre = lax.optimization_barrier(jnp.mean(values, axis=-1, keepdims=True))
    variance = lax.optimization_barrier(jnp.mean(jnp.square(values - centre), axis=-1, keepdims=True))
    return (values - centre) * lax.rsqrt(variance + 1e-05) * gain

def to_global(local, rot_cols, trans_cols, npoints):
    rows_here = local.shape[0]
    heads_here = local.shape[1]
    points = local.reshape(rows_here, heads_here, npoints, 3)
    turned = lax.optimization_barrier(jnp.sum(rot_cols[:, None, None, :, :] * points[:, :, :, None, :], axis=-1))
    return turned + trans_cols[:, None, None, :]

def hat_matrix(vectors):
    comp_x = vectors[:, 0]
    comp_y = vectors[:, 1]
    comp_z = vectors[:, 2]
    zeros_col = jnp.zeros_like(comp_x)
    first_row = jnp.stack([zeros_col, -comp_z, comp_y], -1)
    second_row = jnp.stack([comp_z, zeros_col, -comp_x], -1)
    third_row = jnp.stack([-comp_y, comp_x, zeros_col], -1)
    return jnp.stack([first_row, second_row, third_row], 1)

def frame_step(single_out, frame_velocity_weight, rot_cols, trans_cols, live_rows, step_ratio):
    motion = jnp.dot(single_out, frame_velocity_weight, preferred_element_type=jnp.float32)
    rotvec = step_ratio * jnp.tanh(motion[:, 0:3]) * live_rows[:, None]
    velocity = step_ratio * motion[:, 3:6] * live_rows[:, None]
    angle_sq = lax.optimization_barrier(jnp.sum(jnp.square(rotvec), -1))
    coef_a = jnp.zeros_like(angle_sq)
    coef_b = jnp.zeros_like(angle_sq)
    coef_c = jnp.zeros_like(angle_sq)
    powers = jnp.ones_like(angle_sq)
    for order in range(8):
        parity = (-1.0) ** order
        coef_a = coef_a + powers * (parity / float(math.factorial(2 * order + 1)))
        coef_b = coef_b + powers * (parity / float(math.factorial(2 * order + 2)))
        coef_c = coef_c + powers * (parity / float(math.factorial(2 * order + 3)))
        powers = powers * angle_sq
    cross_mat = hat_matrix(rotvec)
    cross_sq = jnp.einsum('nab,nbc->nac', cross_mat, cross_mat, precision=HIGHEST)
    identity = jnp.eye(3, dtype=jnp.float32)[None]
    turn = identity + coef_a[:, None, None] * cross_mat + coef_b[:, None, None] * cross_sq
    jacobian = identity + coef_b[:, None, None] * cross_mat + coef_c[:, None, None] * cross_sq
    new_rot = jnp.einsum('nab,nbc->nac', rot_cols, turn, precision=HIGHEST)
    moved = jnp.einsum('nab,nb->na', jacobian, velocity, precision=HIGHEST)
    new_trans = trans_cols + jnp.einsum('nab,nb->na', rot_cols, moved, precision=HIGHEST)
    return (jnp.transpose(new_rot, (1, 2, 0)), jnp.transpose(new_trans))

def reference(single, pair, rotations, translations, residue_chain_index, residue_move_mask, timestep, single_projection_weight, head_bias_weight, head_distance_weight, chain_logit_offset, local_output_weight, pair_output_weight, single_norm_gain, frame_velocity_weight, left_pair_weight, right_pair_weight, pair_norm_gain, transition_hidden_weight, transition_middle_weight, transition_back_weight):
    rot_cols = jnp.transpose(rotations, (2, 0, 1))
    trans_cols = jnp.transpose(translations)
    projected = jnp.einsum('nd,dhf->nhf', single.astype(jnp.float32), single_projection_weight.astype(jnp.float32), precision=HIGHEST)
    query_values = rounded(projected[:, :, 0:HEAD_FEATURES])
    key_float = rounded(projected[:, :, HEAD_FEATURES:2 * HEAD_FEATURES]).astype(jnp.float32)
    value_float = rounded(projected[:, :, 2 * HEAD_FEATURES:3 * HEAD_FEATURES]).astype(jnp.float32)
    offset = 3 * HEAD_FEATURES
    query_points = to_global(projected[:, :, offset:offset + 3 * PQ], rot_cols, trans_cols, PQ)
    key_points = rounded(to_global(projected[:, :, offset + 3 * PQ:offset + 6 * PQ], rot_cols, trans_cols, PQ))
    value_points = rounded(to_global(projected[:, :, offset + 6 * PQ:], rot_cols, trans_cols, PV))
    key_flat = key_points.astype(jnp.float32).reshape(RESIDUES, HEAD_TOTAL, 3 * PQ)
    value_flat = value_points.astype(jnp.float32).reshape(RESIDUES, HEAD_TOTAL, 3 * PV)
    key_square = jnp.transpose(lax.optimization_barrier(jnp.sum(jnp.square(key_flat), -1)))
    key_present = residue_move_mask > 0
    point_term_weight = math.sqrt(2.0 / (9.0 * PQ))
    block_rows = math.gcd(RESIDUES, 128)
    block_count = RESIDUES // block_rows

    def attend(args):
        query_rows, qpoint_rows, pair_rows, rot_rows, trans_rows, chain_rows = args
        scalar_logit_term = jnp.einsum('rhc,nhc->rhn', query_rows.astype(jnp.float32), key_float, precision=HIGHEST)
        query_flattened = qpoint_rows.reshape(block_rows, HEAD_TOTAL, 3 * PQ)
        cross_term = jnp.einsum('rhp,nhp->rhn', query_flattened, key_flat, precision=HIGHEST)
        point_distance = lax.optimization_barrier(jnp.sum(jnp.square(query_flattened), -1))[:, :, None] + key_square[None] - 2.0 * cross_term
        pair_float = pair_rows.astype(jnp.float32)
        pair_head_bias = rounded(jnp.einsum('rjc,ch->rhj', pair_float, head_bias_weight.astype(jnp.float32), precision=HIGHEST))
        within_chain = (chain_rows[:, None] == residue_chain_index[None, :]).astype(jnp.float32)
        logit_matrix = LOGIT_FACTOR * (scalar_logit_term / math.sqrt(HEAD_FEATURES) + pair_head_bias.astype(jnp.float32) + chain_logit_offset[None, :, None] * within_chain[:, None, :] - (0.5 * point_term_weight * head_distance_weight)[None, :, None] * point_distance)
        logit_matrix = jnp.where(key_present[None, None, :], logit_matrix, -1000000000.0)
        weights = jax.nn.softmax(logit_matrix, axis=-1)
        attention = rounded(weights).astype(jnp.float32)
        scalar_out = jnp.einsum('rhn,nhc->rhc', attention, value_float, precision=HIGHEST)
        point_global = jnp.einsum('rhn,nhp->rhp', attention, value_flat, precision=HIGHEST).reshape(block_rows, HEAD_TOTAL, PV, 3)
        centred = point_global - trans_rows[:, None, None, :]
        point_local = lax.optimization_barrier(jnp.sum(rot_rows[:, None, None, :, :] * centred[:, :, :, :, None], axis=-2))
        point_norm = jnp.sqrt(lax.optimization_barrier(jnp.sum(jnp.square(point_local), -1)) + 1.0)
        pair_attended = jnp.einsum('rhj,rjc->rhc', attention, pair_float, precision=HIGHEST)
        features = jnp.concatenate([scalar_out, point_local.reshape(block_rows, HEAD_TOTAL, 3 * PV), point_norm], -1)
        first_part = jnp.einsum('rhf,hfd->rd', features, local_output_weight.astype(jnp.float32), precision=HIGHEST)
        second_part = jnp.einsum('rhc,hcd->rd', pair_attended, pair_output_weight.astype(jnp.float32), precision=HIGHEST)
        return first_part + second_part
    update = lax.map(attend, (query_values.reshape(block_count, block_rows, HEAD_TOTAL, HEAD_FEATURES), query_points.reshape(block_count, block_rows, HEAD_TOTAL, PQ, 3), pair.reshape(block_count, block_rows, RESIDUES, C_Z), rot_cols.reshape(block_count, block_rows, 3, 3), trans_cols.reshape(block_count, block_rows, 3), residue_chain_index.reshape(block_count, block_rows))).reshape(RESIDUES, D)
    single_out = rounded(layer_norm(single.astype(jnp.float32) + update, single_norm_gain))
    live_all = (residue_move_mask > 0).astype(jnp.float32)
    step_ratio = 1.0 / (STEPS - timestep[0]).astype(jnp.float32)
    rot_out, trans_out = frame_step(single_out, frame_velocity_weight, rot_cols, trans_cols, live_all, step_ratio)
    left_proj = rounded(jnp.dot(single_out, left_pair_weight, preferred_element_type=jnp.float32))
    right_float = rounded(jnp.dot(single_out, right_pair_weight, preferred_element_type=jnp.float32)).astype(jnp.float32)
    pair_block = math.gcd(RESIDUES, 32)
    pair_count = RESIDUES // pair_block

    def transition(args):
        pair_rows, left_rows, live_rows = args
        summed = pair_rows.astype(jnp.float32) + left_rows.astype(jnp.float32)[:, None, :] + right_float[None]
        normed = rounded(layer_norm(summed, pair_norm_gain)).astype(jnp.float32)
        hidden_one = rounded(jax.nn.relu(jnp.einsum('rjc,ck->rjk', normed, transition_hidden_weight.astype(jnp.float32), precision=HIGHEST))).astype(jnp.float32)
        hidden_two = rounded(jax.nn.relu(jnp.einsum('rjc,ck->rjk', hidden_one, transition_middle_weight.astype(jnp.float32), precision=HIGHEST))).astype(jnp.float32)
        branch = jnp.einsum('rjk,kc->rjc', hidden_two, transition_back_weight.astype(jnp.float32), precision=HIGHEST)
        pair_live = (live_rows[:, None] * live_all[None, :])[:, :, None]
        return rounded(pair_rows.astype(jnp.float32) + pair_live * branch)
    pair_out = lax.map(transition, (pair.reshape(pair_count, pair_block, RESIDUES, C_Z), left_proj.reshape(pair_count, pair_block, C_Z), live_all.reshape(pair_count, pair_block))).reshape(RESIDUES, RESIDUES, C_Z)
    return (single_out, rot_out, trans_out, pair_out)
```

```python
import functools
import math

import jax
import jax.numpy as jnp
from jax import lax
from jax.experimental import pallas as pl
from jax.experimental.pallas import tpu as pltpu
from jax.sharding import PartitionSpec as P

HEAD_FEATURES = 16
PQ = 8
PV = 12
STEPS = 8


LOGIT_FACTOR = math.sqrt(1.0 / 3.0)
HIGHEST = lax.Precision.HIGHEST


def rounded(values):
    return lax.optimization_barrier(values.astype(jnp.bfloat16))


def layer_norm(values, gain):
    centre = jnp.mean(values, axis=-1, keepdims=True)
    variance = jnp.mean(jnp.square(values - centre), axis=-1, keepdims=True)
    return (values - centre) * lax.rsqrt(variance + 1e-05) * gain


def to_global(local, rot_cols, trans_cols, npoints):
    rows_here = local.shape[0]
    heads_here = local.shape[1]
    points = local.reshape(rows_here, heads_here, npoints, 3)
    turned = jnp.sum(rot_cols[:, None, None, :, :] * points[:, :, :, None, :], axis=-1)
    return turned + trans_cols[:, None, None, :]


def key_features(projected, rot_cols, trans_cols):
    rows_here = projected.shape[0]
    heads_here = projected.shape[1]
    offset = 3 * HEAD_FEATURES
    key_points = to_global(
        projected[:, :, offset + 3 * PQ : offset + 6 * PQ], rot_cols, trans_cols, PQ
    )
    value_points = to_global(projected[:, :, offset + 6 * PQ :], rot_cols, trans_cols, PV)
    packed_projection = jnp.concatenate(
        [
            projected[:, :, HEAD_FEATURES : 3 * HEAD_FEATURES],
            key_points.reshape(rows_here, heads_here, 3 * PQ),
            value_points.reshape(rows_here, heads_here, 3 * PV),
        ],
        axis=-1,
    )
    return rounded(
        packed_projection.reshape(rows_here, heads_here * (2 * HEAD_FEATURES + 3 * PQ + 3 * PV))
    )


def hat_matrix(vectors):
    comp_x = vectors[:, 0]
    comp_y = vectors[:, 1]
    comp_z = vectors[:, 2]
    zeros_col = jnp.zeros_like(comp_x)
    first_row = jnp.stack([zeros_col, -comp_z, comp_y], -1)
    second_row = jnp.stack([comp_z, zeros_col, -comp_x], -1)
    third_row = jnp.stack([-comp_y, comp_x, zeros_col], -1)
    return jnp.stack([first_row, second_row, third_row], 1)


def frame_step(single_out, frame_velocity_weight, rot_cols, trans_cols, live_rows, step_ratio):
    motion = jnp.dot(single_out, frame_velocity_weight, preferred_element_type=jnp.float32)
    rotvec = step_ratio * jnp.tanh(motion[:, 0:3]) * live_rows[:, None]
    velocity = step_ratio * motion[:, 3:6] * live_rows[:, None]
    angle_sq = jnp.sum(jnp.square(rotvec), -1)
    coef_a = jnp.zeros_like(angle_sq)
    coef_b = jnp.zeros_like(angle_sq)
    coef_c = jnp.zeros_like(angle_sq)
    powers = jnp.ones_like(angle_sq)
    for order in range(8):
        parity = (-1.0) ** order
        coef_a = coef_a + powers * (parity / float(math.factorial(2 * order + 1)))
        coef_b = coef_b + powers * (parity / float(math.factorial(2 * order + 2)))
        coef_c = coef_c + powers * (parity / float(math.factorial(2 * order + 3)))
        powers = powers * angle_sq
    cross_mat = hat_matrix(rotvec)
    cross_sq = jnp.einsum("nab,nbc->nac", cross_mat, cross_mat, precision=HIGHEST)
    identity = jnp.eye(3, dtype=jnp.float32)[None]
    turn = identity + coef_a[:, None, None] * cross_mat + coef_b[:, None, None] * cross_sq
    jacobian = identity + coef_b[:, None, None] * cross_mat + coef_c[:, None, None] * cross_sq
    new_rot = jnp.einsum("nab,nbc->nac", rot_cols, turn, precision=HIGHEST)
    moved = jnp.einsum("nab,nb->na", jacobian, velocity, precision=HIGHEST)
    new_trans = trans_cols + jnp.einsum("nab,nb->na", rot_cols, moved, precision=HIGHEST)
    return (jnp.transpose(new_rot, (1, 2, 0)), jnp.transpose(new_trans))


def local_logit_rows(
    query_values,
    query_flattened,
    packed_projection,
    pair_head_bias,
    within_chain,
    distance_weight,
    chain_offset,
    key_present,
):
    key_scalar = packed_projection[:, :, 0:HEAD_FEATURES]
    key_flat = packed_projection[:, :, 2 * HEAD_FEATURES : 2 * HEAD_FEATURES + 3 * PQ].astype(
        jnp.float32
    )
    scalar_logit_term = jnp.einsum(
        "rhc,nhc->rhn", query_values, key_scalar, preferred_element_type=jnp.float32
    )
    cross_term = jnp.einsum("rhp,nhp->rhn", query_flattened, key_flat, precision=HIGHEST)
    key_square = jnp.transpose(jnp.sum(jnp.square(key_flat), -1))
    point_distance = (
        jnp.sum(jnp.square(query_flattened), -1)[:, :, None] + key_square[None] - 2.0 * cross_term
    )
    point_term_weight = math.sqrt(2.0 / (9.0 * PQ))
    logit_matrix = LOGIT_FACTOR * (
        scalar_logit_term / math.sqrt(HEAD_FEATURES)
        + pair_head_bias
        + chain_offset[None, :, None] * within_chain[:, None, :]
        - (0.5 * point_term_weight * distance_weight)[None, :, None] * point_distance
    )
    return jnp.where(key_present[None, None, :], logit_matrix, -1000000000.0)


def local_points(scalar_out, point_global, rot_own, trans_own, local_output_weight):
    rows_dev = scalar_out.shape[0]
    heads_here = scalar_out.shape[1]
    point_global = point_global.reshape(rows_dev, heads_here, PV, 3)
    centred = point_global - trans_own[:, None, None, :]
    point_local = jnp.sum(rot_own[:, None, None, :, :] * centred[:, :, :, :, None], axis=-2)
    point_norm = jnp.sqrt(jnp.sum(jnp.square(point_local), -1) + 1.0)
    features = jnp.concatenate(
        [scalar_out, point_local.reshape(rows_dev, heads_here, 3 * PV), point_norm], -1
    )
    return jnp.einsum(
        "rhf,hfd->rd", features, local_output_weight.astype(jnp.float32), precision=HIGHEST
    )


def exchange(block, count, step):
    return lax.ppermute(block, "res", [(k, k ^ step) for k in range(count)])


def gather_blocks(block, count):
    if count < 16 or count & (count - 1):
        whole = lax.all_gather(block, "res", axis=0)
        return None, whole
    held, offsets = block[None], [0]
    quarter = count // 4
    step = quarter // 2
    while step > 1:
        held = jnp.concatenate([held, exchange(held, count, step)], 0)
        offsets = offsets + [o ^ step for o in offsets]
        step //= 2
    parts = [held] + [exchange(held, count, k * quarter) for k in (3, 2, 1)]
    held = jnp.concatenate(parts, 0)
    offsets = [o ^ (k * quarter) for k in (0, 3, 2, 1) for o in offsets]
    other = exchange(held, count, 1)
    return offsets, (held, other)


def sorted_blocks(offsets, blocks):
    if offsets is None:
        return blocks
    held, other = blocks
    entries = [held[e] for e in range(len(offsets))] + [other[e] for e in range(len(offsets))]
    every = dict(zip(offsets + [o ^ 1 for o in offsets], entries))
    both = jnp.stack([every[o] for o in range(len(every))])
    index = lax.axis_index("res")
    bit = 1
    while bit < len(every):
        halves = both.reshape((-1, 2, bit) + held.shape[1:])
        both = jnp.where((index & bit) > 0, halves[:, ::-1], halves).reshape(both.shape)
        bit *= 2
    return both


def transition_kernel(
    rows_block,
    rows_dev,
    offsets,
    live_ref,
    pair_ref,
    left_ref,
    live_row_ref,
    gain_ref,
    hidden_ref,
    middle_ref,
    back_ref,
    *rest,
):
    block_refs, (out_ref, right_ref, live_cols_ref, centring_ref) = rest[:-4], rest[-4:]
    step = pl.program_id(0)
    cols, feats = pair_ref.shape[1:]
    me = lax.axis_index("res")
    col_start = lax.axis_index("head") * cols

    @pl.when(step == 0)
    def _():
        at = 0
        for ref in block_refs:
            for e in range(ref.shape[0]):
                value = ref[e].astype(jnp.float32)
                value = value - jnp.mean(value, axis=-1, keepdims=True)
                owner = me ^ offsets[at] if offsets is not None else at
                at += 1
                right_ref[pl.ds(pl.multiple_of(owner * rows_dev, 8), rows_dev), :] = value
        wide = jnp.broadcast_to(live_row_ref[...].astype(jnp.float32), (feats, live_row_ref.shape[1]))
        live_cols_ref[...] = jnp.where(jnp.transpose(wide) > 0, 1.0, 0.0)
        across = lax.broadcasted_iota(jnp.int32, (feats, feats), 0)
        down = lax.broadcasted_iota(jnp.int32, (feats, feats), 1)
        centring_ref[...] = (jnp.where(across == down, 1.0, 0.0) - 1.0 / feats).astype(jnp.bfloat16)

    columns = pl.ds(pl.multiple_of(col_start, 8), cols)
    pair = pair_ref[...].reshape(rows_block * cols, feats)
    centred = jnp.dot(pair, centring_ref[...], preferred_element_type=jnp.float32)
    left = left_ref[...].astype(jnp.float32)
    left = left - jnp.mean(left, axis=-1, keepdims=True)
    centred = centred.reshape(rows_block, cols, feats) + left[:, None, :] + right_ref[columns, :][None]
    centred = centred.reshape(rows_block * cols, feats)
    averaging = jnp.full((feats, feats), 1.0 / feats, jnp.bfloat16)
    variance = jnp.dot(
        (centred * centred).astype(jnp.bfloat16), averaging, preferred_element_type=jnp.float32
    )
    normed = (centred * lax.rsqrt(variance + 1e-05) * gain_ref[...]).astype(jnp.bfloat16)
    hidden_one = jnp.maximum(
        jnp.dot(normed, hidden_ref[...], preferred_element_type=jnp.float32).astype(jnp.bfloat16), 0
    )
    hidden_two = jnp.maximum(
        jnp.dot(hidden_one, middle_ref[...], preferred_element_type=jnp.float32).astype(
            jnp.bfloat16
        ),
        0,
    )
    branch = jnp.dot(hidden_two, back_ref[...], preferred_element_type=jnp.float32)
    branch = branch.reshape(rows_block, cols, feats)
    live_cols = live_cols_ref[columns, :]
    for r in range(rows_block):
        live = jnp.where(live_ref[me * rows_dev + step * rows_block + r] > 0, 1.0, 0.0)
        out_ref[r] = (
            pair_ref[r].astype(jnp.float32) + live * live_cols * branch[r]
        ).astype(jnp.bfloat16)


def pair_transition(
    pair, left_proj, move_mask, gain, hidden, middle, back, offsets, blocks
):
    rows_dev, cols, feats = pair.shape
    total = move_mask.shape[0]
    rows_block = math.gcd(rows_dev, max(1, 1536 // cols))
    left_wide = left_proj.reshape(rows_dev // rows_block, rows_block, feats)
    whole = lambda *shape: pl.BlockSpec(shape, lambda i: (0,) * len(shape))
    kernel = functools.partial(transition_kernel, rows_block, rows_dev, offsets)
    macs = rows_dev * cols * (2 * feats * feats + 2 * feats * hidden.shape[1] + hidden.shape[1] ** 2)
    return pl.pallas_call(
        kernel,
        grid=(rows_dev // rows_block,),
        in_specs=[
            pl.BlockSpec(memory_space=pltpu.SMEM),
            pl.BlockSpec((rows_block, cols, feats), lambda i: (i, 0, 0)),
            pl.BlockSpec((None, rows_block, feats), lambda i: (i, 0, 0)),
            whole(1, total),
            whole(1, feats),
            whole(*hidden.shape),
            whole(*middle.shape),
            whole(*back.shape),
        ]
        + [whole(*b.shape) for b in blocks],
        out_specs=pl.BlockSpec((rows_block, cols, feats), lambda i: (i, 0, 0)),
        out_shape=jax.ShapeDtypeStruct(pair.shape, pair.dtype),
        scratch_shapes=[
            pltpu.VMEM((total, feats), jnp.float32),
            pltpu.VMEM((total, feats), jnp.float32),
            pltpu.VMEM((feats, feats), jnp.bfloat16),
        ],
        compiler_params=pltpu.CompilerParams(vmem_limit_bytes=48 * 1024 * 1024),
        cost_estimate=pl.CostEstimate(
            flops=2 * macs, bytes_accessed=2 * pair.size * 2, transcendentals=0
        ),
    )(
        move_mask,
        pair,
        left_wide,
        move_mask[None],
        gain[None],
        hidden,
        middle,
        back,
        *blocks,
    )


def shards(
    single,
    pair,
    rotations,
    translations,
    residue_chain_index,
    residue_move_mask,
    timestep,
    single_projection_weight,
    head_bias_weight,
    head_distance_weight,
    chain_logit_offset,
    local_output_weight,
    pair_output_weight,
    single_norm_gain,
    frame_velocity_weight,
    left_pair_weight,
    right_pair_weight,
    pair_norm_gain,
    transition_hidden_weight,
    transition_middle_weight,
    transition_back_weight,
):
    rows_dev = single.shape[0]
    col_count = pair.shape[1]
    total = rotations.shape[2]
    heads_here = single_projection_weight.shape[1]
    row_start = lax.axis_index("res") * rows_dev
    rot_all = jnp.transpose(rotations, (2, 0, 1))
    trans_all = jnp.transpose(translations)
    rot_own = lax.dynamic_slice_in_dim(rot_all, row_start, rows_dev, 0)
    trans_own = lax.dynamic_slice_in_dim(trans_all, row_start, rows_dev, 0)
    own_chain = lax.dynamic_slice_in_dim(residue_chain_index, row_start, rows_dev, 0)
    offset = 3 * HEAD_FEATURES
    feat_count = 2 * HEAD_FEATURES + 3 * PQ + 3 * PV
    count = total // rows_dev
    every_single = sorted_blocks(*gather_blocks(single, count)).reshape(total, -1)
    every_proj = jnp.einsum(
        "nd,dhf->nhf", every_single, single_projection_weight, preferred_element_type=jnp.float32
    )
    projected = lax.dynamic_slice_in_dim(every_proj, row_start, rows_dev, 0)
    packed_projection = key_features(every_proj, rot_all, trans_all)
    packed_projection = packed_projection.reshape(total, heads_here, feat_count)
    query_values = projected[:, :, 0:HEAD_FEATURES].astype(jnp.bfloat16)
    query_flattened = to_global(
        projected[:, :, offset : offset + 3 * PQ], rot_own, trans_own, PQ
    ).reshape(rows_dev, heads_here, 3 * PQ)
    bias_local = jnp.einsum(
        "rjc,ch->rhj", pair, head_bias_weight, preferred_element_type=jnp.float32
    ).astype(jnp.bfloat16)
    pair_head_bias = lax.all_to_all(
        bias_local, "head", split_axis=1, concat_axis=2, tiled=True
    ).astype(jnp.float32)
    within_chain = (own_chain[:, None] == residue_chain_index[None, :]).astype(jnp.float32)
    logit_matrix = local_logit_rows(
        query_values,
        query_flattened,
        packed_projection,
        pair_head_bias,
        within_chain,
        head_distance_weight,
        chain_logit_offset,
        residue_move_mask > 0,
    )
    peak = jnp.max(logit_matrix, axis=-1, keepdims=True)
    exponent = jnp.exp(logit_matrix - peak)
    attention = rounded(exponent / jnp.sum(exponent, axis=-1, keepdims=True))
    scalar_out = jnp.einsum(
        "rhn,nhc->rhc",
        attention,
        packed_projection[:, :, HEAD_FEATURES : 2 * HEAD_FEATURES],
        preferred_element_type=jnp.float32,
    )
    point_global = jnp.einsum(
        "rhn,nhp->rhp",
        attention.astype(jnp.float32),
        packed_projection[:, :, 2 * HEAD_FEATURES + 3 * PQ :].astype(jnp.float32),
        precision=HIGHEST,
    )
    update_local = local_points(scalar_out, point_global, rot_own, trans_own, local_output_weight)
    attention_cols = lax.all_to_all(attention, "head", split_axis=2, concat_axis=1, tiled=True)
    pair_attended = jnp.einsum(
        "rhj,rjc->rhc", attention_cols, pair, preferred_element_type=jnp.float32
    )
    update_pair = jnp.einsum(
        "rhc,hcd->rd", pair_attended, pair_output_weight.astype(jnp.float32), precision=HIGHEST
    )
    update = lax.psum(update_local + update_pair, "head")
    single_out = layer_norm(single.astype(jnp.float32) + update, single_norm_gain).astype(
        jnp.bfloat16
    )
    live_all = (residue_move_mask > 0).astype(jnp.float32)
    live_own = lax.dynamic_slice_in_dim(live_all, row_start, rows_dev, 0)
    step_ratio = 1.0 / (STEPS - timestep[0]).astype(jnp.float32)
    rot_out, trans_out = frame_step(
        single_out, frame_velocity_weight, rot_own, trans_own, live_own, step_ratio
    )
    left_proj = jnp.dot(single_out, left_pair_weight, preferred_element_type=jnp.float32).astype(
        jnp.bfloat16
    )
    right_proj = jnp.dot(single_out, right_pair_weight, preferred_element_type=jnp.float32).astype(
        jnp.bfloat16
    )
    offsets, blocks = gather_blocks(right_proj, count)
    if offsets is None:
        blocks = (blocks,)
    else:
        offsets = offsets + [o ^ 1 for o in offsets]
    pair_out = pair_transition(
        pair,
        left_proj,
        residue_move_mask,
        pair_norm_gain,
        transition_hidden_weight,
        transition_middle_weight,
        transition_back_weight,
        offsets,
        blocks,
    )
    return (single_out, rot_out, trans_out, pair_out)


def solution(mesh):
    placed = (
        P(("batch", "res"), None),
        P(("batch", "res"), "head", None),
        P(None, None, "batch"),
        P(None, "batch"),
        P(),
        P("batch"),
        P(),
        P(None, "head", None),
        P(),
        P("head"),
        P("head"),
        P("head", None, None),
        P(),
        P(),
        P(),
        P(),
        P(),
        P(),
        P(),
        P(),
        P(),
    )
    return jax.shard_map(
        shards,
        mesh=mesh,
        in_specs=placed,
        out_specs=(
            P(("batch", "res"), None),
            P(None, None, ("batch", "res")),
            P(None, ("batch", "res")),
            P(("batch", "res"), "head", None),
        ),
        check_vma=False,
    )
```

```python
import functools
import math

import jax
import jax.numpy as jnp
from jax import lax
from jax.experimental import pallas as pl
from jax.experimental.pallas import tpu as pltpu
from jax.sharding import PartitionSpec as P

HEAD_FEATURES = 16
PQ = 8
PV = 12
STEPS = 8


LOGIT_FACTOR = math.sqrt(1.0 / 3.0)
HIGHEST = lax.Precision.HIGHEST


def rounded(values):
    return lax.optimization_barrier(values.astype(jnp.bfloat16))


def layer_norm(values, gain):
    centre = jnp.mean(values, axis=-1, keepdims=True)
    variance = jnp.mean(jnp.square(values - centre), axis=-1, keepdims=True)
    return (values - centre) * lax.rsqrt(variance + 1e-05) * gain


def to_global(local, rot_cols, trans_cols, npoints):
    rows_here = local.shape[0]
    heads_here = local.shape[1]
    points = local.reshape(rows_here, heads_here, npoints, 3)
    turned = jnp.sum(rot_cols[:, None, None, :, :] * points[:, :, :, None, :], axis=-1)
    return turned + trans_cols[:, None, None, :]


def key_features(projected, rot_cols, trans_cols):
    rows_here = projected.shape[0]
    heads_here = projected.shape[1]
    offset = 3 * HEAD_FEATURES
    key_points = to_global(
        projected[:, :, offset + 3 * PQ : offset + 6 * PQ], rot_cols, trans_cols, PQ
    )
    value_points = to_global(projected[:, :, offset + 6 * PQ :], rot_cols, trans_cols, PV)
    packed_projection = jnp.concatenate(
        [
            projected[:, :, HEAD_FEATURES : 3 * HEAD_FEATURES],
            key_points.reshape(rows_here, heads_here, 3 * PQ),
            value_points.reshape(rows_here, heads_here, 3 * PV),
        ],
        axis=-1,
    )
    return rounded(
        packed_projection.reshape(rows_here, heads_here * (2 * HEAD_FEATURES + 3 * PQ + 3 * PV))
    )


def hat_matrix(vectors):
    comp_x = vectors[:, 0]
    comp_y = vectors[:, 1]
    comp_z = vectors[:, 2]
    zeros_col = jnp.zeros_like(comp_x)
    first_row = jnp.stack([zeros_col, -comp_z, comp_y], -1)
    second_row = jnp.stack([comp_z, zeros_col, -comp_x], -1)
    third_row = jnp.stack([-comp_y, comp_x, zeros_col], -1)
    return jnp.stack([first_row, second_row, third_row], 1)


def frame_step(single_out, frame_velocity_weight, rot_cols, trans_cols, live_rows, step_ratio):
    motion = jnp.dot(single_out, frame_velocity_weight, preferred_element_type=jnp.float32)
    rotvec = step_ratio * jnp.tanh(motion[:, 0:3]) * live_rows[:, None]
    velocity = step_ratio * motion[:, 3:6] * live_rows[:, None]
    angle_sq = jnp.sum(jnp.square(rotvec), -1)
    coef_a = jnp.zeros_like(angle_sq)
    coef_b = jnp.zeros_like(angle_sq)
    coef_c = jnp.zeros_like(angle_sq)
    powers = jnp.ones_like(angle_sq)
    for order in range(8):
        parity = (-1.0) ** order
        coef_a = coef_a + powers * (parity / float(math.factorial(2 * order + 1)))
        coef_b = coef_b + powers * (parity / float(math.factorial(2 * order + 2)))
        coef_c = coef_c + powers * (parity / float(math.factorial(2 * order + 3)))
        powers = powers * angle_sq
    cross_mat = hat_matrix(rotvec)
    cross_sq = jnp.einsum("nab,nbc->nac", cross_mat, cross_mat, precision=HIGHEST)
    identity = jnp.eye(3, dtype=jnp.float32)[None]
    turn = identity + coef_a[:, None, None] * cross_mat + coef_b[:, None, None] * cross_sq
    jacobian = identity + coef_b[:, None, None] * cross_mat + coef_c[:, None, None] * cross_sq
    new_rot = jnp.einsum("nab,nbc->nac", rot_cols, turn, precision=HIGHEST)
    moved = jnp.einsum("nab,nb->na", jacobian, velocity, precision=HIGHEST)
    new_trans = trans_cols + jnp.einsum("nab,nb->na", rot_cols, moved, precision=HIGHEST)
    return (jnp.transpose(new_rot, (1, 2, 0)), jnp.transpose(new_trans))


def local_logit_rows(
    query_values,
    query_flattened,
    packed_projection,
    pair_head_bias,
    within_chain,
    distance_weight,
    chain_offset,
    key_present,
):
    key_scalar = packed_projection[:, :, 0:HEAD_FEATURES]
    key_flat = packed_projection[:, :, 2 * HEAD_FEATURES : 2 * HEAD_FEATURES + 3 * PQ].astype(
        jnp.float32
    )
    scalar_logit_term = jnp.einsum(
        "rhc,nhc->rhn", query_values, key_scalar, preferred_element_type=jnp.float32
    )
    cross_term = jnp.einsum("rhp,nhp->rhn", query_flattened, key_flat, precision=HIGHEST)
    key_square = jnp.transpose(jnp.sum(jnp.square(key_flat), -1))
    point_distance = (
        jnp.sum(jnp.square(query_flattened), -1)[:, :, None] + key_square[None] - 2.0 * cross_term
    )
    point_term_weight = math.sqrt(2.0 / (9.0 * PQ))
    logit_matrix = LOGIT_FACTOR * (
        scalar_logit_term / math.sqrt(HEAD_FEATURES)
        + pair_head_bias
        + chain_offset[None, :, None] * within_chain[:, None, :]
        - (0.5 * point_term_weight * distance_weight)[None, :, None] * point_distance
    )
    return jnp.where(key_present[None, None, :], logit_matrix, -1000000000.0)


def local_points(scalar_out, point_global, rot_own, trans_own, local_output_weight):
    rows_dev = scalar_out.shape[0]
    heads_here = scalar_out.shape[1]
    point_global = point_global.reshape(rows_dev, heads_here, PV, 3)
    centred = point_global - trans_own[:, None, None, :]
    point_local = jnp.sum(rot_own[:, None, None, :, :] * centred[:, :, :, :, None], axis=-2)
    point_norm = jnp.sqrt(jnp.sum(jnp.square(point_local), -1) + 1.0)
    features = jnp.concatenate(
        [scalar_out, point_local.reshape(rows_dev, heads_here, 3 * PV), point_norm], -1
    )
    return jnp.einsum(
        "rhf,hfd->rd", features, local_output_weight.astype(jnp.float32), precision=HIGHEST
    )


def exchange(block, count, step):
    return lax.ppermute(block, "res", [(k, k ^ step) for k in range(count)])


def gather_blocks(block, count):
    if count < 16 or count & (count - 1):
        whole = lax.all_gather(block, "res", axis=0)
        return None, whole
    held, offsets = block[None], [0]
    quarter = count // 4
    step = quarter // 2
    while step > 1:
        held = jnp.concatenate([held, exchange(held, count, step)], 0)
        offsets = offsets + [o ^ step for o in offsets]
        step //= 2
    parts = [held] + [exchange(held, count, k * quarter) for k in (3, 2, 1)]
    held = jnp.concatenate(parts, 0)
    offsets = [o ^ (k * quarter) for k in (0, 3, 2, 1) for o in offsets]
    other = exchange(held, count, 1)
    return offsets, (held, other)


def sorted_blocks(offsets, blocks):
    if offsets is None:
        return blocks
    held, other = blocks
    entries = [held[e] for e in range(len(offsets))] + [other[e] for e in range(len(offsets))]
    every = dict(zip(offsets + [o ^ 1 for o in offsets], entries))
    both = jnp.stack([every[o] for o in range(len(every))])
    index = lax.axis_index("res")
    bit = 1
    while bit < len(every):
        halves = both.reshape((-1, 2, bit) + held.shape[1:])
        both = jnp.where((index & bit) > 0, halves[:, ::-1], halves).reshape(both.shape)
        bit *= 2
    return both


def transition_kernel(
    rows_block,
    rows_dev,
    offsets,
    live_ref,
    pair_ref,
    left_ref,
    live_row_ref,
    gain_ref,
    hidden_ref,
    middle_ref,
    back_ref,
    *rest,
):
    block_refs, (out_ref, right_ref, live_cols_ref, centring_ref) = rest[:-4], rest[-4:]
    step = pl.program_id(0)
    cols, feats = pair_ref.shape[1:]
    me = lax.axis_index("res")
    col_start = lax.axis_index("head") * cols

    @pl.when(step == 0)
    def _():
        at = 0
        for ref in block_refs:
            for e in range(ref.shape[0]):
                value = ref[e].astype(jnp.float32)
                value = value - jnp.mean(value, axis=-1, keepdims=True)
                owner = me ^ offsets[at] if offsets is not None else at
                at += 1
                right_ref[pl.ds(pl.multiple_of(owner * rows_dev, 8), rows_dev), :] = value
        wide = jnp.broadcast_to(live_row_ref[...].astype(jnp.float32), (feats, live_row_ref.shape[1]))
        live_cols_ref[...] = jnp.where(jnp.transpose(wide) > 0, 1.0, 0.0)
        across = lax.broadcasted_iota(jnp.int32, (feats, feats), 0)
        down = lax.broadcasted_iota(jnp.int32, (feats, feats), 1)
        centring_ref[...] = (jnp.where(across == down, 1.0, 0.0) - 1.0 / feats).astype(jnp.bfloat16)

    columns = pl.ds(pl.multiple_of(col_start, 8), cols)
    pair = pair_ref[...].reshape(rows_block * cols, feats)
    centred = jnp.dot(pair, centring_ref[...], preferred_element_type=jnp.float32)
    left = left_ref[...].astype(jnp.float32)
    left = left - jnp.mean(left, axis=-1, keepdims=True)
    centred = centred.reshape(rows_block, cols, feats) + left[:, None, :] + right_ref[columns, :][None]
    centred = centred.reshape(rows_block * cols, feats)
    averaging = jnp.full((feats, feats), 1.0 / feats, jnp.bfloat16)
    variance = jnp.dot(
        (centred * centred).astype(jnp.bfloat16), averaging, preferred_element_type=jnp.float32
    )
    normed = (centred * lax.rsqrt(variance + 1e-05) * gain_ref[...]).astype(jnp.bfloat16)
    hidden_one = jnp.maximum(
        jnp.dot(normed, hidden_ref[...], preferred_element_type=jnp.float32).astype(jnp.bfloat16), 0
    )
    hidden_two = jnp.maximum(
        jnp.dot(hidden_one, middle_ref[...], preferred_element_type=jnp.float32).astype(
            jnp.bfloat16
        ),
        0,
    )
    branch = jnp.dot(hidden_two, back_ref[...], preferred_element_type=jnp.float32)
    branch = branch.reshape(rows_block, cols, feats)
    live_cols = live_cols_ref[columns, :]
    for r in range(rows_block):
        live = jnp.where(live_ref[me * rows_dev + step * rows_block + r] > 0, 1.0, 0.0)
        out_ref[r] = (
            pair_ref[r].astype(jnp.float32) + live * live_cols * branch[r]
        ).astype(jnp.bfloat16)


def pair_transition(
    pair, left_proj, move_mask, gain, hidden, middle, back, offsets, blocks
):
    rows_dev, cols, feats = pair.shape
    total = move_mask.shape[0]
    rows_block = math.gcd(rows_dev, max(1, 1536 // cols))
    left_wide = left_proj.reshape(rows_dev // rows_block, rows_block, feats)
    whole = lambda *shape: pl.BlockSpec(shape, lambda i: (0,) * len(shape))
    kernel = functools.partial(transition_kernel, rows_block, rows_dev, offsets)
    macs = rows_dev * cols * (2 * feats * feats + 2 * feats * hidden.shape[1] + hidden.shape[1] ** 2)
    return pl.pallas_call(
        kernel,
        grid=(rows_dev // rows_block,),
        in_specs=[
            pl.BlockSpec(memory_space=pltpu.SMEM),
            pl.BlockSpec((rows_block, cols, feats), lambda i: (i, 0, 0)),
            pl.BlockSpec((None, rows_block, feats), lambda i: (i, 0, 0)),
            whole(1, total),
            whole(1, feats),
            whole(*hidden.shape),
            whole(*middle.shape),
            whole(*back.shape),
        ]
        + [whole(*b.shape) for b in blocks],
        out_specs=pl.BlockSpec((rows_block, cols, feats), lambda i: (i, 0, 0)),
        out_shape=jax.ShapeDtypeStruct(pair.shape, pair.dtype),
        scratch_shapes=[
            pltpu.VMEM((total, feats), jnp.float32),
            pltpu.VMEM((total, feats), jnp.float32),
            pltpu.VMEM((feats, feats), jnp.bfloat16),
        ],
        compiler_params=pltpu.CompilerParams(vmem_limit_bytes=48 * 1024 * 1024),
        cost_estimate=pl.CostEstimate(
            flops=2 * macs, bytes_accessed=2 * pair.size * 2, transcendentals=0
        ),
    )(
        move_mask,
        pair,
        left_wide,
        move_mask[None],
        gain[None],
        hidden,
        middle,
        back,
        *blocks,
    )


def dot(left, right):
    return jnp.dot(left, right, preferred_element_type=jnp.float32)


def dot_rows(left, right, precision=None):
    return lax.dot_general(
        left, right, (((1,), (1,)), ((), ())), preferred_element_type=jnp.float32, precision=precision
    )


def head_mask(heads, lanes):
    head = lax.broadcasted_iota(jnp.int32, (heads, lanes), 0)
    lane = lax.broadcasted_iota(jnp.int32, (heads, lanes), 1)
    return lax.rem(lane, heads) == head


def as_column(row):
    size = row.shape[1]
    return jnp.sum(jnp.where(head_mask(size, size), row, 0.0), axis=1, keepdims=True)


def halves(values):
    high = values.astype(jnp.bfloat16)
    return high, (values - high.astype(jnp.float32)).astype(jnp.bfloat16)


def point_rows(weight_ref, offset, npoints, coord):
    return jnp.concatenate([weight_ref[offset + 3 * p + coord] for p in range(npoints)], 0)


def turn(parts, rot, shift):
    return [
        rot[c][0] * parts[0] + rot[c][1] * parts[1] + rot[c][2] * parts[2] + shift[c]
        for c in range(3)
    ]


def query_kernel(
    chain_ref,
    pair_ref,
    single_ref,
    weight_ref,
    bias_ref,
    rot_ref,
    trans_ref,
    chain_row_ref,
    distance_ref,
    offset_ref,
    query_ref,
    base_ref,
    frame_ref,
    table_ref,
):
    rows, total, _ = pair_ref.shape
    heads = weight_ref.shape[1]
    me = lax.axis_index("res")
    table_ref[...] = jnp.zeros_like(table_ref)
    for c in range(3):
        for d in range(3):
            table_ref[pl.ds(3 * c + d, 1), :] = rot_ref[c, pl.ds(d, 1), :]
        table_ref[pl.ds(9 + c, 1), :] = trans_ref[pl.ds(c, 1), :]
    row = lax.broadcasted_iota(jnp.int32, (rows, total), 0)
    column = lax.broadcasted_iota(jnp.int32, (rows, total), 1)
    chosen = jnp.where(column == row + me * rows, 1.0, 0.0)
    frame = dot_rows(chosen, table_ref[...], HIGHEST)
    frame_ref[...] = frame
    rot = [[frame[:, 3 * c + d : 3 * c + d + 1] for d in range(3)] for c in range(3)]
    shift = [frame[:, 9 + c : 10 + c] for c in range(3)]

    weight = 0.5 * math.sqrt(2.0 / (9.0 * PQ)) * as_column(distance_ref[...])
    chain_offset = as_column(offset_ref[...])
    single = single_ref[...]
    scalar_rows = weight_ref[pl.ds(0, HEAD_FEATURES)].reshape(HEAD_FEATURES * heads, -1)
    scalar = dot_rows(single, scalar_rows).astype(jnp.bfloat16).astype(jnp.float32)
    scalar = scalar * (1.0 / math.sqrt(HEAD_FEATURES))
    lanes = scalar.shape[1]
    spread = jnp.where(head_mask(heads, lanes)[None], scalar[:, None, :], 0.0)
    query_ref[:, pl.ds(0, lanes)] = spread.reshape(rows * heads, lanes).astype(jnp.bfloat16)
    points = [
        dot_rows(single, point_rows(weight_ref, 3 * HEAD_FEATURES, PQ, c)) for c in range(3)
    ]
    points = turn(points, rot, shift)
    width = PQ * heads
    square = jnp.zeros((rows, heads, width), jnp.float32)
    for c in range(3):
        spread = jnp.where(head_mask(heads, width)[None], points[c][:, None, :], 0.0)
        square = square + spread * spread
        rest = spread * (2.0 * weight)[None]
        for term in range(3):
            part = rest.astype(jnp.bfloat16)
            rest = rest - part.astype(jnp.float32)
            at = lanes + (3 * term + c) * width
            query_ref[:, pl.ds(at, width)] = part.reshape(rows * heads, width)
    square = jnp.sum(square, axis=-1, keepdims=True)
    for r in range(rows):
        bias = dot_rows(bias_ref[...], pair_ref[r]).astype(jnp.bfloat16).astype(jnp.float32)
        within = jnp.where(chain_row_ref[...] == chain_ref[me * rows + r], 1.0, 0.0)
        base_ref[r] = LOGIT_FACTOR * (bias + chain_offset * within - weight * square[r])


def attention_kernel(
    offsets,
    held_ref,
    other_ref,
    weight_ref,
    query_ref,
    base_ref,
    frame_ref,
    rot_ref,
    trans_ref,
    present_ref,
    distance_ref,
    pair_ref,
    single_ref,
    local_ref,
    pair_weight_ref,
    gain_ref,
    left_ref,
    right_ref,
    out_ref,
    left_out_ref,
    right_out_ref,
    every_ref,
    pair_sum_ref,
):
    rows, total, feats = pair_ref.shape
    heads = weight_ref.shape[1]
    me = lax.axis_index("res")
    for ref, step in ((held_ref, 0), (other_ref, 1)):
        for e, o in enumerate(offsets):
            owner = me ^ (o ^ step)
            every_ref[pl.ds(pl.multiple_of(owner * rows, 8), rows), :] = ref[e].astype(jnp.float32)
    every = every_ref[...].astype(jnp.bfloat16)
    rot = [[rot_ref[c, pl.ds(d, 1), :] for d in range(3)] for c in range(3)]
    shift = [trans_ref[pl.ds(c, 1), :] for c in range(3)]

    key_at, value_at = HEAD_FEATURES, 2 * HEAD_FEATURES
    key_rows = weight_ref[pl.ds(key_at, HEAD_FEATURES)].reshape(HEAD_FEATURES * heads, -1)
    keys = dot_rows(key_rows, every).astype(jnp.bfloat16)
    offset = 3 * HEAD_FEATURES + 3 * PQ
    points = [dot_rows(point_rows(weight_ref, offset, PQ, c), every) for c in range(3)]
    points = [p.astype(jnp.bfloat16) for p in turn(points, rot, shift)]
    square = sum(jnp.square(p.astype(jnp.float32)) for p in points)
    square = jnp.sum(square.reshape(PQ, heads, total), axis=0)
    keys = jnp.concatenate([keys] + 3 * points, 0)
    weight = 0.5 * LOGIT_FACTOR * math.sqrt(2.0 / (9.0 * PQ)) * as_column(distance_ref[...])
    logits = dot(query_ref[...], keys).reshape(rows, heads, total)
    logits = LOGIT_FACTOR * logits + base_ref[...] - (weight * square)[None]
    present = present_ref[...] > 0
    logits = jnp.where(present[None], logits, -1000000000.0)
    logits = logits.reshape(rows * heads, total)
    exponent = jnp.exp(logits - jnp.max(logits, axis=-1, keepdims=True))
    attention = (exponent / jnp.sum(exponent, axis=-1, keepdims=True)).astype(jnp.bfloat16)

    for r in range(rows):
        pair_sum_ref[pl.ds(r * heads, heads), :] = dot(
            attention[r * heads : (r + 1) * heads], pair_ref[r]
        )

    def own_head(values):
        lanes = values.shape[0]
        mixed = dot_rows(attention, values).reshape(rows, heads, lanes)
        return jnp.sum(jnp.where(head_mask(heads, lanes)[None], mixed, 0.0), axis=1)

    value_rows = weight_ref[pl.ds(value_at, HEAD_FEATURES)].reshape(HEAD_FEATURES * heads, -1)
    scalar_out = own_head(dot_rows(value_rows, every).astype(jnp.bfloat16))
    offset = 3 * HEAD_FEATURES + 6 * PQ
    points = [dot_rows(point_rows(weight_ref, offset, PV, c), every) for c in range(3)]
    points = [own_head(p.astype(jnp.bfloat16)) for p in turn(points, rot, shift)]
    frame = frame_ref[...]
    centred = [points[c] - frame[:, 9 + c : 10 + c] for c in range(3)]
    local = [
        sum(frame[:, 3 * c + d : 3 * c + d + 1] * centred[c] for c in range(3)) for d in range(3)
    ]
    norm = jnp.sqrt(sum(jnp.square(v) for v in local) + 1.0)

    def product(values, rows_of_weight):
        return dot(jnp.concatenate(halves(values), 0), rows_of_weight)

    first = HEAD_FEATURES * heads
    update = product(scalar_out, local_ref[pl.ds(0, HEAD_FEATURES)].reshape(first, -1))
    for c in range(3):
        update = update + product(local[c], point_rows(local_ref, HEAD_FEATURES, PV, c))
    norm_rows = local_ref[pl.ds(HEAD_FEATURES + 3 * PV, PV)].reshape(PV * heads, -1)
    update = update + product(norm, norm_rows)
    pair_sum = jnp.concatenate(
        [pair_sum_ref[pl.ds(h, rows, stride=heads), :] for h in range(heads)], 1
    )
    update = update + product(pair_sum, pair_weight_ref[...])
    values = single_ref[...].astype(jnp.float32) + update[:rows] + update[rows:]
    single_out = layer_norm(values, gain_ref[...]).astype(jnp.bfloat16)
    out_ref[...] = single_out
    left_out_ref[...] = dot(single_out, left_ref[...]).astype(jnp.bfloat16)
    right_out_ref[...] = dot(single_out, right_ref[...]).astype(jnp.bfloat16)


def frame_kernel(
    step_ref,
    live_ref,
    single_ref,
    velocity_ref,
    rot_ref,
    trans_ref,
    rot_out_ref,
    trans_out_ref,
    table_ref,
):
    rows = single_ref.shape[0]
    total = rot_ref.shape[2]
    me = lax.axis_index("res")
    table_ref[...] = jnp.zeros_like(table_ref)
    for c in range(3):
        for d in range(3):
            table_ref[pl.ds(3 * c + d, 1), :] = rot_ref[c, pl.ds(d, 1), :]
        table_ref[pl.ds(9 + c, 1), :] = trans_ref[pl.ds(c, 1), :]
    table_ref[pl.ds(12, 1), :] = jnp.where(live_ref[...] > 0, 1.0, 0.0)
    row = lax.broadcasted_iota(jnp.int32, (rows, total), 0)
    column = lax.broadcasted_iota(jnp.int32, (rows, total), 1)
    chosen = jnp.where(column == row + me * rows, 1.0, 0.0)
    frame = dot_rows(table_ref[...], chosen, HIGHEST)
    motion = dot_rows(velocity_ref[...], single_ref[...])
    live = frame[12:13]
    ratio = 1.0 / jnp.full((1, rows), STEPS - step_ref[0], jnp.int32).astype(jnp.float32)
    x, y, z = [ratio * jnp.tanh(motion[c : c + 1]) * live for c in range(3)]
    velocity = [ratio * motion[3 + c : 4 + c] * live for c in range(3)]
    angle_sq = x * x + y * y + z * z
    coefs = [jnp.zeros_like(angle_sq) for _ in range(3)]
    powers = jnp.ones_like(angle_sq)
    for order in range(8):
        parity = (-1.0) ** order
        coefs = [
            coef + powers * (parity / float(math.factorial(2 * order + 1 + k)))
            for k, coef in enumerate(coefs)
        ]
        powers = powers * angle_sq
    zero = jnp.zeros_like(x)
    cross = [[zero, -z, y], [z, zero, -x], [-y, x, zero]]
    square = [[sum(cross[a][b] * cross[b][c] for b in range(3)) for c in range(3)] for a in range(3)]
    one = [[jnp.ones_like(x) if a == b else zero for b in range(3)] for a in range(3)]

    def series(first, second):
        return [
            [one[a][b] + first * cross[a][b] + second * square[a][b] for b in range(3)]
            for a in range(3)
        ]

    turned, jacobian = series(coefs[0], coefs[1]), series(coefs[1], coefs[2])
    rot = [[frame[3 * a + b : 3 * a + b + 1] for b in range(3)] for a in range(3)]
    moved = [sum(jacobian[a][b] * velocity[b] for b in range(3)) for a in range(3)]
    for a in range(3):
        for c in range(3):
            rot_out_ref[a, pl.ds(c, 1), :] = sum(rot[a][b] * turned[b][c] for b in range(3))
        trans_out_ref[pl.ds(a, 1), :] = frame[9 + a : 10 + a] + sum(
            rot[a][b] * moved[b] for b in range(3)
        )


def in_vmem(count):
    return [pl.BlockSpec(memory_space=pltpu.VMEM)] * count


def attend(
    single,
    pair,
    rotations,
    translations,
    residue_chain_index,
    residue_move_mask,
    timestep,
    single_projection_weight,
    head_bias_weight,
    head_distance_weight,
    chain_logit_offset,
    local_output_weight,
    pair_output_weight,
    single_norm_gain,
    frame_velocity_weight,
    left_pair_weight,
    right_pair_weight,
):
    rows, total, feats = pair.shape
    heads = single_projection_weight.shape[1]
    width = single.shape[1]
    offsets, (held, other) = gather_blocks(single, total // rows)
    weight = jnp.transpose(single_projection_weight, (2, 1, 0))
    local_weight = jnp.transpose(local_output_weight, (1, 0, 2))
    distance = head_distance_weight[None]
    depth = heads * (HEAD_FEATURES + 9 * PQ)
    query, base, frame = pl.pallas_call(
        query_kernel,
        in_specs=[pl.BlockSpec(memory_space=pltpu.SMEM)] + in_vmem(9),
        out_specs=tuple(in_vmem(3)),
        out_shape=(
            jax.ShapeDtypeStruct((rows * heads, depth), jnp.bfloat16),
            jax.ShapeDtypeStruct((rows, heads, total), jnp.float32),
            jax.ShapeDtypeStruct((rows, 16), jnp.float32),
        ),
        scratch_shapes=[pltpu.VMEM((16, total), jnp.float32)],
        compiler_params=pltpu.CompilerParams(vmem_limit_bytes=24 * 1024 * 1024),
        cost_estimate=pl.CostEstimate(flops=10**9, bytes_accessed=6 * 10**6, transcendentals=0),
    )(
        residue_chain_index,
        pair,
        single,
        weight,
        jnp.transpose(head_bias_weight),
        rotations,
        translations,
        residue_chain_index[None],
        distance,
        chain_logit_offset[None],
    )
    single_out, left_proj, right_proj = pl.pallas_call(
        functools.partial(attention_kernel, offsets),
        in_specs=in_vmem(17),
        out_specs=tuple(in_vmem(3)),
        out_shape=(
            jax.ShapeDtypeStruct((rows, width), jnp.bfloat16),
            jax.ShapeDtypeStruct((rows, feats), jnp.bfloat16),
            jax.ShapeDtypeStruct((rows, feats), jnp.bfloat16),
        ),
        scratch_shapes=[
            pltpu.VMEM((total, width), jnp.float32),
            pltpu.VMEM((rows * heads, feats), jnp.float32),
        ],
        compiler_params=pltpu.CompilerParams(vmem_limit_bytes=40 * 1024 * 1024),
        cost_estimate=pl.CostEstimate(flops=2 * 10**9, bytes_accessed=10**7, transcendentals=0),
    )(
        held,
        other,
        weight,
        query,
        base,
        frame,
        rotations,
        translations,
        residue_move_mask[None],
        distance,
        pair,
        single,
        local_weight,
        pair_output_weight.reshape(heads * feats, width),
        single_norm_gain[None],
        left_pair_weight,
        right_pair_weight,
    )
    velocity_rows = jnp.pad(jnp.transpose(frame_velocity_weight), ((0, 2), (0, 0)))
    rot_out, trans_out = pl.pallas_call(
        frame_kernel,
        in_specs=[pl.BlockSpec(memory_space=pltpu.SMEM)] + in_vmem(5),
        out_specs=tuple(in_vmem(2)),
        out_shape=(
            jax.ShapeDtypeStruct((3, 3, rows), jnp.float32),
            jax.ShapeDtypeStruct((3, rows), jnp.float32),
        ),
        scratch_shapes=[pltpu.VMEM((16, total), jnp.float32)],
        cost_estimate=pl.CostEstimate(flops=10**6, bytes_accessed=10**5, transcendentals=0),
    )(
        timestep,
        residue_move_mask[None],
        single_out,
        velocity_rows,
        rotations,
        translations,
    )
    return single_out, rot_out, trans_out, left_proj, right_proj


def attend_split(
    single,
    pair,
    rotations,
    translations,
    residue_chain_index,
    residue_move_mask,
    timestep,
    single_projection_weight,
    head_bias_weight,
    head_distance_weight,
    chain_logit_offset,
    local_output_weight,
    pair_output_weight,
    single_norm_gain,
    frame_velocity_weight,
    left_pair_weight,
    right_pair_weight,
):
    rows_dev = single.shape[0]
    col_count = pair.shape[1]
    total = rotations.shape[2]
    heads_here = single_projection_weight.shape[1]
    row_start = lax.axis_index("res") * rows_dev
    rot_all = jnp.transpose(rotations, (2, 0, 1))
    trans_all = jnp.transpose(translations)
    rot_own = lax.dynamic_slice_in_dim(rot_all, row_start, rows_dev, 0)
    trans_own = lax.dynamic_slice_in_dim(trans_all, row_start, rows_dev, 0)
    own_chain = lax.dynamic_slice_in_dim(residue_chain_index, row_start, rows_dev, 0)
    offset = 3 * HEAD_FEATURES
    feat_count = 2 * HEAD_FEATURES + 3 * PQ + 3 * PV
    count = total // rows_dev
    every_single = sorted_blocks(*gather_blocks(single, count)).reshape(total, -1)
    every_proj = jnp.einsum(
        "nd,dhf->nhf", every_single, single_projection_weight, preferred_element_type=jnp.float32
    )
    projected = lax.dynamic_slice_in_dim(every_proj, row_start, rows_dev, 0)
    packed_projection = key_features(every_proj, rot_all, trans_all)
    packed_projection = packed_projection.reshape(total, heads_here, feat_count)
    query_values = projected[:, :, 0:HEAD_FEATURES].astype(jnp.bfloat16)
    query_flattened = to_global(
        projected[:, :, offset : offset + 3 * PQ], rot_own, trans_own, PQ
    ).reshape(rows_dev, heads_here, 3 * PQ)
    bias_local = jnp.einsum(
        "rjc,ch->rhj", pair, head_bias_weight, preferred_element_type=jnp.float32
    ).astype(jnp.bfloat16)
    pair_head_bias = lax.all_to_all(
        bias_local, "head", split_axis=1, concat_axis=2, tiled=True
    ).astype(jnp.float32)
    within_chain = (own_chain[:, None] == residue_chain_index[None, :]).astype(jnp.float32)
    logit_matrix = local_logit_rows(
        query_values,
        query_flattened,
        packed_projection,
        pair_head_bias,
        within_chain,
        head_distance_weight,
        chain_logit_offset,
        residue_move_mask > 0,
    )
    peak = jnp.max(logit_matrix, axis=-1, keepdims=True)
    exponent = jnp.exp(logit_matrix - peak)
    attention = rounded(exponent / jnp.sum(exponent, axis=-1, keepdims=True))
    scalar_out = jnp.einsum(
        "rhn,nhc->rhc",
        attention,
        packed_projection[:, :, HEAD_FEATURES : 2 * HEAD_FEATURES],
        preferred_element_type=jnp.float32,
    )
    point_global = jnp.einsum(
        "rhn,nhp->rhp",
        attention.astype(jnp.float32),
        packed_projection[:, :, 2 * HEAD_FEATURES + 3 * PQ :].astype(jnp.float32),
        precision=HIGHEST,
    )
    update_local = local_points(scalar_out, point_global, rot_own, trans_own, local_output_weight)
    attention_cols = lax.all_to_all(attention, "head", split_axis=2, concat_axis=1, tiled=True)
    pair_attended = jnp.einsum(
        "rhj,rjc->rhc", attention_cols, pair, preferred_element_type=jnp.float32
    )
    update_pair = jnp.einsum(
        "rhc,hcd->rd", pair_attended, pair_output_weight.astype(jnp.float32), precision=HIGHEST
    )
    update = lax.psum(update_local + update_pair, "head")
    single_out = layer_norm(single.astype(jnp.float32) + update, single_norm_gain).astype(
        jnp.bfloat16
    )
    live_all = (residue_move_mask > 0).astype(jnp.float32)
    live_own = lax.dynamic_slice_in_dim(live_all, row_start, rows_dev, 0)
    step_ratio = 1.0 / (STEPS - timestep[0]).astype(jnp.float32)
    rot_out, trans_out = frame_step(
        single_out, frame_velocity_weight, rot_own, trans_own, live_own, step_ratio
    )
    left_proj = jnp.dot(single_out, left_pair_weight, preferred_element_type=jnp.float32).astype(
        jnp.bfloat16
    )
    right_proj = jnp.dot(single_out, right_pair_weight, preferred_element_type=jnp.float32).astype(
        jnp.bfloat16
    )
    return single_out, rot_out, trans_out, left_proj, right_proj


def shards(
    single,
    pair,
    rotations,
    translations,
    residue_chain_index,
    residue_move_mask,
    timestep,
    single_projection_weight,
    head_bias_weight,
    head_distance_weight,
    chain_logit_offset,
    local_output_weight,
    pair_output_weight,
    single_norm_gain,
    frame_velocity_weight,
    left_pair_weight,
    right_pair_weight,
    pair_norm_gain,
    transition_hidden_weight,
    transition_middle_weight,
    transition_back_weight,
):
    rows_dev = single.shape[0]
    count = rotations.shape[2] // rows_dev
    whole_heads = lax.axis_size("head") == 1 and count >= 16 and count & (count - 1) == 0
    single_out, rot_out, trans_out, left_proj, right_proj = (
        attend if whole_heads else attend_split
    )(
        single,
        pair,
        rotations,
        translations,
        residue_chain_index,
        residue_move_mask,
        timestep,
        single_projection_weight,
        head_bias_weight,
        head_distance_weight,
        chain_logit_offset,
        local_output_weight,
        pair_output_weight,
        single_norm_gain,
        frame_velocity_weight,
        left_pair_weight,
        right_pair_weight,
    )
    offsets, blocks = gather_blocks(right_proj, count)
    if offsets is None:
        blocks = (blocks,)
    else:
        offsets = offsets + [o ^ 1 for o in offsets]
    pair_out = pair_transition(
        pair,
        left_proj,
        residue_move_mask,
        pair_norm_gain,
        transition_hidden_weight,
        transition_middle_weight,
        transition_back_weight,
        offsets,
        blocks,
    )
    return (single_out, rot_out, trans_out, pair_out)


def solution(mesh):
    placed = (
        P(("batch", "res"), None),
        P(("batch", "res"), "head", None),
        P(None, None, "batch"),
        P(None, "batch"),
        P(),
        P("batch"),
        P(),
        P(None, "head", None),
        P(),
        P("head"),
        P("head"),
        P("head", None, None),
        P(),
        P(),
        P(),
        P(),
        P(),
        P(),
        P(),
        P(),
        P(),
    )
    return jax.shard_map(
        shards,
        mesh=mesh,
        in_specs=placed,
        out_specs=(
            P(("batch", "res"), None),
            P(None, None, ("batch", "res")),
            P(None, ("batch", "res")),
            P(("batch", "res"), "head", None),
        ),
        check_vma=False,
    )
```

```python
import functools
import math

import jax
import jax.numpy as jnp
from jax import lax
from jax.experimental import pallas as pl
from jax.experimental.pallas import tpu as pltpu
from jax.sharding import PartitionSpec as P

HEAD_FEATURES = 16
PQ = 8
PV = 12
STEPS = 8


LOGIT_FACTOR = math.sqrt(1.0 / 3.0)
HIGHEST = lax.Precision.HIGHEST


def rounded(values):
    return lax.optimization_barrier(values.astype(jnp.bfloat16))


def layer_norm(values, gain):
    centre = jnp.mean(values, axis=-1, keepdims=True)
    variance = jnp.mean(jnp.square(values - centre), axis=-1, keepdims=True)
    return (values - centre) * lax.rsqrt(variance + 1e-05) * gain


def to_global(local, rot_cols, trans_cols, npoints):
    rows_here = local.shape[0]
    heads_here = local.shape[1]
    points = local.reshape(rows_here, heads_here, npoints, 3)
    turned = jnp.sum(rot_cols[:, None, None, :, :] * points[:, :, :, None, :], axis=-1)
    return turned + trans_cols[:, None, None, :]


def key_features(projected, rot_cols, trans_cols):
    rows_here = projected.shape[0]
    heads_here = projected.shape[1]
    offset = 3 * HEAD_FEATURES
    key_points = to_global(
        projected[:, :, offset + 3 * PQ : offset + 6 * PQ], rot_cols, trans_cols, PQ
    )
    value_points = to_global(projected[:, :, offset + 6 * PQ :], rot_cols, trans_cols, PV)
    packed_projection = jnp.concatenate(
        [
            projected[:, :, HEAD_FEATURES : 3 * HEAD_FEATURES],
            key_points.reshape(rows_here, heads_here, 3 * PQ),
            value_points.reshape(rows_here, heads_here, 3 * PV),
        ],
        axis=-1,
    )
    return rounded(
        packed_projection.reshape(rows_here, heads_here * (2 * HEAD_FEATURES + 3 * PQ + 3 * PV))
    )


def hat_matrix(vectors):
    comp_x = vectors[:, 0]
    comp_y = vectors[:, 1]
    comp_z = vectors[:, 2]
    zeros_col = jnp.zeros_like(comp_x)
    first_row = jnp.stack([zeros_col, -comp_z, comp_y], -1)
    second_row = jnp.stack([comp_z, zeros_col, -comp_x], -1)
    third_row = jnp.stack([-comp_y, comp_x, zeros_col], -1)
    return jnp.stack([first_row, second_row, third_row], 1)


def frame_step(single_out, frame_velocity_weight, rot_cols, trans_cols, live_rows, step_ratio):
    motion = jnp.dot(single_out, frame_velocity_weight, preferred_element_type=jnp.float32)
    rotvec = step_ratio * jnp.tanh(motion[:, 0:3]) * live_rows[:, None]
    velocity = step_ratio * motion[:, 3:6] * live_rows[:, None]
    angle_sq = jnp.sum(jnp.square(rotvec), -1)
    coef_a = jnp.zeros_like(angle_sq)
    coef_b = jnp.zeros_like(angle_sq)
    coef_c = jnp.zeros_like(angle_sq)
    powers = jnp.ones_like(angle_sq)
    for order in range(8):
        parity = (-1.0) ** order
        coef_a = coef_a + powers * (parity / float(math.factorial(2 * order + 1)))
        coef_b = coef_b + powers * (parity / float(math.factorial(2 * order + 2)))
        coef_c = coef_c + powers * (parity / float(math.factorial(2 * order + 3)))
        powers = powers * angle_sq
    cross_mat = hat_matrix(rotvec)
    cross_sq = jnp.einsum("nab,nbc->nac", cross_mat, cross_mat, precision=HIGHEST)
    identity = jnp.eye(3, dtype=jnp.float32)[None]
    turn = identity + coef_a[:, None, None] * cross_mat + coef_b[:, None, None] * cross_sq
    jacobian = identity + coef_b[:, None, None] * cross_mat + coef_c[:, None, None] * cross_sq
    new_rot = jnp.einsum("nab,nbc->nac", rot_cols, turn, precision=HIGHEST)
    moved = jnp.einsum("nab,nb->na", jacobian, velocity, precision=HIGHEST)
    new_trans = trans_cols + jnp.einsum("nab,nb->na", rot_cols, moved, precision=HIGHEST)
    return (jnp.transpose(new_rot, (1, 2, 0)), jnp.transpose(new_trans))


def local_logit_rows(
    query_values,
    query_flattened,
    packed_projection,
    pair_head_bias,
    within_chain,
    distance_weight,
    chain_offset,
    key_present,
):
    key_scalar = packed_projection[:, :, 0:HEAD_FEATURES]
    key_flat = packed_projection[:, :, 2 * HEAD_FEATURES : 2 * HEAD_FEATURES + 3 * PQ].astype(
        jnp.float32
    )
    scalar_logit_term = jnp.einsum(
        "rhc,nhc->rhn", query_values, key_scalar, preferred_element_type=jnp.float32
    )
    cross_term = jnp.einsum("rhp,nhp->rhn", query_flattened, key_flat, precision=HIGHEST)
    key_square = jnp.transpose(jnp.sum(jnp.square(key_flat), -1))
    point_distance = (
        jnp.sum(jnp.square(query_flattened), -1)[:, :, None] + key_square[None] - 2.0 * cross_term
    )
    point_term_weight = math.sqrt(2.0 / (9.0 * PQ))
    logit_matrix = LOGIT_FACTOR * (
        scalar_logit_term / math.sqrt(HEAD_FEATURES)
        + pair_head_bias
        + chain_offset[None, :, None] * within_chain[:, None, :]
        - (0.5 * point_term_weight * distance_weight)[None, :, None] * point_distance
    )
    return jnp.where(key_present[None, None, :], logit_matrix, -1000000000.0)


def local_points(scalar_out, point_global, rot_own, trans_own, local_output_weight):
    rows_dev = scalar_out.shape[0]
    heads_here = scalar_out.shape[1]
    point_global = point_global.reshape(rows_dev, heads_here, PV, 3)
    centred = point_global - trans_own[:, None, None, :]
    point_local = jnp.sum(rot_own[:, None, None, :, :] * centred[:, :, :, :, None], axis=-2)
    point_norm = jnp.sqrt(jnp.sum(jnp.square(point_local), -1) + 1.0)
    features = jnp.concatenate(
        [scalar_out, point_local.reshape(rows_dev, heads_here, 3 * PV), point_norm], -1
    )
    return jnp.einsum(
        "rhf,hfd->rd", features, local_output_weight.astype(jnp.float32), precision=HIGHEST
    )


def exchange(block, count, step):
    return lax.ppermute(block, "res", [(k, k ^ step) for k in range(count)])


def gather_most(block, count, tied=()):
    held, offsets = block[None], [0]
    quarter = count // 4
    step = quarter // 2
    while step > 1:
        held = jnp.concatenate([held, exchange(held, count, step)], 0)
        offsets = offsets + [o ^ step for o in offsets]
        step //= 2
    held, tied = lax.optimization_barrier((held, tied))
    parts = [held] + [exchange(held, count, k * quarter) for k in (3, 2, 1)]
    held = jnp.concatenate(parts, 0)
    return [o ^ (k * quarter) for k in (0, 3, 2, 1) for o in offsets], held, tied


def gather_blocks(block, count, tied=()):
    if count < 16 or count & (count - 1):
        return None, lax.all_gather(block, "res", axis=0), tied
    offsets, held, tied = gather_most(block, count, tied)
    return offsets, (held, exchange(held, count, 1)), tied


def sorted_blocks(offsets, blocks):
    if offsets is None:
        return blocks
    held, other = blocks
    entries = [held[e] for e in range(len(offsets))] + [other[e] for e in range(len(offsets))]
    every = dict(zip(offsets + [o ^ 1 for o in offsets], entries))
    both = jnp.stack([every[o] for o in range(len(every))])
    index = lax.axis_index("res")
    bit = 1
    while bit < len(every):
        halves = both.reshape((-1, 2, bit) + held.shape[1:])
        both = jnp.where((index & bit) > 0, halves[:, ::-1], halves).reshape(both.shape)
        bit *= 2
    return both


def transition_kernel(
    rows_block,
    rows_dev,
    offsets,
    live_at,
    live_ref,
    pair_ref,
    left_ref,
    live_row_ref,
    gain_ref,
    hidden_ref,
    middle_ref,
    back_ref,
    *rest,
):
    block_refs, (out_ref, right_ref, live_cols_ref, centring_ref) = rest[:-4], rest[-4:]
    step = pl.program_id(0)
    cols, feats = pair_ref.shape[1:]
    me = lax.axis_index("res")
    col_start = lax.axis_index("head") * cols

    @pl.when(step == 0)
    def _():
        at = 0
        for ref in block_refs:
            for e in range(ref.shape[0]):
                value = ref[e].astype(jnp.float32)
                value = value - jnp.mean(value, axis=-1, keepdims=True)
                owner = me ^ offsets[at] if offsets is not None else at
                at += 1
                right_ref[pl.ds(pl.multiple_of(owner * rows_dev, 8), rows_dev), :] = value
        live_row = live_row_ref[pl.ds(live_at, 1), :].astype(jnp.float32)
        wide = jnp.broadcast_to(live_row, (feats, live_row.shape[1]))
        live_cols_ref[...] = jnp.where(jnp.transpose(wide) > 0, 1.0, 0.0)
        across = lax.broadcasted_iota(jnp.int32, (feats, feats), 0)
        down = lax.broadcasted_iota(jnp.int32, (feats, feats), 1)
        centring_ref[...] = (jnp.where(across == down, 1.0, 0.0) - 1.0 / feats).astype(jnp.bfloat16)

    columns = pl.ds(pl.multiple_of(col_start, 8), cols)
    pair = pair_ref[...].reshape(rows_block * cols, feats)
    centred = jnp.dot(pair, centring_ref[...], preferred_element_type=jnp.float32)
    left = left_ref[...].astype(jnp.float32)
    left = left - jnp.mean(left, axis=-1, keepdims=True)
    centred = centred.reshape(rows_block, cols, feats) + left[:, None, :] + right_ref[columns, :][None]
    centred = centred.reshape(rows_block * cols, feats)
    averaging = jnp.full((feats, feats), 1.0 / feats, jnp.bfloat16)
    variance = jnp.dot(
        (centred * centred).astype(jnp.bfloat16), averaging, preferred_element_type=jnp.float32
    )
    normed = (centred * lax.rsqrt(variance + 1e-05) * gain_ref[...]).astype(jnp.bfloat16)
    hidden_one = jnp.maximum(
        jnp.dot(normed, hidden_ref[...], preferred_element_type=jnp.float32).astype(jnp.bfloat16), 0
    )
    hidden_two = jnp.maximum(
        jnp.dot(hidden_one, middle_ref[...], preferred_element_type=jnp.float32).astype(
            jnp.bfloat16
        ),
        0,
    )
    branch = jnp.dot(hidden_two, back_ref[...], preferred_element_type=jnp.float32)
    branch = branch.reshape(rows_block, cols, feats)
    live_cols = live_cols_ref[columns, :]
    for r in range(rows_block):
        live = jnp.where(live_ref[me * rows_dev + step * rows_block + r] > 0, 1.0, 0.0)
        out_ref[r] = (
            pair_ref[r].astype(jnp.float32) + live * live_cols * branch[r]
        ).astype(jnp.bfloat16)


def pair_transition(
    pair, left_proj, move_mask, live_rows, live_at, gain, hidden, middle, back, offsets, blocks
):
    rows_dev, cols, feats = pair.shape
    total = move_mask.shape[0]
    rows_block = math.gcd(rows_dev, max(1, 1536 // cols))
    left_wide = left_proj.reshape(rows_dev // rows_block, rows_block, feats)
    whole = lambda *shape: pl.BlockSpec(shape, lambda i: (0,) * len(shape))
    kernel = functools.partial(transition_kernel, rows_block, rows_dev, offsets, live_at)
    macs = rows_dev * cols * (2 * feats * feats + 2 * feats * hidden.shape[1] + hidden.shape[1] ** 2)
    return pl.pallas_call(
        kernel,
        grid=(rows_dev // rows_block,),
        in_specs=[
            pl.BlockSpec(memory_space=pltpu.SMEM),
            pl.BlockSpec((rows_block, cols, feats), lambda i: (i, 0, 0)),
            pl.BlockSpec((None, rows_block, feats), lambda i: (i, 0, 0)),
            whole(*live_rows.shape),
            whole(1, feats),
            whole(*hidden.shape),
            whole(*middle.shape),
            whole(*back.shape),
        ]
        + [whole(*b.shape) for b in blocks],
        out_specs=pl.BlockSpec((rows_block, cols, feats), lambda i: (i, 0, 0)),
        out_shape=jax.ShapeDtypeStruct(pair.shape, pair.dtype),
        scratch_shapes=[
            pltpu.VMEM((total, feats), jnp.float32),
            pltpu.VMEM((total, feats), jnp.float32),
            pltpu.VMEM((feats, feats), jnp.bfloat16),
        ],
        compiler_params=pltpu.CompilerParams(vmem_limit_bytes=32 * 1024 * 1024),
        cost_estimate=pl.CostEstimate(
            flops=2 * macs, bytes_accessed=2 * pair.size * 2, transcendentals=0
        ),
    )(
        move_mask,
        pair,
        left_wide,
        live_rows,
        gain[None],
        hidden,
        middle,
        back,
        *blocks,
    )


def dot(left, right):
    return jnp.dot(left, right, preferred_element_type=jnp.float32)


def dot_rows(left, right, precision=None):
    return lax.dot_general(
        left, right, (((1,), (1,)), ((), ())), preferred_element_type=jnp.float32, precision=precision
    )


def head_mask(heads, lanes):
    head = lax.broadcasted_iota(jnp.int32, (heads, lanes), 0)
    lane = lax.broadcasted_iota(jnp.int32, (heads, lanes), 1)
    return lax.rem(lane, heads) == head


def as_column(row):
    size = row.shape[1]
    return jnp.sum(jnp.where(head_mask(size, size), row, 0.0), axis=1, keepdims=True)


def halves(values):
    high = values.astype(jnp.bfloat16)
    return high, (values - high.astype(jnp.float32)).astype(jnp.bfloat16)


def point_rows(weight_ref, offset, npoints, coord):
    return jnp.concatenate([weight_ref[offset + 3 * p + coord] for p in range(npoints)], 0)


def turn(parts, rot, shift):
    return [
        rot[c][0] * parts[0] + rot[c][1] * parts[1] + rot[c][2] * parts[2] + shift[c]
        for c in range(3)
    ]


def bias_kernel(weight_ref, pair_ref, out_ref):
    for r in range(pair_ref.shape[0]):
        bias = dot_rows(weight_ref[...], pair_ref[r])
        out_ref[r] = bias.astype(jnp.bfloat16).astype(jnp.float32)


def query_kernel(
    chain_ref,
    bias_ref,
    single_ref,
    weight_ref,
    rot_ref,
    trans_ref,
    rows_ref,
    distance_ref,
    offset_ref,
    query_ref,
    base_ref,
    frame_ref,
    table_ref,
):
    rows, heads, total = bias_ref.shape
    me = lax.axis_index("res")
    table_ref[...] = jnp.zeros_like(table_ref)
    for c in range(3):
        for d in range(3):
            table_ref[pl.ds(3 * c + d, 1), :] = rot_ref[c, pl.ds(d, 1), :]
        table_ref[pl.ds(9 + c, 1), :] = trans_ref[pl.ds(c, 1), :]
    row = lax.broadcasted_iota(jnp.int32, (rows, total), 0)
    column = lax.broadcasted_iota(jnp.int32, (rows, total), 1)
    chosen = jnp.where(column == row + me * rows, 1.0, 0.0)
    frame = dot_rows(chosen, table_ref[...], HIGHEST)
    frame_ref[...] = frame
    rot = [[frame[:, 3 * c + d : 3 * c + d + 1] for d in range(3)] for c in range(3)]
    shift = [frame[:, 9 + c : 10 + c] for c in range(3)]

    weight = 0.5 * math.sqrt(2.0 / (9.0 * PQ)) * as_column(distance_ref[...])
    chain_offset = as_column(offset_ref[...])
    single = single_ref[...]
    scalar_rows = weight_ref[pl.ds(0, HEAD_FEATURES)].reshape(HEAD_FEATURES * heads, -1)
    scalar = dot_rows(single, scalar_rows).astype(jnp.bfloat16).astype(jnp.float32)
    scalar = scalar * (1.0 / math.sqrt(HEAD_FEATURES))
    lanes = scalar.shape[1]
    spread = jnp.where(head_mask(heads, lanes)[None], scalar[:, None, :], 0.0)
    query_ref[:, pl.ds(0, lanes)] = spread.reshape(rows * heads, lanes).astype(jnp.bfloat16)
    points = [
        dot_rows(single, point_rows(weight_ref, 3 * HEAD_FEATURES, PQ, c)) for c in range(3)
    ]
    points = turn(points, rot, shift)
    width = PQ * heads
    square = jnp.zeros((rows, heads, width), jnp.float32)
    for c in range(3):
        spread = jnp.where(head_mask(heads, width)[None], points[c][:, None, :], 0.0)
        square = square + spread * spread
        rest = spread * (2.0 * weight)[None]
        for term in range(3):
            part = rest.astype(jnp.bfloat16)
            rest = rest - part.astype(jnp.float32)
            at = lanes + (3 * term + c) * width
            query_ref[:, pl.ds(at, width)] = part.reshape(rows * heads, width)
    square = jnp.sum(square, axis=-1, keepdims=True)
    for r in range(rows):
        within = jnp.where(rows_ref[pl.ds(0, 1), :] == chain_ref[me * rows + r], 1.0, 0.0)
        base_ref[r] = LOGIT_FACTOR * (bias_ref[r] + chain_offset * within - weight * square[r])


def attention_kernel(
    offsets,
    held_ref,
    other_ref,
    weight_ref,
    query_ref,
    base_ref,
    frame_ref,
    rot_ref,
    trans_ref,
    rows_ref,
    distance_ref,
    pair_ref,
    single_ref,
    local_ref,
    pair_weight_ref,
    gain_ref,
    left_ref,
    right_ref,
    out_ref,
    left_out_ref,
    right_out_ref,
    every_ref,
    pair_sum_ref,
):
    rows, total, feats = pair_ref.shape
    heads = weight_ref.shape[1]
    me = lax.axis_index("res")
    for ref, step in ((held_ref, 0), (other_ref, 1)):
        for e, o in enumerate(offsets):
            owner = me ^ (o ^ step)
            every_ref[pl.ds(pl.multiple_of(owner * rows, 8), rows), :] = ref[e].astype(jnp.float32)
    every = every_ref[...].astype(jnp.bfloat16)
    rot = [[rot_ref[c, pl.ds(d, 1), :] for d in range(3)] for c in range(3)]
    shift = [trans_ref[pl.ds(c, 1), :] for c in range(3)]

    key_at, value_at = HEAD_FEATURES, 2 * HEAD_FEATURES
    key_rows = weight_ref[pl.ds(key_at, HEAD_FEATURES)].reshape(HEAD_FEATURES * heads, -1)
    keys = dot_rows(key_rows, every).astype(jnp.bfloat16)
    offset = 3 * HEAD_FEATURES + 3 * PQ
    points = [dot_rows(point_rows(weight_ref, offset, PQ, c), every) for c in range(3)]
    points = [p.astype(jnp.bfloat16) for p in turn(points, rot, shift)]
    square = sum(jnp.square(p.astype(jnp.float32)) for p in points)
    square = jnp.sum(square.reshape(PQ, heads, total), axis=0)
    keys = jnp.concatenate([keys] + 3 * points, 0)
    weight = 0.5 * LOGIT_FACTOR * math.sqrt(2.0 / (9.0 * PQ)) * as_column(distance_ref[...])
    logits = dot(query_ref[...], keys).reshape(rows, heads, total)
    logits = LOGIT_FACTOR * logits + base_ref[...] - (weight * square)[None]
    present = rows_ref[pl.ds(1, 1), :] > 0
    logits = jnp.where(present[None], logits, -1000000000.0)
    logits = logits.reshape(rows * heads, total)
    exponent = jnp.exp(logits - jnp.max(logits, axis=-1, keepdims=True))
    attention = (exponent / jnp.sum(exponent, axis=-1, keepdims=True)).astype(jnp.bfloat16)

    for r in range(rows):
        pair_sum_ref[pl.ds(r * heads, heads), :] = dot(
            attention[r * heads : (r + 1) * heads], pair_ref[r]
        )

    def own_head(values):
        lanes = values.shape[0]
        mixed = dot_rows(attention, values).reshape(rows, heads, lanes)
        return jnp.sum(jnp.where(head_mask(heads, lanes)[None], mixed, 0.0), axis=1)

    value_rows = weight_ref[pl.ds(value_at, HEAD_FEATURES)].reshape(HEAD_FEATURES * heads, -1)
    scalar_out = own_head(dot_rows(value_rows, every).astype(jnp.bfloat16))
    offset = 3 * HEAD_FEATURES + 6 * PQ
    points = [dot_rows(point_rows(weight_ref, offset, PV, c), every) for c in range(3)]
    points = [own_head(p.astype(jnp.bfloat16)) for p in turn(points, rot, shift)]
    frame = frame_ref[...]
    centred = [points[c] - frame[:, 9 + c : 10 + c] for c in range(3)]
    local = [
        sum(frame[:, 3 * c + d : 3 * c + d + 1] * centred[c] for c in range(3)) for d in range(3)
    ]
    norm = jnp.sqrt(sum(jnp.square(v) for v in local) + 1.0)

    def product(values, rows_of_weight):
        return dot(jnp.concatenate(halves(values), 0), rows_of_weight)

    first = HEAD_FEATURES * heads
    update = product(scalar_out, local_ref[pl.ds(0, HEAD_FEATURES)].reshape(first, -1))
    for c in range(3):
        update = update + product(local[c], point_rows(local_ref, HEAD_FEATURES, PV, c))
    norm_rows = local_ref[pl.ds(HEAD_FEATURES + 3 * PV, PV)].reshape(PV * heads, -1)
    update = update + product(norm, norm_rows)
    pair_sum = jnp.concatenate(
        [pair_sum_ref[pl.ds(h, rows, stride=heads), :] for h in range(heads)], 1
    )
    update = update + product(pair_sum, pair_weight_ref[...])
    values = single_ref[...].astype(jnp.float32) + update[:rows] + update[rows:]
    single_out = layer_norm(values, gain_ref[...]).astype(jnp.bfloat16)
    out_ref[...] = single_out
    left_out_ref[...] = dot(single_out, left_ref[...]).astype(jnp.bfloat16)
    right_out_ref[...] = dot(single_out, right_ref[...]).astype(jnp.bfloat16)


def frame_kernel(
    step_ref,
    rows_ref,
    single_ref,
    velocity_ref,
    rot_ref,
    trans_ref,
    rot_out_ref,
    trans_out_ref,
    table_ref,
):
    rows = single_ref.shape[0]
    total = rot_ref.shape[2]
    me = lax.axis_index("res")
    table_ref[...] = jnp.zeros_like(table_ref)
    for c in range(3):
        for d in range(3):
            table_ref[pl.ds(3 * c + d, 1), :] = rot_ref[c, pl.ds(d, 1), :]
        table_ref[pl.ds(9 + c, 1), :] = trans_ref[pl.ds(c, 1), :]
    table_ref[pl.ds(12, 1), :] = jnp.where(rows_ref[pl.ds(1, 1), :] > 0, 1.0, 0.0)
    row = lax.broadcasted_iota(jnp.int32, (rows, total), 0)
    column = lax.broadcasted_iota(jnp.int32, (rows, total), 1)
    chosen = jnp.where(column == row + me * rows, 1.0, 0.0)
    frame = dot_rows(table_ref[...], chosen, HIGHEST)
    motion = dot_rows(velocity_ref[...], single_ref[...])
    live = frame[12:13]
    ratio = 1.0 / jnp.full((1, rows), STEPS - step_ref[0], jnp.int32).astype(jnp.float32)
    x, y, z = [ratio * jnp.tanh(motion[c : c + 1]) * live for c in range(3)]
    velocity = [ratio * motion[3 + c : 4 + c] * live for c in range(3)]
    angle_sq = x * x + y * y + z * z
    coefs = [jnp.zeros_like(angle_sq) for _ in range(3)]
    powers = jnp.ones_like(angle_sq)
    for order in range(8):
        parity = (-1.0) ** order
        coefs = [
            coef + powers * (parity / float(math.factorial(2 * order + 1 + k)))
            for k, coef in enumerate(coefs)
        ]
        powers = powers * angle_sq
    zero = jnp.zeros_like(x)
    cross = [[zero, -z, y], [z, zero, -x], [-y, x, zero]]
    square = [[sum(cross[a][b] * cross[b][c] for b in range(3)) for c in range(3)] for a in range(3)]
    one = [[jnp.ones_like(x) if a == b else zero for b in range(3)] for a in range(3)]

    def series(first, second):
        return [
            [one[a][b] + first * cross[a][b] + second * square[a][b] for b in range(3)]
            for a in range(3)
        ]

    turned, jacobian = series(coefs[0], coefs[1]), series(coefs[1], coefs[2])
    rot = [[frame[3 * a + b : 3 * a + b + 1] for b in range(3)] for a in range(3)]
    moved = [sum(jacobian[a][b] * velocity[b] for b in range(3)) for a in range(3)]
    for a in range(3):
        for c in range(3):
            rot_out_ref[a, pl.ds(c, 1), :] = sum(rot[a][b] * turned[b][c] for b in range(3))
        trans_out_ref[pl.ds(a, 1), :] = frame[9 + a : 10 + a] + sum(
            rot[a][b] * moved[b] for b in range(3)
        )


def in_vmem(count):
    return [pl.BlockSpec(memory_space=pltpu.VMEM)] * count


def attend(
    single,
    pair,
    rotations,
    translations,
    residue_chain_index,
    residue_move_mask,
    timestep,
    single_projection_weight,
    head_bias_weight,
    head_distance_weight,
    chain_logit_offset,
    local_output_weight,
    pair_output_weight,
    single_norm_gain,
    frame_velocity_weight,
    left_pair_weight,
    right_pair_weight,
):
    rows, total, feats = pair.shape
    heads = single_projection_weight.shape[1]
    width = single.shape[1]
    table = jnp.stack([residue_chain_index, residue_move_mask])
    gain = single_norm_gain[None]
    offsets, held, (table, gain) = gather_most(single, total // rows, (table, gain))
    weight = jnp.transpose(single_projection_weight, (2, 1, 0))
    local_weight = jnp.transpose(local_output_weight, (1, 0, 2))
    distance = head_distance_weight[None]
    depth = heads * (HEAD_FEATURES + 9 * PQ)
    bias = pl.pallas_call(
        bias_kernel,
        in_specs=in_vmem(2),
        out_specs=pl.BlockSpec(memory_space=pltpu.VMEM),
        out_shape=jax.ShapeDtypeStruct((rows, heads, total), jnp.float32),
        compiler_params=pltpu.CompilerParams(vmem_limit_bytes=16 * 1024 * 1024),
        cost_estimate=pl.CostEstimate(flops=10**9, bytes_accessed=6 * 10**6, transcendentals=0),
    )(jnp.transpose(head_bias_weight), pair)
    held, bias, local_weight = lax.optimization_barrier((held, bias, local_weight))
    other = exchange(held, total // rows, 1)
    query, base, frame = pl.pallas_call(
        query_kernel,
        in_specs=[pl.BlockSpec(memory_space=pltpu.SMEM)] + in_vmem(8),
        out_specs=tuple(in_vmem(3)),
        out_shape=(
            jax.ShapeDtypeStruct((rows * heads, depth), jnp.bfloat16),
            jax.ShapeDtypeStruct((rows, heads, total), jnp.float32),
            jax.ShapeDtypeStruct((rows, 16), jnp.float32),
        ),
        scratch_shapes=[pltpu.VMEM((16, total), jnp.float32)],
        compiler_params=pltpu.CompilerParams(vmem_limit_bytes=24 * 1024 * 1024),
        cost_estimate=pl.CostEstimate(flops=10**9, bytes_accessed=6 * 10**6, transcendentals=0),
    )(
        residue_chain_index,
        bias,
        single,
        weight,
        rotations,
        translations,
        table,
        distance,
        chain_logit_offset[None],
    )
    single_out, left_proj, right_proj = pl.pallas_call(
        functools.partial(attention_kernel, offsets),
        in_specs=in_vmem(17),
        out_specs=tuple(in_vmem(3)),
        out_shape=(
            jax.ShapeDtypeStruct((rows, width), jnp.bfloat16),
            jax.ShapeDtypeStruct((rows, feats), jnp.bfloat16),
            jax.ShapeDtypeStruct((rows, feats), jnp.bfloat16),
        ),
        scratch_shapes=[
            pltpu.VMEM((total, width), jnp.float32),
            pltpu.VMEM((rows * heads, feats), jnp.float32),
        ],
        compiler_params=pltpu.CompilerParams(vmem_limit_bytes=40 * 1024 * 1024),
        cost_estimate=pl.CostEstimate(flops=2 * 10**9, bytes_accessed=10**7, transcendentals=0),
    )(
        held,
        other,
        weight,
        query,
        base,
        frame,
        rotations,
        translations,
        table,
        distance,
        pair,
        single,
        local_weight,
        pair_output_weight.reshape(heads * feats, width),
        gain,
        left_pair_weight,
        right_pair_weight,
    )
    velocity_rows = jnp.transpose(frame_velocity_weight)
    rot_out, trans_out = pl.pallas_call(
        frame_kernel,
        in_specs=[pl.BlockSpec(memory_space=pltpu.SMEM)] + in_vmem(5),
        out_specs=tuple(in_vmem(2)),
        out_shape=(
            jax.ShapeDtypeStruct((3, 3, rows), jnp.float32),
            jax.ShapeDtypeStruct((3, rows), jnp.float32),
        ),
        scratch_shapes=[pltpu.VMEM((16, total), jnp.float32)],
        compiler_params=pltpu.CompilerParams(vmem_limit_bytes=4 * 1024 * 1024),
        cost_estimate=pl.CostEstimate(flops=10**6, bytes_accessed=10**5, transcendentals=0),
    )(
        timestep,
        table,
        single_out,
        velocity_rows,
        rotations,
        translations,
    )
    return single_out, rot_out, trans_out, left_proj, right_proj, table, 1


def attend_split(
    single,
    pair,
    rotations,
    translations,
    residue_chain_index,
    residue_move_mask,
    timestep,
    single_projection_weight,
    head_bias_weight,
    head_distance_weight,
    chain_logit_offset,
    local_output_weight,
    pair_output_weight,
    single_norm_gain,
    frame_velocity_weight,
    left_pair_weight,
    right_pair_weight,
):
    rows_dev = single.shape[0]
    col_count = pair.shape[1]
    total = rotations.shape[2]
    heads_here = single_projection_weight.shape[1]
    row_start = lax.axis_index("res") * rows_dev
    rot_all = jnp.transpose(rotations, (2, 0, 1))
    trans_all = jnp.transpose(translations)
    rot_own = lax.dynamic_slice_in_dim(rot_all, row_start, rows_dev, 0)
    trans_own = lax.dynamic_slice_in_dim(trans_all, row_start, rows_dev, 0)
    own_chain = lax.dynamic_slice_in_dim(residue_chain_index, row_start, rows_dev, 0)
    offset = 3 * HEAD_FEATURES
    feat_count = 2 * HEAD_FEATURES + 3 * PQ + 3 * PV
    count = total // rows_dev
    every_single = sorted_blocks(*gather_blocks(single, count)[:2]).reshape(total, -1)
    every_proj = jnp.einsum(
        "nd,dhf->nhf", every_single, single_projection_weight, preferred_element_type=jnp.float32
    )
    projected = lax.dynamic_slice_in_dim(every_proj, row_start, rows_dev, 0)
    packed_projection = key_features(every_proj, rot_all, trans_all)
    packed_projection = packed_projection.reshape(total, heads_here, feat_count)
    query_values = projected[:, :, 0:HEAD_FEATURES].astype(jnp.bfloat16)
    query_flattened = to_global(
        projected[:, :, offset : offset + 3 * PQ], rot_own, trans_own, PQ
    ).reshape(rows_dev, heads_here, 3 * PQ)
    bias_local = jnp.einsum(
        "rjc,ch->rhj", pair, head_bias_weight, preferred_element_type=jnp.float32
    ).astype(jnp.bfloat16)
    pair_head_bias = lax.all_to_all(
        bias_local, "head", split_axis=1, concat_axis=2, tiled=True
    ).astype(jnp.float32)
    within_chain = (own_chain[:, None] == residue_chain_index[None, :]).astype(jnp.float32)
    logit_matrix = local_logit_rows(
        query_values,
        query_flattened,
        packed_projection,
        pair_head_bias,
        within_chain,
        head_distance_weight,
        chain_logit_offset,
        residue_move_mask > 0,
    )
    peak = jnp.max(logit_matrix, axis=-1, keepdims=True)
    exponent = jnp.exp(logit_matrix - peak)
    attention = rounded(exponent / jnp.sum(exponent, axis=-1, keepdims=True))
    scalar_out = jnp.einsum(
        "rhn,nhc->rhc",
        attention,
        packed_projection[:, :, HEAD_FEATURES : 2 * HEAD_FEATURES],
        preferred_element_type=jnp.float32,
    )
    point_global = jnp.einsum(
        "rhn,nhp->rhp",
        attention.astype(jnp.float32),
        packed_projection[:, :, 2 * HEAD_FEATURES + 3 * PQ :].astype(jnp.float32),
        precision=HIGHEST,
    )
    update_local = local_points(scalar_out, point_global, rot_own, trans_own, local_output_weight)
    attention_cols = lax.all_to_all(attention, "head", split_axis=2, concat_axis=1, tiled=True)
    pair_attended = jnp.einsum(
        "rhj,rjc->rhc", attention_cols, pair, preferred_element_type=jnp.float32
    )
    update_pair = jnp.einsum(
        "rhc,hcd->rd", pair_attended, pair_output_weight.astype(jnp.float32), precision=HIGHEST
    )
    update = lax.psum(update_local + update_pair, "head")
    single_out = layer_norm(single.astype(jnp.float32) + update, single_norm_gain).astype(
        jnp.bfloat16
    )
    live_all = (residue_move_mask > 0).astype(jnp.float32)
    live_own = lax.dynamic_slice_in_dim(live_all, row_start, rows_dev, 0)
    step_ratio = 1.0 / (STEPS - timestep[0]).astype(jnp.float32)
    rot_out, trans_out = frame_step(
        single_out, frame_velocity_weight, rot_own, trans_own, live_own, step_ratio
    )
    left_proj = jnp.dot(single_out, left_pair_weight, preferred_element_type=jnp.float32).astype(
        jnp.bfloat16
    )
    right_proj = jnp.dot(single_out, right_pair_weight, preferred_element_type=jnp.float32).astype(
        jnp.bfloat16
    )
    live_rows = residue_move_mask[None]
    return single_out, rot_out, trans_out, left_proj, right_proj, live_rows, 0


def shards(
    single,
    pair,
    rotations,
    translations,
    residue_chain_index,
    residue_move_mask,
    timestep,
    single_projection_weight,
    head_bias_weight,
    head_distance_weight,
    chain_logit_offset,
    local_output_weight,
    pair_output_weight,
    single_norm_gain,
    frame_velocity_weight,
    left_pair_weight,
    right_pair_weight,
    pair_norm_gain,
    transition_hidden_weight,
    transition_middle_weight,
    transition_back_weight,
):
    rows_dev = single.shape[0]
    count = rotations.shape[2] // rows_dev
    whole_heads = lax.axis_size("head") == 1 and count >= 16 and count & (count - 1) == 0
    single_out, rot_out, trans_out, left_proj, right_proj, live_rows, live_at = (
        attend if whole_heads else attend_split
    )(
        single,
        pair,
        rotations,
        translations,
        residue_chain_index,
        residue_move_mask,
        timestep,
        single_projection_weight,
        head_bias_weight,
        head_distance_weight,
        chain_logit_offset,
        local_output_weight,
        pair_output_weight,
        single_norm_gain,
        frame_velocity_weight,
        left_pair_weight,
        right_pair_weight,
    )
    offsets, blocks, _ = gather_blocks(right_proj, count)
    if offsets is None:
        blocks = (blocks,)
    else:
        offsets = offsets + [o ^ 1 for o in offsets]
    pair_out = pair_transition(
        pair,
        left_proj,
        residue_move_mask,
        live_rows,
        live_at,
        pair_norm_gain,
        transition_hidden_weight,
        transition_middle_weight,
        transition_back_weight,
        offsets,
        blocks,
    )
    return (single_out, rot_out, trans_out, pair_out)


def solution(mesh):
    placed = (
        P(("batch", "res"), None),
        P(("batch", "res"), "head", None),
        P(None, None, "batch"),
        P(None, "batch"),
        P(),
        P("batch"),
        P(),
        P(None, "head", None),
        P(),
        P("head"),
        P("head"),
        P("head", None, None),
        P(),
        P(),
        P(),
        P(),
        P(),
        P(),
        P(),
        P(),
        P(),
    )
    return jax.shard_map(
        shards,
        mesh=mesh,
        in_specs=placed,
        out_specs=(
            P(("batch", "res"), None),
            P(None, None, ("batch", "res")),
            P(None, ("batch", "res")),
            P(("batch", "res"), "head", None),
        ),
        check_vma=False,
    )
```

```python
import functools
import math

import jax
import jax.numpy as jnp
from jax import lax
from jax.experimental import pallas as pl
from jax.experimental.pallas import tpu as pltpu
from jax.sharding import PartitionSpec as P

HEAD_FEATURES = 16
PQ = 8
PV = 12
STEPS = 8


LOGIT_FACTOR = math.sqrt(1.0 / 3.0)
HIGHEST = lax.Precision.HIGHEST


def rounded(values):
    return lax.optimization_barrier(values.astype(jnp.bfloat16))


def layer_norm(values, gain):
    centre = jnp.mean(values, axis=-1, keepdims=True)
    variance = jnp.mean(jnp.square(values - centre), axis=-1, keepdims=True)
    return (values - centre) * lax.rsqrt(variance + 1e-05) * gain


def to_global(local, rot_cols, trans_cols, npoints):
    rows_here = local.shape[0]
    heads_here = local.shape[1]
    points = local.reshape(rows_here, heads_here, npoints, 3)
    turned = jnp.sum(rot_cols[:, None, None, :, :] * points[:, :, :, None, :], axis=-1)
    return turned + trans_cols[:, None, None, :]


def key_features(projected, rot_cols, trans_cols):
    rows_here = projected.shape[0]
    heads_here = projected.shape[1]
    offset = 3 * HEAD_FEATURES
    key_points = to_global(
        projected[:, :, offset + 3 * PQ : offset + 6 * PQ], rot_cols, trans_cols, PQ
    )
    value_points = to_global(projected[:, :, offset + 6 * PQ :], rot_cols, trans_cols, PV)
    packed_projection = jnp.concatenate(
        [
            projected[:, :, HEAD_FEATURES : 3 * HEAD_FEATURES],
            key_points.reshape(rows_here, heads_here, 3 * PQ),
            value_points.reshape(rows_here, heads_here, 3 * PV),
        ],
        axis=-1,
    )
    return rounded(
        packed_projection.reshape(rows_here, heads_here * (2 * HEAD_FEATURES + 3 * PQ + 3 * PV))
    )


def hat_matrix(vectors):
    comp_x = vectors[:, 0]
    comp_y = vectors[:, 1]
    comp_z = vectors[:, 2]
    zeros_col = jnp.zeros_like(comp_x)
    first_row = jnp.stack([zeros_col, -comp_z, comp_y], -1)
    second_row = jnp.stack([comp_z, zeros_col, -comp_x], -1)
    third_row = jnp.stack([-comp_y, comp_x, zeros_col], -1)
    return jnp.stack([first_row, second_row, third_row], 1)


def frame_step(single_out, frame_velocity_weight, rot_cols, trans_cols, live_rows, step_ratio):
    motion = jnp.dot(single_out, frame_velocity_weight, preferred_element_type=jnp.float32)
    rotvec = step_ratio * jnp.tanh(motion[:, 0:3]) * live_rows[:, None]
    velocity = step_ratio * motion[:, 3:6] * live_rows[:, None]
    angle_sq = jnp.sum(jnp.square(rotvec), -1)
    coef_a = jnp.zeros_like(angle_sq)
    coef_b = jnp.zeros_like(angle_sq)
    coef_c = jnp.zeros_like(angle_sq)
    powers = jnp.ones_like(angle_sq)
    for order in range(8):
        parity = (-1.0) ** order
        coef_a = coef_a + powers * (parity / float(math.factorial(2 * order + 1)))
        coef_b = coef_b + powers * (parity / float(math.factorial(2 * order + 2)))
        coef_c = coef_c + powers * (parity / float(math.factorial(2 * order + 3)))
        powers = powers * angle_sq
    cross_mat = hat_matrix(rotvec)
    cross_sq = jnp.einsum("nab,nbc->nac", cross_mat, cross_mat, precision=HIGHEST)
    identity = jnp.eye(3, dtype=jnp.float32)[None]
    turn = identity + coef_a[:, None, None] * cross_mat + coef_b[:, None, None] * cross_sq
    jacobian = identity + coef_b[:, None, None] * cross_mat + coef_c[:, None, None] * cross_sq
    new_rot = jnp.einsum("nab,nbc->nac", rot_cols, turn, precision=HIGHEST)
    moved = jnp.einsum("nab,nb->na", jacobian, velocity, precision=HIGHEST)
    new_trans = trans_cols + jnp.einsum("nab,nb->na", rot_cols, moved, precision=HIGHEST)
    return (jnp.transpose(new_rot, (1, 2, 0)), jnp.transpose(new_trans))


def local_logit_rows(
    query_values,
    query_flattened,
    packed_projection,
    pair_head_bias,
    within_chain,
    distance_weight,
    chain_offset,
    key_present,
):
    key_scalar = packed_projection[:, :, 0:HEAD_FEATURES]
    key_flat = packed_projection[:, :, 2 * HEAD_FEATURES : 2 * HEAD_FEATURES + 3 * PQ].astype(
        jnp.float32
    )
    scalar_logit_term = jnp.einsum(
        "rhc,nhc->rhn", query_values, key_scalar, preferred_element_type=jnp.float32
    )
    cross_term = jnp.einsum("rhp,nhp->rhn", query_flattened, key_flat, precision=HIGHEST)
    key_square = jnp.transpose(jnp.sum(jnp.square(key_flat), -1))
    point_distance = (
        jnp.sum(jnp.square(query_flattened), -1)[:, :, None] + key_square[None] - 2.0 * cross_term
    )
    point_term_weight = math.sqrt(2.0 / (9.0 * PQ))
    logit_matrix = LOGIT_FACTOR * (
        scalar_logit_term / math.sqrt(HEAD_FEATURES)
        + pair_head_bias
        + chain_offset[None, :, None] * within_chain[:, None, :]
        - (0.5 * point_term_weight * distance_weight)[None, :, None] * point_distance
    )
    return jnp.where(key_present[None, None, :], logit_matrix, -1000000000.0)


def local_points(scalar_out, point_global, rot_own, trans_own, local_output_weight):
    rows_dev = scalar_out.shape[0]
    heads_here = scalar_out.shape[1]
    point_global = point_global.reshape(rows_dev, heads_here, PV, 3)
    centred = point_global - trans_own[:, None, None, :]
    point_local = jnp.sum(rot_own[:, None, None, :, :] * centred[:, :, :, :, None], axis=-2)
    point_norm = jnp.sqrt(jnp.sum(jnp.square(point_local), -1) + 1.0)
    features = jnp.concatenate(
        [scalar_out, point_local.reshape(rows_dev, heads_here, 3 * PV), point_norm], -1
    )
    return jnp.einsum(
        "rhf,hfd->rd", features, local_output_weight.astype(jnp.float32), precision=HIGHEST
    )


def exchange(block, count, step):
    return lax.ppermute(block, "res", [(k, k ^ step) for k in range(count)])


def gather_most(block, count, tied=()):
    held, offsets = block[None], [0]
    quarter = count // 4
    step = quarter // 2
    while step > 1:
        held = jnp.concatenate([held, exchange(held, count, step)], 0)
        offsets = offsets + [o ^ step for o in offsets]
        step //= 2
    held, tied = lax.optimization_barrier((held, tied))
    parts = [held] + [exchange(held, count, k * quarter) for k in (3, 2, 1)]
    held = jnp.concatenate(parts, 0)
    return [o ^ (k * quarter) for k in (0, 3, 2, 1) for o in offsets], held, tied


def gather_blocks(block, count, tied=()):
    if count < 16 or count & (count - 1):
        return None, lax.all_gather(block, "res", axis=0), tied
    offsets, held, tied = gather_most(block, count, tied)
    return offsets, (held, exchange(held, count, 1)), tied


def sorted_blocks(offsets, blocks):
    if offsets is None:
        return blocks
    held, other = blocks
    entries = [held[e] for e in range(len(offsets))] + [other[e] for e in range(len(offsets))]
    every = dict(zip(offsets + [o ^ 1 for o in offsets], entries))
    both = jnp.stack([every[o] for o in range(len(every))])
    index = lax.axis_index("res")
    bit = 1
    while bit < len(every):
        halves = both.reshape((-1, 2, bit) + held.shape[1:])
        both = jnp.where((index & bit) > 0, halves[:, ::-1], halves).reshape(both.shape)
        bit *= 2
    return both


def transition_kernel(
    rows_block,
    rows_part,
    rows_dev,
    offsets,
    live_at,
    live_ref,
    pair_ref,
    left_ref,
    live_row_ref,
    gain_ref,
    hidden_ref,
    middle_ref,
    back_ref,
    *rest,
):
    block_refs, (out_ref, right_ref, live_cols_ref, centring_ref) = rest[:-4], rest[-4:]
    step = pl.program_id(0)
    cols, feats = pair_ref.shape[1:]
    me = lax.axis_index("res")
    col_start = lax.axis_index("head") * cols

    @pl.when(step == 0)
    def _():
        at = 0
        for ref in block_refs:
            for e in range(ref.shape[0]):
                value = ref[e].astype(jnp.float32)
                value = value - jnp.mean(value, axis=-1, keepdims=True)
                owner = me ^ offsets[at] if offsets is not None else at
                at += 1
                right_ref[pl.ds(pl.multiple_of(owner * rows_dev, 8), rows_dev), :] = value
        live_row = live_row_ref[pl.ds(live_at, 1), :].astype(jnp.float32)
        wide = jnp.broadcast_to(live_row, (feats, live_row.shape[1]))
        live_cols_ref[...] = jnp.where(jnp.transpose(wide) > 0, 1.0, 0.0)
        across = lax.broadcasted_iota(jnp.int32, (feats, feats), 0)
        down = lax.broadcasted_iota(jnp.int32, (feats, feats), 1)
        centring_ref[...] = (jnp.where(across == down, 1.0, 0.0) - 1.0 / feats).astype(jnp.bfloat16)

    columns = pl.ds(pl.multiple_of(col_start, 8), cols)
    right = right_ref[columns, :][None]
    live_cols = live_cols_ref[columns, :][None]
    left = left_ref[...].astype(jnp.float32)
    left = left - jnp.mean(left, axis=-1, keepdims=True)
    for first in range(0, rows_block, rows_part):
        at = step * rows_block + first
        pair_rows = pair_ref[pl.ds(at, rows_part)]
        pair = pair_rows.reshape(rows_part * cols, feats)
        centred = jnp.dot(pair, centring_ref[...], preferred_element_type=jnp.float32)
        centred = centred.reshape(rows_part, cols, feats)
        centred = centred + left[first : first + rows_part][:, None, :] + right
        variance = jnp.mean(centred * centred, axis=-1, keepdims=True)
        scale = lax.rsqrt(variance + 1e-05)
        gains = [
            gain_ref[...] * jnp.where(live_ref[me * rows_dev + at + r] > 0, 1.0, 0.0)
            for r in range(rows_part)
        ]
        normed = centred * scale * jnp.stack(gains)
        normed = normed.astype(jnp.bfloat16).reshape(rows_part * cols, feats)
        hidden_one = jnp.dot(normed, hidden_ref[...], preferred_element_type=jnp.float32)
        hidden_one = jnp.maximum(hidden_one.astype(jnp.bfloat16), 0)
        hidden_two = jnp.dot(hidden_one, middle_ref[...], preferred_element_type=jnp.float32)
        hidden_two = jnp.maximum(hidden_two.astype(jnp.bfloat16), 0)
        branch = jnp.dot(hidden_two, back_ref[...], preferred_element_type=jnp.float32)
        branch = branch.reshape(rows_part, cols, feats)
        out_ref[pl.ds(first, rows_part)] = (
            pair_rows.astype(jnp.float32) + live_cols * branch
        ).astype(jnp.bfloat16)


def pair_transition(
    pair, left_proj, move_mask, live_rows, live_at, gain, hidden, middle, back, offsets, blocks
):
    rows_dev, cols, feats = pair.shape
    total = move_mask.shape[0]
    rows_part = math.gcd(rows_dev, max(1, 1536 // cols))
    rows_block = rows_part * math.gcd(rows_dev // rows_part, 3)
    left_wide = left_proj.reshape(rows_dev // rows_block, rows_block, feats)
    whole = lambda *shape: pl.BlockSpec(shape, lambda i: (0,) * len(shape))
    kernel = functools.partial(
        transition_kernel, rows_block, rows_part, rows_dev, offsets, live_at
    )
    macs = rows_dev * cols * (2 * feats * feats + 2 * feats * hidden.shape[1] + hidden.shape[1] ** 2)
    return pl.pallas_call(
        kernel,
        grid=(rows_dev // rows_block,),
        in_specs=[
            pl.BlockSpec(memory_space=pltpu.SMEM),
            pl.BlockSpec(memory_space=pltpu.VMEM),
            pl.BlockSpec((None, rows_block, feats), lambda i: (i, 0, 0)),
            whole(*live_rows.shape),
            whole(1, feats),
            whole(*hidden.shape),
            whole(*middle.shape),
            whole(*back.shape),
        ]
        + [whole(*b.shape) for b in blocks],
        out_specs=pl.BlockSpec((rows_block, cols, feats), lambda i: (i, 0, 0)),
        out_shape=jax.ShapeDtypeStruct(pair.shape, pair.dtype),
        scratch_shapes=[
            pltpu.VMEM((total, feats), jnp.float32),
            pltpu.VMEM((total, feats), jnp.float32),
            pltpu.VMEM((feats, feats), jnp.bfloat16),
        ],
        compiler_params=pltpu.CompilerParams(vmem_limit_bytes=32 * 1024 * 1024),
        cost_estimate=pl.CostEstimate(
            flops=2 * macs, bytes_accessed=2 * pair.size * 2, transcendentals=0
        ),
    )(
        move_mask,
        pair,
        left_wide,
        live_rows,
        gain[None],
        hidden,
        middle,
        back,
        *blocks,
    )


def dot(left, right):
    return jnp.dot(left, right, preferred_element_type=jnp.float32)


def dot_rows(left, right, precision=None):
    return lax.dot_general(
        left, right, (((1,), (1,)), ((), ())), preferred_element_type=jnp.float32, precision=precision
    )


def head_mask(heads, lanes):
    head = lax.broadcasted_iota(jnp.int32, (heads, lanes), 0)
    lane = lax.broadcasted_iota(jnp.int32, (heads, lanes), 1)
    return lax.rem(lane, heads) == head


def as_column(row):
    size = row.shape[1]
    return jnp.sum(jnp.where(head_mask(size, size), row, 0.0), axis=1, keepdims=True)


def halves(values):
    high = values.astype(jnp.bfloat16)
    return high, (values - high.astype(jnp.float32)).astype(jnp.bfloat16)


def point_rows(weight_ref, offset, npoints, coord):
    return jnp.concatenate([weight_ref[offset + 3 * p + coord] for p in range(npoints)], 0)


def turn(parts, rot, shift):
    return [
        rot[c][0] * parts[0] + rot[c][1] * parts[1] + rot[c][2] * parts[2] + shift[c]
        for c in range(3)
    ]


def bias_kernel(weight_ref, pair_ref, out_ref):
    for r in range(pair_ref.shape[0]):
        bias = dot_rows(weight_ref[...], pair_ref[r])
        out_ref[r] = bias.astype(jnp.bfloat16).astype(jnp.float32)


def query_kernel(
    chain_ref,
    bias_ref,
    single_ref,
    weight_ref,
    rot_ref,
    trans_ref,
    rows_ref,
    distance_ref,
    offset_ref,
    query_ref,
    base_ref,
    frame_ref,
    table_ref,
):
    rows, heads, total = bias_ref.shape
    me = lax.axis_index("res")
    table_ref[...] = jnp.zeros_like(table_ref)
    for c in range(3):
        for d in range(3):
            table_ref[pl.ds(3 * c + d, 1), :] = rot_ref[c, pl.ds(d, 1), :]
        table_ref[pl.ds(9 + c, 1), :] = trans_ref[pl.ds(c, 1), :]
    row = lax.broadcasted_iota(jnp.int32, (rows, total), 0)
    column = lax.broadcasted_iota(jnp.int32, (rows, total), 1)
    chosen = jnp.where(column == row + me * rows, 1.0, 0.0)
    frame = dot_rows(chosen, table_ref[...], HIGHEST)
    frame_ref[...] = frame
    rot = [[frame[:, 3 * c + d : 3 * c + d + 1] for d in range(3)] for c in range(3)]
    shift = [frame[:, 9 + c : 10 + c] for c in range(3)]

    weight = 0.5 * math.sqrt(2.0 / (9.0 * PQ)) * as_column(distance_ref[...])
    chain_offset = as_column(offset_ref[...])
    single = single_ref[...]
    scalar_rows = weight_ref[pl.ds(0, HEAD_FEATURES)].reshape(HEAD_FEATURES * heads, -1)
    scalar = dot_rows(single, scalar_rows).astype(jnp.bfloat16).astype(jnp.float32)
    scalar = scalar * (1.0 / math.sqrt(HEAD_FEATURES))
    lanes = scalar.shape[1]
    spread = jnp.where(head_mask(heads, lanes)[None], scalar[:, None, :], 0.0)
    query_ref[:, pl.ds(0, lanes)] = spread.reshape(rows * heads, lanes).astype(jnp.bfloat16)
    points = [
        dot_rows(single, point_rows(weight_ref, 3 * HEAD_FEATURES, PQ, c)) for c in range(3)
    ]
    points = turn(points, rot, shift)
    width = PQ * heads
    square = jnp.zeros((rows, heads, width), jnp.float32)
    for c in range(3):
        spread = jnp.where(head_mask(heads, width)[None], points[c][:, None, :], 0.0)
        square = square + spread * spread
        rest = spread * (2.0 * weight)[None]
        for term in range(3):
            part = rest.astype(jnp.bfloat16)
            rest = rest - part.astype(jnp.float32)
            at = lanes + (3 * term + c) * width
            query_ref[:, pl.ds(at, width)] = part.reshape(rows * heads, width)
    square = jnp.sum(square, axis=-1, keepdims=True)
    for r in range(rows):
        within = jnp.where(rows_ref[pl.ds(0, 1), :] == chain_ref[me * rows + r], 1.0, 0.0)
        base_ref[r] = LOGIT_FACTOR * (bias_ref[r] + chain_offset * within - weight * square[r])


def attention_kernel(
    offsets,
    held_ref,
    other_ref,
    weight_ref,
    query_ref,
    base_ref,
    frame_ref,
    rot_ref,
    trans_ref,
    rows_ref,
    distance_ref,
    pair_ref,
    single_ref,
    local_ref,
    pair_weight_ref,
    gain_ref,
    left_ref,
    right_ref,
    out_ref,
    copy_ref,
    left_out_ref,
    right_out_ref,
    every_ref,
    pair_sum_ref,
):
    rows, total, feats = pair_ref.shape
    heads = weight_ref.shape[1]
    me = lax.axis_index("res")
    for ref, step in ((held_ref, 0), (other_ref, 1)):
        for e, o in enumerate(offsets):
            owner = me ^ (o ^ step)
            every_ref[pl.ds(pl.multiple_of(owner * rows, 8), rows), :] = ref[e].astype(jnp.float32)
    every = every_ref[...].astype(jnp.bfloat16)
    rot = [[rot_ref[c, pl.ds(d, 1), :] for d in range(3)] for c in range(3)]
    shift = [trans_ref[pl.ds(c, 1), :] for c in range(3)]

    key_at, value_at = HEAD_FEATURES, 2 * HEAD_FEATURES
    key_rows = weight_ref[pl.ds(key_at, HEAD_FEATURES)].reshape(HEAD_FEATURES * heads, -1)
    keys = dot_rows(key_rows, every).astype(jnp.bfloat16)
    offset = 3 * HEAD_FEATURES + 3 * PQ
    points = [dot_rows(point_rows(weight_ref, offset, PQ, c), every) for c in range(3)]
    points = [p.astype(jnp.bfloat16) for p in turn(points, rot, shift)]
    square = sum(jnp.square(p.astype(jnp.float32)) for p in points)
    square = jnp.sum(square.reshape(PQ, heads, total), axis=0)
    keys = jnp.concatenate([keys] + 3 * points, 0)
    weight = 0.5 * LOGIT_FACTOR * math.sqrt(2.0 / (9.0 * PQ)) * as_column(distance_ref[...])
    logits = dot(query_ref[...], keys).reshape(rows, heads, total)
    logits = LOGIT_FACTOR * logits + base_ref[...] - (weight * square)[None]
    present = rows_ref[pl.ds(1, 1), :] > 0
    logits = jnp.where(present[None], logits, -1000000000.0)
    logits = logits.reshape(rows * heads, total)
    exponent = jnp.exp(logits - jnp.max(logits, axis=-1, keepdims=True))
    attention = (exponent / jnp.sum(exponent, axis=-1, keepdims=True)).astype(jnp.bfloat16)

    for r in range(rows):
        pair_sum_ref[pl.ds(r * heads, heads), :] = dot(
            attention[r * heads : (r + 1) * heads], pair_ref[r]
        )

    def own_head(values):
        lanes = values.shape[0]
        mixed = dot_rows(attention, values).reshape(rows, heads, lanes)
        return jnp.sum(jnp.where(head_mask(heads, lanes)[None], mixed, 0.0), axis=1)

    value_rows = weight_ref[pl.ds(value_at, HEAD_FEATURES)].reshape(HEAD_FEATURES * heads, -1)
    scalar_out = own_head(dot_rows(value_rows, every).astype(jnp.bfloat16))
    offset = 3 * HEAD_FEATURES + 6 * PQ
    points = [dot_rows(point_rows(weight_ref, offset, PV, c), every) for c in range(3)]
    points = [own_head(p.astype(jnp.bfloat16)) for p in turn(points, rot, shift)]
    frame = frame_ref[...]
    centred = [points[c] - frame[:, 9 + c : 10 + c] for c in range(3)]
    local = [
        sum(frame[:, 3 * c + d : 3 * c + d + 1] * centred[c] for c in range(3)) for d in range(3)
    ]
    norm = jnp.sqrt(sum(jnp.square(v) for v in local) + 1.0)

    def product(values, rows_of_weight):
        return dot(jnp.concatenate(halves(values), 0), rows_of_weight)

    first = HEAD_FEATURES * heads
    update = product(scalar_out, local_ref[pl.ds(0, HEAD_FEATURES)].reshape(first, -1))
    for c in range(3):
        update = update + product(local[c], point_rows(local_ref, HEAD_FEATURES, PV, c))
    norm_rows = local_ref[pl.ds(HEAD_FEATURES + 3 * PV, PV)].reshape(PV * heads, -1)
    update = update + product(norm, norm_rows)
    pair_sum = jnp.concatenate(
        [pair_sum_ref[pl.ds(h, rows, stride=heads), :] for h in range(heads)], 1
    )
    update = update + product(pair_sum, pair_weight_ref[...])
    values = single_ref[...].astype(jnp.float32) + update[:rows] + update[rows:]
    single_out = layer_norm(values, gain_ref[...]).astype(jnp.bfloat16)
    out_ref[...] = single_out
    copy_ref[...] = single_out
    left_out_ref[...] = dot(single_out, left_ref[...]).astype(jnp.bfloat16)
    right_out_ref[...] = dot(single_out, right_ref[...]).astype(jnp.bfloat16)


def frame_kernel(
    rows_ref,
    single_ref,
    velocity_ref,
    rot_ref,
    trans_ref,
    rot_out_ref,
    trans_out_ref,
    table_ref,
):
    rows = single_ref.shape[0]
    total = rot_ref.shape[2]
    me = lax.axis_index("res")
    table_ref[...] = jnp.zeros_like(table_ref)
    for c in range(3):
        for d in range(3):
            table_ref[pl.ds(3 * c + d, 1), :] = rot_ref[c, pl.ds(d, 1), :]
        table_ref[pl.ds(9 + c, 1), :] = trans_ref[pl.ds(c, 1), :]
    table_ref[pl.ds(12, 1), :] = jnp.where(rows_ref[pl.ds(1, 1), :] > 0, 1.0, 0.0)
    row = lax.broadcasted_iota(jnp.int32, (rows, total), 0)
    column = lax.broadcasted_iota(jnp.int32, (rows, total), 1)
    chosen = jnp.where(column == row + me * rows, 1.0, 0.0)
    frame = dot_rows(table_ref[...], chosen, HIGHEST)
    motion = dot_rows(velocity_ref[...], single_ref[...])
    live = frame[12:13]
    ratio = 1.0 / (STEPS - rows_ref[pl.ds(2, 1), :].astype(jnp.float32))[:, :rows]
    x, y, z = [ratio * jnp.tanh(motion[c : c + 1]) * live for c in range(3)]
    velocity = [ratio * motion[3 + c : 4 + c] * live for c in range(3)]
    angle_sq = x * x + y * y + z * z
    coefs = [jnp.zeros_like(angle_sq) for _ in range(3)]
    powers = jnp.ones_like(angle_sq)
    for order in range(8):
        parity = (-1.0) ** order
        coefs = [
            coef + powers * (parity / float(math.factorial(2 * order + 1 + k)))
            for k, coef in enumerate(coefs)
        ]
        powers = powers * angle_sq
    zero = jnp.zeros_like(x)
    cross = [[zero, -z, y], [z, zero, -x], [-y, x, zero]]
    square = [[sum(cross[a][b] * cross[b][c] for b in range(3)) for c in range(3)] for a in range(3)]
    one = [[jnp.ones_like(x) if a == b else zero for b in range(3)] for a in range(3)]

    def series(first, second):
        return [
            [one[a][b] + first * cross[a][b] + second * square[a][b] for b in range(3)]
            for a in range(3)
        ]

    turned, jacobian = series(coefs[0], coefs[1]), series(coefs[1], coefs[2])
    rot = [[frame[3 * a + b : 3 * a + b + 1] for b in range(3)] for a in range(3)]
    moved = [sum(jacobian[a][b] * velocity[b] for b in range(3)) for a in range(3)]
    for a in range(3):
        for c in range(3):
            rot_out_ref[a, pl.ds(c, 1), :] = sum(rot[a][b] * turned[b][c] for b in range(3))
        trans_out_ref[pl.ds(a, 1), :] = frame[9 + a : 10 + a] + sum(
            rot[a][b] * moved[b] for b in range(3)
        )


def in_vmem(count):
    return [pl.BlockSpec(memory_space=pltpu.VMEM)] * count


def attend(
    single,
    pair,
    rotations,
    translations,
    residue_chain_index,
    residue_move_mask,
    timestep,
    single_projection_weight,
    head_bias_weight,
    head_distance_weight,
    chain_logit_offset,
    local_output_weight,
    pair_output_weight,
    single_norm_gain,
    frame_velocity_weight,
    left_pair_weight,
    right_pair_weight,
):
    rows, total, feats = pair.shape
    heads = single_projection_weight.shape[1]
    width = single.shape[1]
    step_row = jnp.broadcast_to(timestep, (total,))
    table = jnp.stack([residue_chain_index, residue_move_mask, step_row])
    gain = single_norm_gain[None]
    offsets, held, (table, gain) = gather_most(single, total // rows, (table, gain))
    weight = jnp.transpose(single_projection_weight, (2, 1, 0))
    local_weight = jnp.transpose(local_output_weight, (1, 0, 2))
    distance = head_distance_weight[None]
    depth = heads * (HEAD_FEATURES + 9 * PQ)
    bias = pl.pallas_call(
        bias_kernel,
        in_specs=in_vmem(2),
        out_specs=pl.BlockSpec(memory_space=pltpu.VMEM),
        out_shape=jax.ShapeDtypeStruct((rows, heads, total), jnp.float32),
        compiler_params=pltpu.CompilerParams(vmem_limit_bytes=16 * 1024 * 1024),
        cost_estimate=pl.CostEstimate(flops=10**9, bytes_accessed=6 * 10**6, transcendentals=0),
    )(jnp.transpose(head_bias_weight), pair)
    held, bias, local_weight = lax.optimization_barrier((held, bias, local_weight))
    other = exchange(held, total // rows, 1)
    query, base, frame = pl.pallas_call(
        query_kernel,
        in_specs=[pl.BlockSpec(memory_space=pltpu.SMEM)] + in_vmem(8),
        out_specs=tuple(in_vmem(3)),
        out_shape=(
            jax.ShapeDtypeStruct((rows * heads, depth), jnp.bfloat16),
            jax.ShapeDtypeStruct((rows, heads, total), jnp.float32),
            jax.ShapeDtypeStruct((rows, 16), jnp.float32),
        ),
        scratch_shapes=[pltpu.VMEM((16, total), jnp.float32)],
        compiler_params=pltpu.CompilerParams(vmem_limit_bytes=24 * 1024 * 1024),
        cost_estimate=pl.CostEstimate(flops=10**9, bytes_accessed=6 * 10**6, transcendentals=0),
    )(
        residue_chain_index,
        bias,
        single,
        weight,
        rotations,
        translations,
        table,
        distance,
        chain_logit_offset[None],
    )
    single_out, single_copy, left_proj, right_proj = pl.pallas_call(
        functools.partial(attention_kernel, offsets),
        in_specs=in_vmem(17),
        out_specs=tuple(in_vmem(4)),
        out_shape=(
            jax.ShapeDtypeStruct((rows, width), jnp.bfloat16),
            jax.ShapeDtypeStruct((rows, width), jnp.bfloat16),
            jax.ShapeDtypeStruct((rows, feats), jnp.bfloat16),
            jax.ShapeDtypeStruct((rows, feats), jnp.bfloat16),
        ),
        scratch_shapes=[
            pltpu.VMEM((total, width), jnp.float32),
            pltpu.VMEM((rows * heads, feats), jnp.float32),
        ],
        compiler_params=pltpu.CompilerParams(vmem_limit_bytes=40 * 1024 * 1024),
        cost_estimate=pl.CostEstimate(flops=2 * 10**9, bytes_accessed=10**7, transcendentals=0),
    )(
        held,
        other,
        weight,
        query,
        base,
        frame,
        rotations,
        translations,
        table,
        distance,
        pair,
        single,
        local_weight,
        pair_output_weight.reshape(heads * feats, width),
        gain,
        left_pair_weight,
        right_pair_weight,
    )
    velocity_rows = jnp.transpose(frame_velocity_weight)
    rot_out, trans_out = pl.pallas_call(
        frame_kernel,
        in_specs=in_vmem(5),
        out_specs=tuple(in_vmem(2)),
        out_shape=(
            jax.ShapeDtypeStruct((3, 3, rows), jnp.float32),
            jax.ShapeDtypeStruct((3, rows), jnp.float32),
        ),
        scratch_shapes=[pltpu.VMEM((16, total), jnp.float32)],
        compiler_params=pltpu.CompilerParams(vmem_limit_bytes=4 * 1024 * 1024),
        cost_estimate=pl.CostEstimate(flops=10**6, bytes_accessed=10**5, transcendentals=0),
    )(
        table,
        single_copy,
        velocity_rows,
        rotations,
        translations,
    )
    return single_out, rot_out, trans_out, left_proj, right_proj, table, 1


def attend_split(
    single,
    pair,
    rotations,
    translations,
    residue_chain_index,
    residue_move_mask,
    timestep,
    single_projection_weight,
    head_bias_weight,
    head_distance_weight,
    chain_logit_offset,
    local_output_weight,
    pair_output_weight,
    single_norm_gain,
    frame_velocity_weight,
    left_pair_weight,
    right_pair_weight,
):
    rows_dev = single.shape[0]
    col_count = pair.shape[1]
    total = rotations.shape[2]
    heads_here = single_projection_weight.shape[1]
    row_start = lax.axis_index("res") * rows_dev
    rot_all = jnp.transpose(rotations, (2, 0, 1))
    trans_all = jnp.transpose(translations)
    rot_own = lax.dynamic_slice_in_dim(rot_all, row_start, rows_dev, 0)
    trans_own = lax.dynamic_slice_in_dim(trans_all, row_start, rows_dev, 0)
    own_chain = lax.dynamic_slice_in_dim(residue_chain_index, row_start, rows_dev, 0)
    offset = 3 * HEAD_FEATURES
    feat_count = 2 * HEAD_FEATURES + 3 * PQ + 3 * PV
    count = total // rows_dev
    every_single = sorted_blocks(*gather_blocks(single, count)[:2]).reshape(total, -1)
    every_proj = jnp.einsum(
        "nd,dhf->nhf", every_single, single_projection_weight, preferred_element_type=jnp.float32
    )
    projected = lax.dynamic_slice_in_dim(every_proj, row_start, rows_dev, 0)
    packed_projection = key_features(every_proj, rot_all, trans_all)
    packed_projection = packed_projection.reshape(total, heads_here, feat_count)
    query_values = projected[:, :, 0:HEAD_FEATURES].astype(jnp.bfloat16)
    query_flattened = to_global(
        projected[:, :, offset : offset + 3 * PQ], rot_own, trans_own, PQ
    ).reshape(rows_dev, heads_here, 3 * PQ)
    bias_local = jnp.einsum(
        "rjc,ch->rhj", pair, head_bias_weight, preferred_element_type=jnp.float32
    ).astype(jnp.bfloat16)
    pair_head_bias = lax.all_to_all(
        bias_local, "head", split_axis=1, concat_axis=2, tiled=True
    ).astype(jnp.float32)
    within_chain = (own_chain[:, None] == residue_chain_index[None, :]).astype(jnp.float32)
    logit_matrix = local_logit_rows(
        query_values,
        query_flattened,
        packed_projection,
        pair_head_bias,
        within_chain,
        head_distance_weight,
        chain_logit_offset,
        residue_move_mask > 0,
    )
    peak = jnp.max(logit_matrix, axis=-1, keepdims=True)
    exponent = jnp.exp(logit_matrix - peak)
    attention = rounded(exponent / jnp.sum(exponent, axis=-1, keepdims=True))
    scalar_out = jnp.einsum(
        "rhn,nhc->rhc",
        attention,
        packed_projection[:, :, HEAD_FEATURES : 2 * HEAD_FEATURES],
        preferred_element_type=jnp.float32,
    )
    point_global = jnp.einsum(
        "rhn,nhp->rhp",
        attention.astype(jnp.float32),
        packed_projection[:, :, 2 * HEAD_FEATURES + 3 * PQ :].astype(jnp.float32),
        precision=HIGHEST,
    )
    update_local = local_points(scalar_out, point_global, rot_own, trans_own, local_output_weight)
    attention_cols = lax.all_to_all(attention, "head", split_axis=2, concat_axis=1, tiled=True)
    pair_attended = jnp.einsum(
        "rhj,rjc->rhc", attention_cols, pair, preferred_element_type=jnp.float32
    )
    update_pair = jnp.einsum(
        "rhc,hcd->rd", pair_attended, pair_output_weight.astype(jnp.float32), precision=HIGHEST
    )
    update = lax.psum(update_local + update_pair, "head")
    single_out = layer_norm(single.astype(jnp.float32) + update, single_norm_gain).astype(
        jnp.bfloat16
    )
    live_all = (residue_move_mask > 0).astype(jnp.float32)
    live_own = lax.dynamic_slice_in_dim(live_all, row_start, rows_dev, 0)
    step_ratio = 1.0 / (STEPS - timestep[0]).astype(jnp.float32)
    rot_out, trans_out = frame_step(
        single_out, frame_velocity_weight, rot_own, trans_own, live_own, step_ratio
    )
    left_proj = jnp.dot(single_out, left_pair_weight, preferred_element_type=jnp.float32).astype(
        jnp.bfloat16
    )
    right_proj = jnp.dot(single_out, right_pair_weight, preferred_element_type=jnp.float32).astype(
        jnp.bfloat16
    )
    live_rows = residue_move_mask[None]
    return single_out, rot_out, trans_out, left_proj, right_proj, live_rows, 0


def shards(
    single,
    pair,
    rotations,
    translations,
    residue_chain_index,
    residue_move_mask,
    timestep,
    single_projection_weight,
    head_bias_weight,
    head_distance_weight,
    chain_logit_offset,
    local_output_weight,
    pair_output_weight,
    single_norm_gain,
    frame_velocity_weight,
    left_pair_weight,
    right_pair_weight,
    pair_norm_gain,
    transition_hidden_weight,
    transition_middle_weight,
    transition_back_weight,
):
    rows_dev = single.shape[0]
    count = rotations.shape[2] // rows_dev
    whole_heads = lax.axis_size("head") == 1 and count >= 16 and count & (count - 1) == 0
    single_out, rot_out, trans_out, left_proj, right_proj, live_rows, live_at = (
        attend if whole_heads else attend_split
    )(
        single,
        pair,
        rotations,
        translations,
        residue_chain_index,
        residue_move_mask,
        timestep,
        single_projection_weight,
        head_bias_weight,
        head_distance_weight,
        chain_logit_offset,
        local_output_weight,
        pair_output_weight,
        single_norm_gain,
        frame_velocity_weight,
        left_pair_weight,
        right_pair_weight,
    )
    offsets, blocks, _ = gather_blocks(right_proj, count)
    if offsets is None:
        blocks = (blocks,)
    else:
        offsets = offsets + [o ^ 1 for o in offsets]
    pair_out = pair_transition(
        pair,
        left_proj,
        residue_move_mask,
        live_rows,
        live_at,
        pair_norm_gain,
        transition_hidden_weight,
        transition_middle_weight,
        transition_back_weight,
        offsets,
        blocks,
    )
    return (single_out, rot_out, trans_out, pair_out)


def solution(mesh):
    placed = (
        P(("batch", "res"), None),
        P(("batch", "res"), "head", None),
        P(None, None, "batch"),
        P(None, "batch"),
        P(),
        P("batch"),
        P(),
        P(None, "head", None),
        P(),
        P("head"),
        P("head"),
        P("head", None, None),
        P(),
        P(),
        P(),
        P(),
        P(),
        P(),
        P(),
        P(),
        P(),
    )
    return jax.shard_map(
        shards,
        mesh=mesh,
        in_specs=placed,
        out_specs=(
            P(("batch", "res"), None),
            P(None, None, ("batch", "res")),
            P(None, ("batch", "res")),
            P(("batch", "res"), "head", None),
        ),
        check_vma=False,
    )
```

```python
import functools
import math

import jax
import jax.numpy as jnp
from jax import lax
from jax.experimental import pallas as pl
from jax.experimental.pallas import tpu as pltpu
from jax.sharding import PartitionSpec as P

HEAD_FEATURES = 16
PQ = 8
PV = 12
STEPS = 8


LOGIT_FACTOR = math.sqrt(1.0 / 3.0)
HIGHEST = lax.Precision.HIGHEST


def rounded(values):
    return lax.optimization_barrier(values.astype(jnp.bfloat16))


def layer_norm(values, gain):
    centre = jnp.mean(values, axis=-1, keepdims=True)
    variance = jnp.mean(jnp.square(values - centre), axis=-1, keepdims=True)
    return (values - centre) * lax.rsqrt(variance + 1e-05) * gain


def to_global(local, rot_cols, trans_cols, npoints):
    rows_here = local.shape[0]
    heads_here = local.shape[1]
    points = local.reshape(rows_here, heads_here, npoints, 3)
    turned = jnp.sum(rot_cols[:, None, None, :, :] * points[:, :, :, None, :], axis=-1)
    return turned + trans_cols[:, None, None, :]


def key_features(projected, rot_cols, trans_cols):
    rows_here = projected.shape[0]
    heads_here = projected.shape[1]
    offset = 3 * HEAD_FEATURES
    key_points = to_global(
        projected[:, :, offset + 3 * PQ : offset + 6 * PQ], rot_cols, trans_cols, PQ
    )
    value_points = to_global(projected[:, :, offset + 6 * PQ :], rot_cols, trans_cols, PV)
    packed_projection = jnp.concatenate(
        [
            projected[:, :, HEAD_FEATURES : 3 * HEAD_FEATURES],
            key_points.reshape(rows_here, heads_here, 3 * PQ),
            value_points.reshape(rows_here, heads_here, 3 * PV),
        ],
        axis=-1,
    )
    return rounded(
        packed_projection.reshape(rows_here, heads_here * (2 * HEAD_FEATURES + 3 * PQ + 3 * PV))
    )


def hat_matrix(vectors):
    comp_x = vectors[:, 0]
    comp_y = vectors[:, 1]
    comp_z = vectors[:, 2]
    zeros_col = jnp.zeros_like(comp_x)
    first_row = jnp.stack([zeros_col, -comp_z, comp_y], -1)
    second_row = jnp.stack([comp_z, zeros_col, -comp_x], -1)
    third_row = jnp.stack([-comp_y, comp_x, zeros_col], -1)
    return jnp.stack([first_row, second_row, third_row], 1)


def frame_step(single_out, frame_velocity_weight, rot_cols, trans_cols, live_rows, step_ratio):
    motion = jnp.dot(single_out, frame_velocity_weight, preferred_element_type=jnp.float32)
    rotvec = step_ratio * jnp.tanh(motion[:, 0:3]) * live_rows[:, None]
    velocity = step_ratio * motion[:, 3:6] * live_rows[:, None]
    angle_sq = jnp.sum(jnp.square(rotvec), -1)
    coef_a = jnp.zeros_like(angle_sq)
    coef_b = jnp.zeros_like(angle_sq)
    coef_c = jnp.zeros_like(angle_sq)
    powers = jnp.ones_like(angle_sq)
    for order in range(8):
        parity = (-1.0) ** order
        coef_a = coef_a + powers * (parity / float(math.factorial(2 * order + 1)))
        coef_b = coef_b + powers * (parity / float(math.factorial(2 * order + 2)))
        coef_c = coef_c + powers * (parity / float(math.factorial(2 * order + 3)))
        powers = powers * angle_sq
    cross_mat = hat_matrix(rotvec)
    cross_sq = jnp.einsum("nab,nbc->nac", cross_mat, cross_mat, precision=HIGHEST)
    identity = jnp.eye(3, dtype=jnp.float32)[None]
    turn = identity + coef_a[:, None, None] * cross_mat + coef_b[:, None, None] * cross_sq
    jacobian = identity + coef_b[:, None, None] * cross_mat + coef_c[:, None, None] * cross_sq
    new_rot = jnp.einsum("nab,nbc->nac", rot_cols, turn, precision=HIGHEST)
    moved = jnp.einsum("nab,nb->na", jacobian, velocity, precision=HIGHEST)
    new_trans = trans_cols + jnp.einsum("nab,nb->na", rot_cols, moved, precision=HIGHEST)
    return (jnp.transpose(new_rot, (1, 2, 0)), jnp.transpose(new_trans))


def local_logit_rows(
    query_values,
    query_flattened,
    packed_projection,
    pair_head_bias,
    within_chain,
    distance_weight,
    chain_offset,
    key_present,
):
    key_scalar = packed_projection[:, :, 0:HEAD_FEATURES]
    key_flat = packed_projection[:, :, 2 * HEAD_FEATURES : 2 * HEAD_FEATURES + 3 * PQ].astype(
        jnp.float32
    )
    scalar_logit_term = jnp.einsum(
        "rhc,nhc->rhn", query_values, key_scalar, preferred_element_type=jnp.float32
    )
    cross_term = jnp.einsum("rhp,nhp->rhn", query_flattened, key_flat, precision=HIGHEST)
    key_square = jnp.transpose(jnp.sum(jnp.square(key_flat), -1))
    point_distance = (
        jnp.sum(jnp.square(query_flattened), -1)[:, :, None] + key_square[None] - 2.0 * cross_term
    )
    point_term_weight = math.sqrt(2.0 / (9.0 * PQ))
    logit_matrix = LOGIT_FACTOR * (
        scalar_logit_term / math.sqrt(HEAD_FEATURES)
        + pair_head_bias
        + chain_offset[None, :, None] * within_chain[:, None, :]
        - (0.5 * point_term_weight * distance_weight)[None, :, None] * point_distance
    )
    return jnp.where(key_present[None, None, :], logit_matrix, -1000000000.0)


def local_points(scalar_out, point_global, rot_own, trans_own, local_output_weight):
    rows_dev = scalar_out.shape[0]
    heads_here = scalar_out.shape[1]
    point_global = point_global.reshape(rows_dev, heads_here, PV, 3)
    centred = point_global - trans_own[:, None, None, :]
    point_local = jnp.sum(rot_own[:, None, None, :, :] * centred[:, :, :, :, None], axis=-2)
    point_norm = jnp.sqrt(jnp.sum(jnp.square(point_local), -1) + 1.0)
    features = jnp.concatenate(
        [scalar_out, point_local.reshape(rows_dev, heads_here, 3 * PV), point_norm], -1
    )
    return jnp.einsum(
        "rhf,hfd->rd", features, local_output_weight.astype(jnp.float32), precision=HIGHEST
    )


def exchange(block, count, step):
    return lax.ppermute(block, "res", [(k, k ^ step) for k in range(count)])


def gather_most(block, count, tied=()):
    held, offsets = block[None], [0]
    quarter = count // 4
    step = quarter // 2
    while step > 1:
        held = jnp.concatenate([held, exchange(held, count, step)], 0)
        offsets = offsets + [o ^ step for o in offsets]
        step //= 2
    held, tied = lax.optimization_barrier((held, tied))
    parts = [held] + [exchange(held, count, k * quarter) for k in (3, 2, 1)]
    held = jnp.concatenate(parts, 0)
    return [o ^ (k * quarter) for k in (0, 3, 2, 1) for o in offsets], held, tied


def gather_blocks(block, count, tied=()):
    if count < 16 or count & (count - 1):
        return None, lax.all_gather(block, "res", axis=0), tied
    offsets, held, tied = gather_most(block, count, tied)
    return offsets, (held, exchange(held, count, 1)), tied


def sorted_blocks(offsets, blocks):
    if offsets is None:
        return blocks
    held, other = blocks
    entries = [held[e] for e in range(len(offsets))] + [other[e] for e in range(len(offsets))]
    every = dict(zip(offsets + [o ^ 1 for o in offsets], entries))
    both = jnp.stack([every[o] for o in range(len(every))])
    index = lax.axis_index("res")
    bit = 1
    while bit < len(every):
        halves = both.reshape((-1, 2, bit) + held.shape[1:])
        both = jnp.where((index & bit) > 0, halves[:, ::-1], halves).reshape(both.shape)
        bit *= 2
    return both


def transition_kernel(
    rows_block,
    rows_part,
    rows_dev,
    offsets,
    live_at,
    live_ref,
    pair_ref,
    left_ref,
    live_row_ref,
    gain_ref,
    hidden_ref,
    middle_ref,
    back_ref,
    *rest,
):
    block_refs, (out_ref, right_ref, live_cols_ref, centring_ref) = rest[:-4], rest[-4:]
    step = pl.program_id(0)
    cols, feats = pair_ref.shape[1:]
    me = lax.axis_index("res")
    col_start = lax.axis_index("head") * cols
    total = right_ref.shape[0]

    @pl.when(step == 0)
    def _():
        at = 0
        for ref in block_refs:
            for e in range(ref.shape[0]):
                value = ref[e].astype(jnp.float32)
                value = value - jnp.mean(value, axis=-1, keepdims=True)
                owner = me ^ offsets[at] if offsets is not None else at
                at += 1
                right_ref[pl.ds(pl.multiple_of(owner * rows_dev, 8), rows_dev), :] = value
        live_row = live_row_ref[pl.ds(live_at, 1), pl.ds(0, total)].astype(jnp.float32)
        wide = jnp.broadcast_to(live_row, (feats, live_row.shape[1]))
        live_cols_ref[...] = jnp.where(jnp.transpose(wide) > 0, 1.0, 0.0)
        across = lax.broadcasted_iota(jnp.int32, (feats, feats), 0)
        down = lax.broadcasted_iota(jnp.int32, (feats, feats), 1)
        centring_ref[...] = (jnp.where(across == down, 1.0, 0.0) - 1.0 / feats).astype(jnp.bfloat16)

    columns = pl.ds(pl.multiple_of(col_start, 8), cols)
    right = right_ref[columns, :][None]
    live_cols = live_cols_ref[columns, :][None]
    left = left_ref[...].astype(jnp.float32)
    left = left - jnp.mean(left, axis=-1, keepdims=True)
    for first in range(0, rows_block, rows_part):
        at = step * rows_block + first
        pair_rows = pair_ref[pl.ds(at, rows_part)]
        pair = pair_rows.reshape(rows_part * cols, feats)
        centred = jnp.dot(pair, centring_ref[...], preferred_element_type=jnp.float32)
        centred = centred.reshape(rows_part, cols, feats)
        centred = centred + left[first : first + rows_part][:, None, :] + right
        variance = jnp.mean(centred * centred, axis=-1, keepdims=True)
        scale = lax.rsqrt(variance + 1e-05)
        gains = [
            gain_ref[...] * jnp.where(live_ref[me * rows_dev + at + r] > 0, 1.0, 0.0)
            for r in range(rows_part)
        ]
        normed = centred * scale * jnp.stack(gains)
        normed = normed.astype(jnp.bfloat16).reshape(rows_part * cols, feats)
        hidden_one = jnp.dot(normed, hidden_ref[...], preferred_element_type=jnp.float32)
        hidden_one = jnp.maximum(hidden_one.astype(jnp.bfloat16), 0)
        hidden_two = jnp.dot(hidden_one, middle_ref[...], preferred_element_type=jnp.float32)
        hidden_two = jnp.maximum(hidden_two.astype(jnp.bfloat16), 0)
        branch = jnp.dot(hidden_two, back_ref[...], preferred_element_type=jnp.float32)
        branch = branch.reshape(rows_part, cols, feats)
        out_ref[pl.ds(first, rows_part)] = (
            pair_rows.astype(jnp.float32) + live_cols * branch
        ).astype(jnp.bfloat16)


def pair_transition(
    pair, left_proj, move_mask, live_rows, live_at, gain, hidden, middle, back, offsets, blocks
):
    rows_dev, cols, feats = pair.shape
    total = move_mask.shape[0]
    rows_part = math.gcd(rows_dev, max(1, 1536 // cols))
    rows_block = rows_part * math.gcd(rows_dev // rows_part, 3)
    left_wide = left_proj.reshape(rows_dev // rows_block, rows_block, feats)
    whole = lambda *shape: pl.BlockSpec(shape, lambda i: (0,) * len(shape))
    kernel = functools.partial(
        transition_kernel, rows_block, rows_part, rows_dev, offsets, live_at
    )
    macs = rows_dev * cols * (2 * feats * feats + 2 * feats * hidden.shape[1] + hidden.shape[1] ** 2)
    return pl.pallas_call(
        kernel,
        grid=(rows_dev // rows_block,),
        in_specs=[
            pl.BlockSpec(memory_space=pltpu.SMEM),
            pl.BlockSpec(memory_space=pltpu.VMEM),
            pl.BlockSpec((None, rows_block, feats), lambda i: (i, 0, 0)),
            whole(*live_rows.shape),
            whole(1, feats),
            whole(*hidden.shape),
            whole(*middle.shape),
            whole(*back.shape),
        ]
        + [whole(*b.shape) for b in blocks],
        out_specs=pl.BlockSpec((rows_block, cols, feats), lambda i: (i, 0, 0)),
        out_shape=jax.ShapeDtypeStruct(pair.shape, pair.dtype),
        scratch_shapes=[
            pltpu.VMEM((total, feats), jnp.float32),
            pltpu.VMEM((total, feats), jnp.float32),
            pltpu.VMEM((feats, feats), jnp.bfloat16),
        ],
        compiler_params=pltpu.CompilerParams(vmem_limit_bytes=32 * 1024 * 1024),
        cost_estimate=pl.CostEstimate(
            flops=2 * macs, bytes_accessed=2 * pair.size * 2, transcendentals=0
        ),
    )(
        move_mask,
        pair,
        left_wide,
        live_rows,
        gain[None],
        hidden,
        middle,
        back,
        *blocks,
    )


def dot(left, right):
    return jnp.dot(left, right, preferred_element_type=jnp.float32)


def dot_rows(left, right, precision=None):
    return lax.dot_general(
        left, right, (((1,), (1,)), ((), ())), preferred_element_type=jnp.float32, precision=precision
    )


def head_mask(heads, lanes):
    head = lax.broadcasted_iota(jnp.int32, (heads, lanes), 0)
    lane = lax.broadcasted_iota(jnp.int32, (heads, lanes), 1)
    return lax.rem(lane, heads) == head


def as_column(row):
    size = row.shape[1]
    return jnp.sum(jnp.where(head_mask(size, size), row, 0.0), axis=1, keepdims=True)


def halves(values):
    high = values.astype(jnp.bfloat16)
    return high, (values - high.astype(jnp.float32)).astype(jnp.bfloat16)


def point_rows(weight_ref, offset, npoints, coord):
    return jnp.concatenate([weight_ref[offset + 3 * p + coord] for p in range(npoints)], 0)


def turn(parts, rot, shift):
    return [
        rot[c][0] * parts[0] + rot[c][1] * parts[1] + rot[c][2] * parts[2] + shift[c]
        for c in range(3)
    ]


def bias_kernel(weight_ref, pair_ref, out_ref, copy_ref):
    count = pair_ref.shape[0]
    first = pl.program_id(0) * count
    for r in range(count):
        bias = dot_rows(weight_ref[...], pair_ref[r])
        out_ref[first + r] = bias.astype(jnp.bfloat16).astype(jnp.float32)
    copy_ref[pl.ds(first, count)] = pair_ref[...]


def query_kernel(
    chain_ref,
    bias_ref,
    single_ref,
    weight_ref,
    rot_ref,
    trans_ref,
    rows_ref,
    distance_ref,
    offset_ref,
    query_ref,
    base_ref,
    frame_ref,
    table_ref,
):
    rows, heads, total = bias_ref.shape
    me = lax.axis_index("res")
    table_ref[...] = jnp.zeros_like(table_ref)
    for c in range(3):
        for d in range(3):
            table_ref[pl.ds(3 * c + d, 1), :] = rot_ref[c, pl.ds(d, 1), :]
        table_ref[pl.ds(9 + c, 1), :] = trans_ref[pl.ds(c, 1), :]
    row = lax.broadcasted_iota(jnp.int32, (rows, total), 0)
    column = lax.broadcasted_iota(jnp.int32, (rows, total), 1)
    chosen = jnp.where(column == row + me * rows, 1.0, 0.0)
    frame = dot_rows(chosen, table_ref[...], HIGHEST)
    frame_ref[...] = frame
    rot = [[frame[:, 3 * c + d : 3 * c + d + 1] for d in range(3)] for c in range(3)]
    shift = [frame[:, 9 + c : 10 + c] for c in range(3)]

    weight = 0.5 * math.sqrt(2.0 / (9.0 * PQ)) * as_column(distance_ref[...])
    chain_offset = as_column(offset_ref[...])
    single = single_ref[...]
    scalar_rows = weight_ref[pl.ds(0, HEAD_FEATURES)].reshape(HEAD_FEATURES * heads, -1)
    scalar = dot_rows(single, scalar_rows).astype(jnp.bfloat16).astype(jnp.float32)
    scalar = scalar * (1.0 / math.sqrt(HEAD_FEATURES))
    lanes = scalar.shape[1]
    spread = jnp.where(head_mask(heads, lanes)[None], scalar[:, None, :], 0.0)
    query_ref[:, pl.ds(0, lanes)] = spread.reshape(rows * heads, lanes).astype(jnp.bfloat16)
    points = [
        dot_rows(single, point_rows(weight_ref, 3 * HEAD_FEATURES, PQ, c)) for c in range(3)
    ]
    points = turn(points, rot, shift)
    width = PQ * heads
    square = jnp.zeros((rows, heads, width), jnp.float32)
    for c in range(3):
        spread = jnp.where(head_mask(heads, width)[None], points[c][:, None, :], 0.0)
        square = square + spread * spread
        rest = spread * (2.0 * weight)[None]
        for term in range(3):
            part = rest.astype(jnp.bfloat16)
            rest = rest - part.astype(jnp.float32)
            at = lanes + (3 * term + c) * width
            query_ref[:, pl.ds(at, width)] = part.reshape(rows * heads, width)
    square = jnp.sum(square, axis=-1, keepdims=True)
    own_row = rows_ref[pl.ds(0, 1), pl.ds(0, total)]
    for r in range(rows):
        within = jnp.where(own_row == chain_ref[me * rows + r], 1.0, 0.0)
        base_ref[r] = LOGIT_FACTOR * (bias_ref[r] + chain_offset * within - weight * square[r])


def attention_kernel(
    offsets,
    held_ref,
    other_ref,
    weight_ref,
    query_ref,
    base_ref,
    frame_ref,
    rot_ref,
    trans_ref,
    rows_ref,
    distance_ref,
    pair_ref,
    single_ref,
    local_ref,
    pair_weight_ref,
    gain_ref,
    left_ref,
    right_ref,
    out_ref,
    copy_ref,
    left_out_ref,
    right_out_ref,
    every_ref,
    pair_sum_ref,
):
    rows, total, feats = pair_ref.shape
    heads = weight_ref.shape[1]
    me = lax.axis_index("res")
    for ref, step in ((held_ref, 0), (other_ref, 1)):
        for e, o in enumerate(offsets):
            owner = me ^ (o ^ step)
            every_ref[pl.ds(pl.multiple_of(owner * rows, 8), rows), :] = ref[e].astype(jnp.float32)
    every = every_ref[...].astype(jnp.bfloat16)
    rot = [[rot_ref[c, pl.ds(d, 1), :] for d in range(3)] for c in range(3)]
    shift = [trans_ref[pl.ds(c, 1), :] for c in range(3)]

    scalars, key_points = HEAD_FEATURES * heads, PQ * heads
    offset = 3 * HEAD_FEATURES + 3 * PQ
    weight_rows = [weight_ref[pl.ds(HEAD_FEATURES, 2 * HEAD_FEATURES)].reshape(2 * scalars, -1)]
    weight_rows += [point_rows(weight_ref, offset, PQ, c) for c in range(3)]
    offset = offset + 3 * PQ
    weight_rows += [point_rows(weight_ref, offset, PV, c) for c in range(3)]
    projected = dot_rows(jnp.concatenate(weight_rows, 0), every)
    parts, at = [], 0
    for size in [scalars] * 2 + [key_points] * 3 + [PV * heads] * 3:
        parts.append(projected[at : at + size])
        at += size
    keys = parts[0].astype(jnp.bfloat16)
    points = [p.astype(jnp.bfloat16) for p in turn(parts[2:5], rot, shift)]
    square = sum(jnp.square(p.astype(jnp.float32)) for p in points)
    square = jnp.sum(square.reshape(PQ, heads, total), axis=0)
    keys = jnp.concatenate([keys] + 3 * points, 0)
    weight = 0.5 * LOGIT_FACTOR * math.sqrt(2.0 / (9.0 * PQ)) * as_column(distance_ref[...])
    logits = dot(query_ref[...], keys).reshape(rows, heads, total)
    logits = LOGIT_FACTOR * logits + base_ref[...] - (weight * square)[None]
    present = rows_ref[pl.ds(1, 1), pl.ds(0, total)] > 0
    logits = jnp.where(present[None], logits, -1000000000.0)
    logits = logits.reshape(rows * heads, total)
    exponent = jnp.exp(logits - jnp.max(logits, axis=-1, keepdims=True))
    attention = (exponent / jnp.sum(exponent, axis=-1, keepdims=True)).astype(jnp.bfloat16)

    for r in range(rows):
        pair_sum_ref[pl.ds(r * heads, heads), :] = dot(
            attention[r * heads : (r + 1) * heads], pair_ref[r]
        )

    def own_head(values):
        lanes = values.shape[0]
        mixed = dot_rows(attention, values).reshape(rows, heads, lanes)
        return jnp.sum(jnp.where(head_mask(heads, lanes)[None], mixed, 0.0), axis=1)

    scalar_out = own_head(parts[1].astype(jnp.bfloat16))
    points = [own_head(p.astype(jnp.bfloat16)) for p in turn(parts[5:8], rot, shift)]
    frame = frame_ref[...]
    centred = [points[c] - frame[:, 9 + c : 10 + c] for c in range(3)]
    local = [
        sum(frame[:, 3 * c + d : 3 * c + d + 1] * centred[c] for c in range(3)) for d in range(3)
    ]
    norm = jnp.sqrt(sum(jnp.square(v) for v in local) + 1.0)

    def product(values, rows_of_weight):
        return dot(jnp.concatenate(halves(values), 0), rows_of_weight)

    first = HEAD_FEATURES * heads
    update = product(scalar_out, local_ref[pl.ds(0, HEAD_FEATURES)].reshape(first, -1))
    for c in range(3):
        update = update + product(local[c], point_rows(local_ref, HEAD_FEATURES, PV, c))
    norm_rows = local_ref[pl.ds(HEAD_FEATURES + 3 * PV, PV)].reshape(PV * heads, -1)
    update = update + product(norm, norm_rows)
    pair_sum = jnp.concatenate(
        [pair_sum_ref[pl.ds(h, rows, stride=heads), :] for h in range(heads)], 1
    )
    update = update + product(pair_sum, pair_weight_ref[...])
    values = single_ref[...].astype(jnp.float32) + update[:rows] + update[rows:]
    single_out = layer_norm(values, gain_ref[...][None]).astype(jnp.bfloat16)
    out_ref[...] = single_out
    copy_ref[...] = single_out
    left_out_ref[...] = dot(single_out, left_ref[...]).astype(jnp.bfloat16)
    right_out_ref[...] = dot(single_out, right_ref[...]).astype(jnp.bfloat16)


def frame_kernel(
    rows_ref,
    single_ref,
    velocity_ref,
    rot_ref,
    trans_ref,
    rot_out_ref,
    trans_out_ref,
    table_ref,
):
    rows = single_ref.shape[0]
    total = rot_ref.shape[2]
    me = lax.axis_index("res")
    table_ref[...] = jnp.zeros_like(table_ref)
    for c in range(3):
        for d in range(3):
            table_ref[pl.ds(3 * c + d, 1), :] = rot_ref[c, pl.ds(d, 1), :]
        table_ref[pl.ds(9 + c, 1), :] = trans_ref[pl.ds(c, 1), :]
    table_ref[pl.ds(12, 1), :] = jnp.where(rows_ref[pl.ds(1, 1), pl.ds(0, total)] > 0, 1.0, 0.0)
    row = lax.broadcasted_iota(jnp.int32, (rows, total), 0)
    column = lax.broadcasted_iota(jnp.int32, (rows, total), 1)
    chosen = jnp.where(column == row + me * rows, 1.0, 0.0)
    frame = dot_rows(table_ref[...], chosen, HIGHEST)
    motion = dot_rows(velocity_ref[...], single_ref[...])
    live = frame[12:13]
    ratio = 1.0 / (STEPS - rows_ref[pl.ds(2, 1), :].astype(jnp.float32))[:, :rows]
    x, y, z = [ratio * jnp.tanh(motion[c : c + 1]) * live for c in range(3)]
    velocity = [ratio * motion[3 + c : 4 + c] * live for c in range(3)]
    angle_sq = x * x + y * y + z * z
    coefs = [jnp.zeros_like(angle_sq) for _ in range(3)]
    powers = jnp.ones_like(angle_sq)
    for order in range(8):
        parity = (-1.0) ** order
        coefs = [
            coef + powers * (parity / float(math.factorial(2 * order + 1 + k)))
            for k, coef in enumerate(coefs)
        ]
        powers = powers * angle_sq
    zero = jnp.zeros_like(x)
    cross = [[zero, -z, y], [z, zero, -x], [-y, x, zero]]
    square = [[sum(cross[a][b] * cross[b][c] for b in range(3)) for c in range(3)] for a in range(3)]
    one = [[jnp.ones_like(x) if a == b else zero for b in range(3)] for a in range(3)]

    def series(first, second):
        return [
            [one[a][b] + first * cross[a][b] + second * square[a][b] for b in range(3)]
            for a in range(3)
        ]

    turned, jacobian = series(coefs[0], coefs[1]), series(coefs[1], coefs[2])
    rot = [[frame[3 * a + b : 3 * a + b + 1] for b in range(3)] for a in range(3)]
    moved = [sum(jacobian[a][b] * velocity[b] for b in range(3)) for a in range(3)]
    for a in range(3):
        for c in range(3):
            rot_out_ref[a, pl.ds(c, 1), :] = sum(rot[a][b] * turned[b][c] for b in range(3))
        trans_out_ref[pl.ds(a, 1), :] = frame[9 + a : 10 + a] + sum(
            rot[a][b] * moved[b] for b in range(3)
        )


def stacked_rows(*rows):
    longest = max(row.shape[0] for row in rows)
    wide = [
        row if row.shape[0] in (1, longest) else jnp.pad(row, (0, longest - row.shape[0]))
        for row in rows
    ]
    wide = [jnp.broadcast_to(row, (longest,)) for row in wide]
    at = lax.broadcasted_iota(jnp.int32, (len(rows), longest), 0)
    table = jnp.broadcast_to(wide[0][None], (len(rows), longest))
    for k in range(1, len(rows)):
        table = jnp.where(at == k, wide[k][None], table)
    return table


def in_vmem(count):
    return [pl.BlockSpec(memory_space=pltpu.VMEM)] * count


def attend(
    single,
    pair,
    rotations,
    translations,
    residue_chain_index,
    residue_move_mask,
    timestep,
    single_projection_weight,
    head_bias_weight,
    head_distance_weight,
    chain_logit_offset,
    local_output_weight,
    pair_output_weight,
    single_norm_gain,
    frame_velocity_weight,
    left_pair_weight,
    right_pair_weight,
):
    rows, total, feats = pair.shape
    heads = single_projection_weight.shape[1]
    width = single.shape[1]
    table = stacked_rows(residue_chain_index, residue_move_mask, timestep)
    offsets, held, table = gather_most(single, total // rows, table)
    weight = jnp.transpose(single_projection_weight, (2, 1, 0))
    local_weight = jnp.transpose(local_output_weight, (1, 0, 2))
    distance = head_distance_weight[None]
    depth = heads * (HEAD_FEATURES + 9 * PQ)
    part = math.gcd(rows, 8)
    bias, pair = pl.pallas_call(
        bias_kernel,
        grid=(rows // part,),
        in_specs=[
            pl.BlockSpec((heads, feats), lambda i: (0, 0)),
            pl.BlockSpec((part, total, feats), lambda i: (i, 0, 0)),
        ],
        out_specs=tuple(in_vmem(2)),
        out_shape=(
            jax.ShapeDtypeStruct((rows, heads, total), jnp.float32),
            jax.ShapeDtypeStruct(pair.shape, pair.dtype),
        ),
        compiler_params=pltpu.CompilerParams(vmem_limit_bytes=51200 * 1024),
        cost_estimate=pl.CostEstimate(flops=10**9, bytes_accessed=6 * 10**6, transcendentals=0),
    )(jnp.transpose(head_bias_weight), pair)
    held, bias, pair, local_weight = lax.optimization_barrier((held, bias, pair, local_weight))
    other = exchange(held, total // rows, 1)
    query, base, frame = pl.pallas_call(
        query_kernel,
        in_specs=[pl.BlockSpec(memory_space=pltpu.SMEM)] + in_vmem(8),
        out_specs=tuple(in_vmem(3)),
        out_shape=(
            jax.ShapeDtypeStruct((rows * heads, depth), jnp.bfloat16),
            jax.ShapeDtypeStruct((rows, heads, total), jnp.float32),
            jax.ShapeDtypeStruct((rows, 16), jnp.float32),
        ),
        scratch_shapes=[pltpu.VMEM((16, total), jnp.float32)],
        compiler_params=pltpu.CompilerParams(vmem_limit_bytes=24 * 1024 * 1024),
        cost_estimate=pl.CostEstimate(flops=10**9, bytes_accessed=6 * 10**6, transcendentals=0),
    )(
        residue_chain_index,
        bias,
        single,
        weight,
        rotations,
        translations,
        table,
        distance,
        chain_logit_offset[None],
    )
    single_out, single_copy, left_proj, right_proj = pl.pallas_call(
        functools.partial(attention_kernel, offsets),
        in_specs=in_vmem(17),
        out_specs=tuple(in_vmem(4)),
        out_shape=(
            jax.ShapeDtypeStruct((rows, width), jnp.bfloat16),
            jax.ShapeDtypeStruct((rows, width), jnp.bfloat16),
            jax.ShapeDtypeStruct((rows, feats), jnp.bfloat16),
            jax.ShapeDtypeStruct((rows, feats), jnp.bfloat16),
        ),
        scratch_shapes=[
            pltpu.VMEM((total, width), jnp.float32),
            pltpu.VMEM((rows * heads, feats), jnp.float32),
        ],
        compiler_params=pltpu.CompilerParams(vmem_limit_bytes=40 * 1024 * 1024),
        cost_estimate=pl.CostEstimate(flops=2 * 10**9, bytes_accessed=10**7, transcendentals=0),
    )(
        held,
        other,
        weight,
        query,
        base,
        frame,
        rotations,
        translations,
        table,
        distance,
        pair,
        single,
        local_weight,
        pair_output_weight.reshape(heads * feats, width),
        single_norm_gain,
        left_pair_weight,
        right_pair_weight,
    )
    velocity_rows = jnp.transpose(frame_velocity_weight)
    rot_out, trans_out = pl.pallas_call(
        frame_kernel,
        in_specs=in_vmem(5),
        out_specs=tuple(in_vmem(2)),
        out_shape=(
            jax.ShapeDtypeStruct((3, 3, rows), jnp.float32),
            jax.ShapeDtypeStruct((3, rows), jnp.float32),
        ),
        scratch_shapes=[pltpu.VMEM((16, total), jnp.float32)],
        compiler_params=pltpu.CompilerParams(vmem_limit_bytes=4 * 1024 * 1024),
        cost_estimate=pl.CostEstimate(flops=10**6, bytes_accessed=10**5, transcendentals=0),
    )(
        table,
        single_copy,
        velocity_rows,
        rotations,
        translations,
    )
    return single_out, rot_out, trans_out, left_proj, right_proj, table, 1, pair


def attend_split(
    single,
    pair,
    rotations,
    translations,
    residue_chain_index,
    residue_move_mask,
    timestep,
    single_projection_weight,
    head_bias_weight,
    head_distance_weight,
    chain_logit_offset,
    local_output_weight,
    pair_output_weight,
    single_norm_gain,
    frame_velocity_weight,
    left_pair_weight,
    right_pair_weight,
):
    rows_dev = single.shape[0]
    col_count = pair.shape[1]
    total = rotations.shape[2]
    heads_here = single_projection_weight.shape[1]
    row_start = lax.axis_index("res") * rows_dev
    rot_all = jnp.transpose(rotations, (2, 0, 1))
    trans_all = jnp.transpose(translations)
    rot_own = lax.dynamic_slice_in_dim(rot_all, row_start, rows_dev, 0)
    trans_own = lax.dynamic_slice_in_dim(trans_all, row_start, rows_dev, 0)
    own_chain = lax.dynamic_slice_in_dim(residue_chain_index, row_start, rows_dev, 0)
    offset = 3 * HEAD_FEATURES
    feat_count = 2 * HEAD_FEATURES + 3 * PQ + 3 * PV
    count = total // rows_dev
    every_single = sorted_blocks(*gather_blocks(single, count)[:2]).reshape(total, -1)
    every_proj = jnp.einsum(
        "nd,dhf->nhf", every_single, single_projection_weight, preferred_element_type=jnp.float32
    )
    projected = lax.dynamic_slice_in_dim(every_proj, row_start, rows_dev, 0)
    packed_projection = key_features(every_proj, rot_all, trans_all)
    packed_projection = packed_projection.reshape(total, heads_here, feat_count)
    query_values = projected[:, :, 0:HEAD_FEATURES].astype(jnp.bfloat16)
    query_flattened = to_global(
        projected[:, :, offset : offset + 3 * PQ], rot_own, trans_own, PQ
    ).reshape(rows_dev, heads_here, 3 * PQ)
    bias_local = jnp.einsum(
        "rjc,ch->rhj", pair, head_bias_weight, preferred_element_type=jnp.float32
    ).astype(jnp.bfloat16)
    pair_head_bias = lax.all_to_all(
        bias_local, "head", split_axis=1, concat_axis=2, tiled=True
    ).astype(jnp.float32)
    within_chain = (own_chain[:, None] == residue_chain_index[None, :]).astype(jnp.float32)
    logit_matrix = local_logit_rows(
        query_values,
        query_flattened,
        packed_projection,
        pair_head_bias,
        within_chain,
        head_distance_weight,
        chain_logit_offset,
        residue_move_mask > 0,
    )
    peak = jnp.max(logit_matrix, axis=-1, keepdims=True)
    exponent = jnp.exp(logit_matrix - peak)
    attention = rounded(exponent / jnp.sum(exponent, axis=-1, keepdims=True))
    scalar_out = jnp.einsum(
        "rhn,nhc->rhc",
        attention,
        packed_projection[:, :, HEAD_FEATURES : 2 * HEAD_FEATURES],
        preferred_element_type=jnp.float32,
    )
    point_global = jnp.einsum(
        "rhn,nhp->rhp",
        attention.astype(jnp.float32),
        packed_projection[:, :, 2 * HEAD_FEATURES + 3 * PQ :].astype(jnp.float32),
        precision=HIGHEST,
    )
    update_local = local_points(scalar_out, point_global, rot_own, trans_own, local_output_weight)
    attention_cols = lax.all_to_all(attention, "head", split_axis=2, concat_axis=1, tiled=True)
    pair_attended = jnp.einsum(
        "rhj,rjc->rhc", attention_cols, pair, preferred_element_type=jnp.float32
    )
    update_pair = jnp.einsum(
        "rhc,hcd->rd", pair_attended, pair_output_weight.astype(jnp.float32), precision=HIGHEST
    )
    update = lax.psum(update_local + update_pair, "head")
    single_out = layer_norm(single.astype(jnp.float32) + update, single_norm_gain).astype(
        jnp.bfloat16
    )
    live_all = (residue_move_mask > 0).astype(jnp.float32)
    live_own = lax.dynamic_slice_in_dim(live_all, row_start, rows_dev, 0)
    step_ratio = 1.0 / (STEPS - timestep[0]).astype(jnp.float32)
    rot_out, trans_out = frame_step(
        single_out, frame_velocity_weight, rot_own, trans_own, live_own, step_ratio
    )
    left_proj = jnp.dot(single_out, left_pair_weight, preferred_element_type=jnp.float32).astype(
        jnp.bfloat16
    )
    right_proj = jnp.dot(single_out, right_pair_weight, preferred_element_type=jnp.float32).astype(
        jnp.bfloat16
    )
    live_rows = residue_move_mask[None]
    return single_out, rot_out, trans_out, left_proj, right_proj, live_rows, 0, pair


def shards(
    single,
    pair,
    rotations,
    translations,
    residue_chain_index,
    residue_move_mask,
    timestep,
    single_projection_weight,
    head_bias_weight,
    head_distance_weight,
    chain_logit_offset,
    local_output_weight,
    pair_output_weight,
    single_norm_gain,
    frame_velocity_weight,
    left_pair_weight,
    right_pair_weight,
    pair_norm_gain,
    transition_hidden_weight,
    transition_middle_weight,
    transition_back_weight,
):
    rows_dev = single.shape[0]
    count = rotations.shape[2] // rows_dev
    whole_heads = lax.axis_size("head") == 1 and count >= 16 and count & (count - 1) == 0
    single_out, rot_out, trans_out, left_proj, right_proj, live_rows, live_at, pair = (
        attend if whole_heads else attend_split
    )(
        single,
        pair,
        rotations,
        translations,
        residue_chain_index,
        residue_move_mask,
        timestep,
        single_projection_weight,
        head_bias_weight,
        head_distance_weight,
        chain_logit_offset,
        local_output_weight,
        pair_output_weight,
        single_norm_gain,
        frame_velocity_weight,
        left_pair_weight,
        right_pair_weight,
    )
    offsets, blocks, _ = gather_blocks(right_proj, count)
    if offsets is None:
        blocks = (blocks,)
    else:
        offsets = offsets + [o ^ 1 for o in offsets]
    pair_out = pair_transition(
        pair,
        left_proj,
        residue_move_mask,
        live_rows,
        live_at,
        pair_norm_gain,
        transition_hidden_weight,
        transition_middle_weight,
        transition_back_weight,
        offsets,
        blocks,
    )
    return (single_out, rot_out, trans_out, pair_out)


def solution(mesh):
    placed = (
        P(("batch", "res"), None),
        P(("batch", "res"), "head", None),
        P(None, None, "batch"),
        P(None, "batch"),
        P(),
        P("batch"),
        P(),
        P(None, "head", None),
        P(),
        P("head"),
        P("head"),
        P("head", None, None),
        P(),
        P(),
        P(),
        P(),
        P(),
        P(),
        P(),
        P(),
        P(),
    )
    return jax.shard_map(
        shards,
        mesh=mesh,
        in_specs=placed,
        out_specs=(
            P(("batch", "res"), None),
            P(None, None, ("batch", "res")),
            P(None, ("batch", "res")),
            P(("batch", "res"), "head", None),
        ),
        check_vma=False,
    )
```

```python
import functools
import math

import jax
import jax.numpy as jnp
from jax import lax
from jax.experimental import pallas as pl
from jax.experimental.pallas import tpu as pltpu
from jax.sharding import PartitionSpec as P

HEAD_FEATURES = 16
PQ = 8
PV = 12
STEPS = 8


LOGIT_FACTOR = math.sqrt(1.0 / 3.0)
HIGHEST = lax.Precision.HIGHEST


def rounded(values):
    return lax.optimization_barrier(values.astype(jnp.bfloat16))


def layer_norm(values, gain):
    centre = jnp.mean(values, axis=-1, keepdims=True)
    variance = jnp.mean(jnp.square(values - centre), axis=-1, keepdims=True)
    return (values - centre) * lax.rsqrt(variance + 1e-05) * gain


def to_global(local, rot_cols, trans_cols, npoints):
    rows_here = local.shape[0]
    heads_here = local.shape[1]
    points = local.reshape(rows_here, heads_here, npoints, 3)
    turned = jnp.sum(rot_cols[:, None, None, :, :] * points[:, :, :, None, :], axis=-1)
    return turned + trans_cols[:, None, None, :]


def key_features(projected, rot_cols, trans_cols):
    rows_here = projected.shape[0]
    heads_here = projected.shape[1]
    offset = 3 * HEAD_FEATURES
    key_points = to_global(
        projected[:, :, offset + 3 * PQ : offset + 6 * PQ], rot_cols, trans_cols, PQ
    )
    value_points = to_global(projected[:, :, offset + 6 * PQ :], rot_cols, trans_cols, PV)
    packed_projection = jnp.concatenate(
        [
            projected[:, :, HEAD_FEATURES : 3 * HEAD_FEATURES],
            key_points.reshape(rows_here, heads_here, 3 * PQ),
            value_points.reshape(rows_here, heads_here, 3 * PV),
        ],
        axis=-1,
    )
    return rounded(
        packed_projection.reshape(rows_here, heads_here * (2 * HEAD_FEATURES + 3 * PQ + 3 * PV))
    )


def hat_matrix(vectors):
    comp_x = vectors[:, 0]
    comp_y = vectors[:, 1]
    comp_z = vectors[:, 2]
    zeros_col = jnp.zeros_like(comp_x)
    first_row = jnp.stack([zeros_col, -comp_z, comp_y], -1)
    second_row = jnp.stack([comp_z, zeros_col, -comp_x], -1)
    third_row = jnp.stack([-comp_y, comp_x, zeros_col], -1)
    return jnp.stack([first_row, second_row, third_row], 1)


def frame_step(single_out, frame_velocity_weight, rot_cols, trans_cols, live_rows, step_ratio):
    motion = jnp.dot(single_out, frame_velocity_weight, preferred_element_type=jnp.float32)
    rotvec = step_ratio * jnp.tanh(motion[:, 0:3]) * live_rows[:, None]
    velocity = step_ratio * motion[:, 3:6] * live_rows[:, None]
    angle_sq = jnp.sum(jnp.square(rotvec), -1)
    coef_a = jnp.zeros_like(angle_sq)
    coef_b = jnp.zeros_like(angle_sq)
    coef_c = jnp.zeros_like(angle_sq)
    powers = jnp.ones_like(angle_sq)
    for order in range(8):
        parity = (-1.0) ** order
        coef_a = coef_a + powers * (parity / float(math.factorial(2 * order + 1)))
        coef_b = coef_b + powers * (parity / float(math.factorial(2 * order + 2)))
        coef_c = coef_c + powers * (parity / float(math.factorial(2 * order + 3)))
        powers = powers * angle_sq
    cross_mat = hat_matrix(rotvec)
    cross_sq = jnp.einsum("nab,nbc->nac", cross_mat, cross_mat, precision=HIGHEST)
    identity = jnp.eye(3, dtype=jnp.float32)[None]
    turn = identity + coef_a[:, None, None] * cross_mat + coef_b[:, None, None] * cross_sq
    jacobian = identity + coef_b[:, None, None] * cross_mat + coef_c[:, None, None] * cross_sq
    new_rot = jnp.einsum("nab,nbc->nac", rot_cols, turn, precision=HIGHEST)
    moved = jnp.einsum("nab,nb->na", jacobian, velocity, precision=HIGHEST)
    new_trans = trans_cols + jnp.einsum("nab,nb->na", rot_cols, moved, precision=HIGHEST)
    return (jnp.transpose(new_rot, (1, 2, 0)), jnp.transpose(new_trans))


def local_logit_rows(
    query_values,
    query_flattened,
    packed_projection,
    pair_head_bias,
    within_chain,
    distance_weight,
    chain_offset,
    key_present,
):
    key_scalar = packed_projection[:, :, 0:HEAD_FEATURES]
    key_flat = packed_projection[:, :, 2 * HEAD_FEATURES : 2 * HEAD_FEATURES + 3 * PQ].astype(
        jnp.float32
    )
    scalar_logit_term = jnp.einsum(
        "rhc,nhc->rhn", query_values, key_scalar, preferred_element_type=jnp.float32
    )
    cross_term = jnp.einsum("rhp,nhp->rhn", query_flattened, key_flat, precision=HIGHEST)
    key_square = jnp.transpose(jnp.sum(jnp.square(key_flat), -1))
    point_distance = (
        jnp.sum(jnp.square(query_flattened), -1)[:, :, None] + key_square[None] - 2.0 * cross_term
    )
    point_term_weight = math.sqrt(2.0 / (9.0 * PQ))
    logit_matrix = LOGIT_FACTOR * (
        scalar_logit_term / math.sqrt(HEAD_FEATURES)
        + pair_head_bias
        + chain_offset[None, :, None] * within_chain[:, None, :]
        - (0.5 * point_term_weight * distance_weight)[None, :, None] * point_distance
    )
    return jnp.where(key_present[None, None, :], logit_matrix, -1000000000.0)


def local_points(scalar_out, point_global, rot_own, trans_own, local_output_weight):
    rows_dev = scalar_out.shape[0]
    heads_here = scalar_out.shape[1]
    point_global = point_global.reshape(rows_dev, heads_here, PV, 3)
    centred = point_global - trans_own[:, None, None, :]
    point_local = jnp.sum(rot_own[:, None, None, :, :] * centred[:, :, :, :, None], axis=-2)
    point_norm = jnp.sqrt(jnp.sum(jnp.square(point_local), -1) + 1.0)
    features = jnp.concatenate(
        [scalar_out, point_local.reshape(rows_dev, heads_here, 3 * PV), point_norm], -1
    )
    return jnp.einsum(
        "rhf,hfd->rd", features, local_output_weight.astype(jnp.float32), precision=HIGHEST
    )


def exchange(block, count, step):
    return lax.ppermute(block, "res", [(k, k ^ step) for k in range(count)])


def gather_most(block, count, tied=(), own=None):
    held, offsets = block[None], [0]
    quarter = count // 4
    step = quarter // 2
    while step > 1:
        other = exchange(held, count, step)
        if own is not None and len(held) == 1:
            held = own[None]
        held = jnp.concatenate([held, other], 0)
        offsets = offsets + [o ^ step for o in offsets]
        step //= 2
    held, tied = lax.optimization_barrier((held, tied))
    parts = [held] + [exchange(held, count, k * quarter) for k in (3, 2, 1)]
    held = jnp.concatenate(parts, 0)
    return [o ^ (k * quarter) for k in (0, 3, 2, 1) for o in offsets], held, tied


def gather_blocks(block, count, tied=()):
    if count < 16 or count & (count - 1):
        return None, lax.all_gather(block, "res", axis=0), tied
    offsets, held, tied = gather_most(block, count, tied)
    return offsets, (held, exchange(held, count, 1)), tied


def sorted_blocks(offsets, blocks):
    if offsets is None:
        return blocks
    held, other = blocks
    entries = [held[e] for e in range(len(offsets))] + [other[e] for e in range(len(offsets))]
    every = dict(zip(offsets + [o ^ 1 for o in offsets], entries))
    both = jnp.stack([every[o] for o in range(len(every))])
    index = lax.axis_index("res")
    bit = 1
    while bit < len(every):
        halves = both.reshape((-1, 2, bit) + held.shape[1:])
        both = jnp.where((index & bit) > 0, halves[:, ::-1], halves).reshape(both.shape)
        bit *= 2
    return both


def transition_kernel(
    rows_block,
    rows_part,
    rows_dev,
    offsets,
    live_at,
    live_ref,
    pair_ref,
    left_ref,
    live_row_ref,
    gain_ref,
    hidden_ref,
    middle_ref,
    back_ref,
    *rest,
):
    block_refs, (out_ref, right_ref, live_cols_ref, centring_ref) = rest[:-4], rest[-4:]
    step = pl.program_id(0)
    cols, feats = pair_ref.shape[1:]
    me = lax.axis_index("res")
    col_start = lax.axis_index("head") * cols
    total = right_ref.shape[0]

    @pl.when(step == 0)
    def _():
        at = 0
        for ref in block_refs:
            for e in range(ref.shape[0]):
                value = ref[e].astype(jnp.float32)
                value = value - jnp.mean(value, axis=-1, keepdims=True)
                owner = me ^ offsets[at] if offsets is not None else at
                at += 1
                right_ref[pl.ds(pl.multiple_of(owner * rows_dev, 8), rows_dev), :] = value
        live_row = live_row_ref[pl.ds(live_at, 1), pl.ds(0, total)].astype(jnp.float32)
        wide = jnp.broadcast_to(live_row, (feats, live_row.shape[1]))
        live_cols_ref[...] = jnp.where(jnp.transpose(wide) > 0, 1.0, 0.0)
        across = lax.broadcasted_iota(jnp.int32, (feats, feats), 0)
        down = lax.broadcasted_iota(jnp.int32, (feats, feats), 1)
        centring_ref[...] = (jnp.where(across == down, 1.0, 0.0) - 1.0 / feats).astype(jnp.bfloat16)

    columns = pl.ds(pl.multiple_of(col_start, 8), cols)
    right = right_ref[columns, :][None]
    live_cols = live_cols_ref[columns, :][None]
    left = left_ref[...].astype(jnp.float32)
    left = left - jnp.mean(left, axis=-1, keepdims=True)
    for first in range(0, rows_block, rows_part):
        at = step * rows_block + first
        pair_rows = pair_ref[pl.ds(at, rows_part)]
        pair = pair_rows.reshape(rows_part * cols, feats)
        centred = jnp.dot(pair, centring_ref[...], preferred_element_type=jnp.float32)
        centred = centred.reshape(rows_part, cols, feats)
        centred = centred + left[first : first + rows_part][:, None, :] + right
        variance = jnp.mean(centred * centred, axis=-1, keepdims=True)
        scale = lax.rsqrt(variance + 1e-05)
        gains = [
            gain_ref[...] * jnp.where(live_ref[me * rows_dev + at + r] > 0, 1.0, 0.0)
            for r in range(rows_part)
        ]
        normed = centred * scale * jnp.stack(gains)
        normed = normed.astype(jnp.bfloat16).reshape(rows_part * cols, feats)
        hidden_one = jnp.dot(normed, hidden_ref[...], preferred_element_type=jnp.float32)
        hidden_one = jnp.maximum(hidden_one.astype(jnp.bfloat16), 0)
        hidden_two = jnp.dot(hidden_one, middle_ref[...], preferred_element_type=jnp.float32)
        hidden_two = jnp.maximum(hidden_two.astype(jnp.bfloat16), 0)
        branch = jnp.dot(hidden_two, back_ref[...], preferred_element_type=jnp.float32)
        branch = branch.reshape(rows_part, cols, feats)
        out_ref[pl.ds(first, rows_part)] = (
            pair_rows.astype(jnp.float32) + live_cols * branch
        ).astype(jnp.bfloat16)


def pair_transition(
    pair, left_proj, move_mask, live_rows, live_at, gain, hidden, middle, back, offsets, blocks
):
    rows_dev, cols, feats = pair.shape
    total = move_mask.shape[0]
    rows_part = math.gcd(rows_dev, max(1, 1536 // cols))
    rows_block = rows_part * math.gcd(rows_dev // rows_part, 3)
    left_wide = left_proj.reshape(rows_dev // rows_block, rows_block, feats)
    whole = lambda *shape: pl.BlockSpec(shape, lambda i: (0,) * len(shape))
    kernel = functools.partial(
        transition_kernel, rows_block, rows_part, rows_dev, offsets, live_at
    )
    macs = rows_dev * cols * (2 * feats * feats + 2 * feats * hidden.shape[1] + hidden.shape[1] ** 2)
    return pl.pallas_call(
        kernel,
        grid=(rows_dev // rows_block,),
        in_specs=[
            pl.BlockSpec(memory_space=pltpu.SMEM),
            pl.BlockSpec(memory_space=pltpu.VMEM),
            pl.BlockSpec((None, rows_block, feats), lambda i: (i, 0, 0)),
            whole(*live_rows.shape),
            whole(1, feats),
            whole(*hidden.shape),
            whole(*middle.shape),
            whole(*back.shape),
        ]
        + [whole(*b.shape) for b in blocks],
        out_specs=pl.BlockSpec((rows_block, cols, feats), lambda i: (i, 0, 0)),
        out_shape=jax.ShapeDtypeStruct(pair.shape, pair.dtype),
        scratch_shapes=[
            pltpu.VMEM((total, feats), jnp.float32),
            pltpu.VMEM((total, feats), jnp.float32),
            pltpu.VMEM((feats, feats), jnp.bfloat16),
        ],
        compiler_params=pltpu.CompilerParams(vmem_limit_bytes=32 * 1024 * 1024),
        cost_estimate=pl.CostEstimate(
            flops=2 * macs, bytes_accessed=2 * pair.size * 2, transcendentals=0
        ),
    )(
        move_mask,
        pair,
        left_wide,
        live_rows,
        gain[None],
        hidden,
        middle,
        back,
        *blocks,
    )


def dot(left, right):
    return jnp.dot(left, right, preferred_element_type=jnp.float32)


def dot_rows(left, right, precision=None):
    return lax.dot_general(
        left, right, (((1,), (1,)), ((), ())), preferred_element_type=jnp.float32, precision=precision
    )


def head_mask(heads, lanes):
    head = lax.broadcasted_iota(jnp.int32, (heads, lanes), 0)
    lane = lax.broadcasted_iota(jnp.int32, (heads, lanes), 1)
    return lax.rem(lane, heads) == head


def as_column(row):
    size = row.shape[1]
    return jnp.sum(jnp.where(head_mask(size, size), row, 0.0), axis=1, keepdims=True)


def halves(values):
    high = values.astype(jnp.bfloat16).astype(jnp.float32)
    return jnp.concatenate([high, values - high], 0).astype(jnp.bfloat16)


def point_rows(weight_ref, offset, npoints, coord):
    return jnp.concatenate([weight_ref[offset + 3 * p + coord] for p in range(npoints)], 0)


def turn(parts, rot, shift):
    return [
        rot[c][0] * parts[0] + rot[c][1] * parts[1] + rot[c][2] * parts[2] + shift[c]
        for c in range(3)
    ]


def copy_kernel(source_ref, out_ref):
    out_ref[...] = source_ref[...]


def bias_kernel(source_ref, pair_ref, out_ref, copy_ref, weight_ref, weight_sem, sems):
    pieces = sems.shape[0]
    count = pair_ref.shape[0] // pieces
    copies = [
        pltpu.make_async_copy(
            pair_ref.at[pl.ds(k * count, count)], copy_ref.at[pl.ds(k * count, count)], sems.at[k]
        )
        for k in range(pieces)
    ]
    weight_copy = pltpu.make_async_copy(source_ref, weight_ref, weight_sem)
    weight_copy.start()
    for copy in copies:
        copy.start()
    weight_copy.wait()
    for k, copy in enumerate(copies):
        copy.wait()
        for r in range(k * count, (k + 1) * count):
            bias = dot_rows(weight_ref[...], copy_ref[r])
            out_ref[r] = bias.astype(jnp.bfloat16).astype(jnp.float32)


def query_kernel(
    chain_ref,
    bias_ref,
    single_ref,
    weight_ref,
    rot_ref,
    trans_ref,
    rows_ref,
    distance_ref,
    offset_ref,
    query_ref,
    base_ref,
    frame_ref,
    table_ref,
):
    rows, heads, total = bias_ref.shape
    me = lax.axis_index("res")
    table_ref[...] = jnp.zeros_like(table_ref)
    for c in range(3):
        for d in range(3):
            table_ref[pl.ds(3 * c + d, 1), :] = rot_ref[c, pl.ds(d, 1), :]
        table_ref[pl.ds(9 + c, 1), :] = trans_ref[pl.ds(c, 1), :]
    row = lax.broadcasted_iota(jnp.int32, (rows, total), 0)
    column = lax.broadcasted_iota(jnp.int32, (rows, total), 1)
    chosen = jnp.where(column == row + me * rows, 1.0, 0.0)
    frame = dot_rows(chosen, table_ref[...], HIGHEST)
    frame_ref[...] = frame
    rot = [[frame[:, 3 * c + d : 3 * c + d + 1] for d in range(3)] for c in range(3)]
    shift = [frame[:, 9 + c : 10 + c] for c in range(3)]

    weight = 0.5 * math.sqrt(2.0 / (9.0 * PQ)) * as_column(distance_ref[...])
    chain_offset = as_column(offset_ref[...])
    single = single_ref[...]
    scalar_rows = weight_ref[pl.ds(0, HEAD_FEATURES)].reshape(HEAD_FEATURES * heads, -1)
    scalar = dot_rows(single, scalar_rows).astype(jnp.bfloat16).astype(jnp.float32)
    scalar = scalar * (1.0 / math.sqrt(HEAD_FEATURES))
    lanes = scalar.shape[1]
    spread = jnp.where(head_mask(heads, lanes)[None], scalar[:, None, :], 0.0)
    query_ref[:, pl.ds(0, lanes)] = spread.reshape(rows * heads, lanes).astype(jnp.bfloat16)
    points = [
        dot_rows(single, point_rows(weight_ref, 3 * HEAD_FEATURES, PQ, c)) for c in range(3)
    ]
    points = turn(points, rot, shift)
    width = PQ * heads
    square = jnp.zeros((rows, heads, width), jnp.float32)
    for c in range(3):
        spread = jnp.where(head_mask(heads, width)[None], points[c][:, None, :], 0.0)
        square = square + spread * spread
        rest = spread * (2.0 * weight)[None]
        for term in range(3):
            part = rest.astype(jnp.bfloat16)
            rest = rest - part.astype(jnp.float32)
            at = lanes + (3 * term + c) * width
            query_ref[:, pl.ds(at, width)] = part.reshape(rows * heads, width)
    square = jnp.sum(square, axis=-1, keepdims=True)
    own_row = rows_ref[pl.ds(0, 1), pl.ds(0, total)]
    for r in range(rows):
        within = jnp.where(own_row == chain_ref[me * rows + r], 1.0, 0.0)
        base_ref[r] = LOGIT_FACTOR * (bias_ref[r] + chain_offset * within - weight * square[r])


def attention_kernel(
    offsets,
    held_ref,
    other_ref,
    weight_ref,
    query_ref,
    base_ref,
    frame_ref,
    rot_ref,
    trans_ref,
    rows_ref,
    distance_ref,
    pair_ref,
    single_ref,
    local_ref,
    pair_weight_ref,
    gain_ref,
    left_ref,
    right_ref,
    out_ref,
    copy_ref,
    left_out_ref,
    right_out_ref,
    every_ref,
    pair_sum_ref,
):
    rows, total, feats = pair_ref.shape
    heads = weight_ref.shape[1]
    me = lax.axis_index("res")
    for ref, step in ((held_ref, 0), (other_ref, 1)):
        for e, o in enumerate(offsets):
            owner = me ^ (o ^ step)
            every_ref[pl.ds(pl.multiple_of(owner * rows, 8), rows), :] = ref[e].astype(jnp.float32)
    every = every_ref[...].astype(jnp.bfloat16)
    rot = [[rot_ref[c, pl.ds(d, 1), :] for d in range(3)] for c in range(3)]
    shift = [trans_ref[pl.ds(c, 1), :] for c in range(3)]

    scalars, key_points = HEAD_FEATURES * heads, PQ * heads
    offset = 3 * HEAD_FEATURES + 3 * PQ
    weight_rows = [weight_ref[pl.ds(HEAD_FEATURES, 2 * HEAD_FEATURES)].reshape(2 * scalars, -1)]
    weight_rows += [point_rows(weight_ref, offset, PQ, c) for c in range(3)]
    offset = offset + 3 * PQ
    weight_rows += [point_rows(weight_ref, offset, PV, c) for c in range(3)]
    projected = dot_rows(jnp.concatenate(weight_rows, 0), every)
    parts, at = [], 0
    for size in [scalars] * 2 + [key_points] * 3 + [PV * heads] * 3:
        parts.append(projected[at : at + size])
        at += size
    keys = parts[0].astype(jnp.bfloat16)
    points = [p.astype(jnp.bfloat16) for p in turn(parts[2:5], rot, shift)]
    square = sum(jnp.square(p.astype(jnp.float32)) for p in points)
    square = jnp.sum(square.reshape(PQ, heads, total), axis=0)
    keys = jnp.concatenate([keys] + 3 * points, 0)
    weight = 0.5 * LOGIT_FACTOR * math.sqrt(2.0 / (9.0 * PQ)) * as_column(distance_ref[...])
    logits = dot(query_ref[...], keys).reshape(rows, heads, total)
    logits = LOGIT_FACTOR * logits + base_ref[...] - (weight * square)[None]
    present = rows_ref[pl.ds(1, 1), pl.ds(0, total)] > 0
    logits = jnp.where(present[None], logits, -1000000000.0)
    logits = logits.reshape(rows * heads, total)
    exponent = jnp.exp(logits - jnp.max(logits, axis=-1, keepdims=True))
    attention = (exponent / jnp.sum(exponent, axis=-1, keepdims=True)).astype(jnp.bfloat16)

    for r in range(rows):
        pair_sum_ref[pl.ds(r * heads, heads), :] = dot(
            attention[r * heads : (r + 1) * heads], pair_ref[r]
        )

    def own_head(values):
        lanes = values.shape[0]
        mixed = dot_rows(attention, values).reshape(rows, heads, lanes)
        return jnp.sum(jnp.where(head_mask(heads, lanes)[None], mixed, 0.0), axis=1)

    scalar_out = own_head(parts[1].astype(jnp.bfloat16))
    points = [own_head(p.astype(jnp.bfloat16)) for p in turn(parts[5:8], rot, shift)]
    frame = frame_ref[...]
    centred = [points[c] - frame[:, 9 + c : 10 + c] for c in range(3)]
    local = [
        sum(frame[:, 3 * c + d : 3 * c + d + 1] * centred[c] for c in range(3)) for d in range(3)
    ]
    norm = jnp.sqrt(sum(jnp.square(v) for v in local) + 1.0)

    def product(values, rows_of_weight):
        return dot(halves(values), rows_of_weight)

    first = HEAD_FEATURES * heads
    update = product(scalar_out, local_ref[pl.ds(0, HEAD_FEATURES)].reshape(first, -1))
    for c in range(3):
        update = update + product(local[c], point_rows(local_ref, HEAD_FEATURES, PV, c))
    norm_rows = local_ref[pl.ds(HEAD_FEATURES + 3 * PV, PV)].reshape(PV * heads, -1)
    update = update + product(norm, norm_rows)
    pair_sum = jnp.concatenate(
        [pair_sum_ref[pl.ds(h, rows, stride=heads), :] for h in range(heads)], 1
    )
    update = update + product(pair_sum, pair_weight_ref[...])
    values = single_ref[...].astype(jnp.float32) + update[:rows] + update[rows:]
    single_out = layer_norm(values, gain_ref[...][None]).astype(jnp.bfloat16)
    out_ref[...] = single_out
    copy_ref[...] = single_out
    left_out_ref[...] = dot(single_out, left_ref[...]).astype(jnp.bfloat16)
    right_out_ref[...] = dot(single_out, right_ref[...]).astype(jnp.bfloat16)


def frame_kernel(
    rows_ref,
    single_ref,
    velocity_ref,
    rot_ref,
    trans_ref,
    rot_out_ref,
    trans_out_ref,
    table_ref,
):
    rows = single_ref.shape[0]
    total = rot_ref.shape[2]
    me = lax.axis_index("res")
    table_ref[...] = jnp.zeros_like(table_ref)
    for c in range(3):
        for d in range(3):
            table_ref[pl.ds(3 * c + d, 1), :] = rot_ref[c, pl.ds(d, 1), :]
        table_ref[pl.ds(9 + c, 1), :] = trans_ref[pl.ds(c, 1), :]
    table_ref[pl.ds(12, 1), :] = jnp.where(rows_ref[pl.ds(1, 1), pl.ds(0, total)] > 0, 1.0, 0.0)
    row = lax.broadcasted_iota(jnp.int32, (rows, total), 0)
    column = lax.broadcasted_iota(jnp.int32, (rows, total), 1)
    chosen = jnp.where(column == row + me * rows, 1.0, 0.0)
    frame = dot_rows(table_ref[...], chosen, HIGHEST)
    motion = dot_rows(velocity_ref[...], single_ref[...])
    live = frame[12:13]
    ratio = 1.0 / (STEPS - rows_ref[pl.ds(2, 1), :].astype(jnp.float32))[:, :rows]
    x, y, z = [ratio * jnp.tanh(motion[c : c + 1]) * live for c in range(3)]
    velocity = [ratio * motion[3 + c : 4 + c] * live for c in range(3)]
    angle_sq = x * x + y * y + z * z
    coefs = [jnp.zeros_like(angle_sq) for _ in range(3)]
    powers = jnp.ones_like(angle_sq)
    for order in range(8):
        parity = (-1.0) ** order
        coefs = [
            coef + powers * (parity / float(math.factorial(2 * order + 1 + k)))
            for k, coef in enumerate(coefs)
        ]
        powers = powers * angle_sq
    zero = jnp.zeros_like(x)
    cross = [[zero, -z, y], [z, zero, -x], [-y, x, zero]]
    square = [[sum(cross[a][b] * cross[b][c] for b in range(3)) for c in range(3)] for a in range(3)]
    one = [[jnp.ones_like(x) if a == b else zero for b in range(3)] for a in range(3)]

    def series(first, second):
        return [
            [one[a][b] + first * cross[a][b] + second * square[a][b] for b in range(3)]
            for a in range(3)
        ]

    turned, jacobian = series(coefs[0], coefs[1]), series(coefs[1], coefs[2])
    rot = [[frame[3 * a + b : 3 * a + b + 1] for b in range(3)] for a in range(3)]
    moved = [sum(jacobian[a][b] * velocity[b] for b in range(3)) for a in range(3)]
    for a in range(3):
        for c in range(3):
            rot_out_ref[a, pl.ds(c, 1), :] = sum(rot[a][b] * turned[b][c] for b in range(3))
        trans_out_ref[pl.ds(a, 1), :] = frame[9 + a : 10 + a] + sum(
            rot[a][b] * moved[b] for b in range(3)
        )


def stacked_rows(*rows):
    longest = max(row.shape[0] for row in rows)
    wide = [
        row if row.shape[0] in (1, longest) else jnp.pad(row, (0, longest - row.shape[0]))
        for row in rows
    ]
    wide = [jnp.broadcast_to(row, (longest,)) for row in wide]
    at = lax.broadcasted_iota(jnp.int32, (len(rows), longest), 0)
    table = jnp.broadcast_to(wide[0][None], (len(rows), longest))
    for k in range(1, len(rows)):
        table = jnp.where(at == k, wide[k][None], table)
    return table


def in_vmem(count):
    return [pl.BlockSpec(memory_space=pltpu.VMEM)] * count


def attend(
    single,
    pair,
    rotations,
    translations,
    residue_chain_index,
    residue_move_mask,
    timestep,
    single_projection_weight,
    head_bias_weight,
    head_distance_weight,
    chain_logit_offset,
    local_output_weight,
    pair_output_weight,
    single_norm_gain,
    frame_velocity_weight,
    left_pair_weight,
    right_pair_weight,
):
    rows, total, feats = pair.shape
    heads = single_projection_weight.shape[1]
    width = single.shape[1]
    table = stacked_rows(residue_chain_index, residue_move_mask, timestep)
    own_rows = pl.pallas_call(
        copy_kernel,
        grid=(1,),
        in_specs=[pl.BlockSpec((rows, width), lambda i: (0, 0))],
        out_specs=pl.BlockSpec(memory_space=pltpu.VMEM),
        out_shape=jax.ShapeDtypeStruct(single.shape, single.dtype),
        compiler_params=pltpu.CompilerParams(vmem_limit_bytes=2 * 1024 * 1024),
        cost_estimate=pl.CostEstimate(flops=0, bytes_accessed=10**5, transcendentals=0),
    )(single)
    offsets, held, table = gather_most(single, total // rows, table, own_rows)
    weight = jnp.transpose(single_projection_weight, (2, 1, 0))
    local_weight = jnp.transpose(local_output_weight, (1, 0, 2))
    distance = head_distance_weight[None]
    depth = heads * (HEAD_FEATURES + 9 * PQ)
    bias, pair = pl.pallas_call(
        bias_kernel,
        in_specs=[
            pl.BlockSpec(memory_space=pl.ANY),
            pl.BlockSpec(memory_space=pl.ANY),
        ],
        out_specs=tuple(in_vmem(2)),
        out_shape=(
            jax.ShapeDtypeStruct((rows, heads, total), jnp.float32),
            jax.ShapeDtypeStruct(pair.shape, pair.dtype),
        ),
        scratch_shapes=[
            pltpu.VMEM((heads, feats), head_bias_weight.dtype),
            pltpu.SemaphoreType.DMA,
            pltpu.SemaphoreType.DMA((math.gcd(rows, 3),)),
        ],
        compiler_params=pltpu.CompilerParams(vmem_limit_bytes=51200 * 1024),
        cost_estimate=pl.CostEstimate(flops=10**9, bytes_accessed=6 * 10**6, transcendentals=0),
    )(jnp.transpose(head_bias_weight), pair)
    held, bias, pair, local_weight = lax.optimization_barrier((held, bias, pair, local_weight))
    other = exchange(held, total // rows, 1)
    query, base, frame = pl.pallas_call(
        query_kernel,
        in_specs=[pl.BlockSpec(memory_space=pltpu.SMEM)] + in_vmem(8),
        out_specs=tuple(in_vmem(3)),
        out_shape=(
            jax.ShapeDtypeStruct((rows * heads, depth), jnp.bfloat16),
            jax.ShapeDtypeStruct((rows, heads, total), jnp.float32),
            jax.ShapeDtypeStruct((rows, 16), jnp.float32),
        ),
        scratch_shapes=[pltpu.VMEM((16, total), jnp.float32)],
        compiler_params=pltpu.CompilerParams(vmem_limit_bytes=24 * 1024 * 1024),
        cost_estimate=pl.CostEstimate(flops=10**9, bytes_accessed=6 * 10**6, transcendentals=0),
    )(
        residue_chain_index,
        bias,
        single,
        weight,
        rotations,
        translations,
        table,
        distance,
        chain_logit_offset[None],
    )
    single_out, single_copy, left_proj, right_proj = pl.pallas_call(
        functools.partial(attention_kernel, offsets),
        in_specs=in_vmem(17),
        out_specs=tuple(in_vmem(4)),
        out_shape=(
            jax.ShapeDtypeStruct((rows, width), jnp.bfloat16),
            jax.ShapeDtypeStruct((rows, width), jnp.bfloat16),
            jax.ShapeDtypeStruct((rows, feats), jnp.bfloat16),
            jax.ShapeDtypeStruct((rows, feats), jnp.bfloat16),
        ),
        scratch_shapes=[
            pltpu.VMEM((total, width), jnp.float32),
            pltpu.VMEM((rows * heads, feats), jnp.float32),
        ],
        compiler_params=pltpu.CompilerParams(vmem_limit_bytes=40 * 1024 * 1024),
        cost_estimate=pl.CostEstimate(flops=2 * 10**9, bytes_accessed=10**7, transcendentals=0),
    )(
        held,
        other,
        weight,
        query,
        base,
        frame,
        rotations,
        translations,
        table,
        distance,
        pair,
        single,
        local_weight,
        pair_output_weight.reshape(heads * feats, width),
        single_norm_gain,
        left_pair_weight,
        right_pair_weight,
    )
    velocity_rows = jnp.transpose(frame_velocity_weight)
    rot_out, trans_out = pl.pallas_call(
        frame_kernel,
        in_specs=in_vmem(5),
        out_specs=tuple(in_vmem(2)),
        out_shape=(
            jax.ShapeDtypeStruct((3, 3, rows), jnp.float32),
            jax.ShapeDtypeStruct((3, rows), jnp.float32),
        ),
        scratch_shapes=[pltpu.VMEM((16, total), jnp.float32)],
        compiler_params=pltpu.CompilerParams(vmem_limit_bytes=4 * 1024 * 1024),
        cost_estimate=pl.CostEstimate(flops=10**6, bytes_accessed=10**5, transcendentals=0),
    )(
        table,
        single_copy,
        velocity_rows,
        rotations,
        translations,
    )
    return single_out, rot_out, trans_out, left_proj, right_proj, table, 1, pair


def attend_split(
    single,
    pair,
    rotations,
    translations,
    residue_chain_index,
    residue_move_mask,
    timestep,
    single_projection_weight,
    head_bias_weight,
    head_distance_weight,
    chain_logit_offset,
    local_output_weight,
    pair_output_weight,
    single_norm_gain,
    frame_velocity_weight,
    left_pair_weight,
    right_pair_weight,
):
    rows_dev = single.shape[0]
    col_count = pair.shape[1]
    total = rotations.shape[2]
    heads_here = single_projection_weight.shape[1]
    row_start = lax.axis_index("res") * rows_dev
    rot_all = jnp.transpose(rotations, (2, 0, 1))
    trans_all = jnp.transpose(translations)
    rot_own = lax.dynamic_slice_in_dim(rot_all, row_start, rows_dev, 0)
    trans_own = lax.dynamic_slice_in_dim(trans_all, row_start, rows_dev, 0)
    own_chain = lax.dynamic_slice_in_dim(residue_chain_index, row_start, rows_dev, 0)
    offset = 3 * HEAD_FEATURES
    feat_count = 2 * HEAD_FEATURES + 3 * PQ + 3 * PV
    count = total // rows_dev
    every_single = sorted_blocks(*gather_blocks(single, count)[:2]).reshape(total, -1)
    every_proj = jnp.einsum(
        "nd,dhf->nhf", every_single, single_projection_weight, preferred_element_type=jnp.float32
    )
    projected = lax.dynamic_slice_in_dim(every_proj, row_start, rows_dev, 0)
    packed_projection = key_features(every_proj, rot_all, trans_all)
    packed_projection = packed_projection.reshape(total, heads_here, feat_count)
    query_values = projected[:, :, 0:HEAD_FEATURES].astype(jnp.bfloat16)
    query_flattened = to_global(
        projected[:, :, offset : offset + 3 * PQ], rot_own, trans_own, PQ
    ).reshape(rows_dev, heads_here, 3 * PQ)
    bias_local = jnp.einsum(
        "rjc,ch->rhj", pair, head_bias_weight, preferred_element_type=jnp.float32
    ).astype(jnp.bfloat16)
    pair_head_bias = lax.all_to_all(
        bias_local, "head", split_axis=1, concat_axis=2, tiled=True
    ).astype(jnp.float32)
    within_chain = (own_chain[:, None] == residue_chain_index[None, :]).astype(jnp.float32)
    logit_matrix = local_logit_rows(
        query_values,
        query_flattened,
        packed_projection,
        pair_head_bias,
        within_chain,
        head_distance_weight,
        chain_logit_offset,
        residue_move_mask > 0,
    )
    peak = jnp.max(logit_matrix, axis=-1, keepdims=True)
    exponent = jnp.exp(logit_matrix - peak)
    attention = rounded(exponent / jnp.sum(exponent, axis=-1, keepdims=True))
    scalar_out = jnp.einsum(
        "rhn,nhc->rhc",
        attention,
        packed_projection[:, :, HEAD_FEATURES : 2 * HEAD_FEATURES],
        preferred_element_type=jnp.float32,
    )
    point_global = jnp.einsum(
        "rhn,nhp->rhp",
        attention.astype(jnp.float32),
        packed_projection[:, :, 2 * HEAD_FEATURES + 3 * PQ :].astype(jnp.float32),
        precision=HIGHEST,
    )
    update_local = local_points(scalar_out, point_global, rot_own, trans_own, local_output_weight)
    attention_cols = lax.all_to_all(attention, "head", split_axis=2, concat_axis=1, tiled=True)
    pair_attended = jnp.einsum(
        "rhj,rjc->rhc", attention_cols, pair, preferred_element_type=jnp.float32
    )
    update_pair = jnp.einsum(
        "rhc,hcd->rd", pair_attended, pair_output_weight.astype(jnp.float32), precision=HIGHEST
    )
    update = lax.psum(update_local + update_pair, "head")
    single_out = layer_norm(single.astype(jnp.float32) + update, single_norm_gain).astype(
        jnp.bfloat16
    )
    live_all = (residue_move_mask > 0).astype(jnp.float32)
    live_own = lax.dynamic_slice_in_dim(live_all, row_start, rows_dev, 0)
    step_ratio = 1.0 / (STEPS - timestep[0]).astype(jnp.float32)
    rot_out, trans_out = frame_step(
        single_out, frame_velocity_weight, rot_own, trans_own, live_own, step_ratio
    )
    left_proj = jnp.dot(single_out, left_pair_weight, preferred_element_type=jnp.float32).astype(
        jnp.bfloat16
    )
    right_proj = jnp.dot(single_out, right_pair_weight, preferred_element_type=jnp.float32).astype(
        jnp.bfloat16
    )
    live_rows = residue_move_mask[None]
    return single_out, rot_out, trans_out, left_proj, right_proj, live_rows, 0, pair


def shards(
    single,
    pair,
    rotations,
    translations,
    residue_chain_index,
    residue_move_mask,
    timestep,
    single_projection_weight,
    head_bias_weight,
    head_distance_weight,
    chain_logit_offset,
    local_output_weight,
    pair_output_weight,
    single_norm_gain,
    frame_velocity_weight,
    left_pair_weight,
    right_pair_weight,
    pair_norm_gain,
    transition_hidden_weight,
    transition_middle_weight,
    transition_back_weight,
):
    rows_dev = single.shape[0]
    count = rotations.shape[2] // rows_dev
    whole_heads = lax.axis_size("head") == 1 and count >= 16 and count & (count - 1) == 0
    single_out, rot_out, trans_out, left_proj, right_proj, live_rows, live_at, pair = (
        attend if whole_heads else attend_split
    )(
        single,
        pair,
        rotations,
        translations,
        residue_chain_index,
        residue_move_mask,
        timestep,
        single_projection_weight,
        head_bias_weight,
        head_distance_weight,
        chain_logit_offset,
        local_output_weight,
        pair_output_weight,
        single_norm_gain,
        frame_velocity_weight,
        left_pair_weight,
        right_pair_weight,
    )
    offsets, blocks, _ = gather_blocks(right_proj, count)
    if offsets is None:
        blocks = (blocks,)
    else:
        offsets = offsets + [o ^ 1 for o in offsets]
    pair_out = pair_transition(
        pair,
        left_proj,
        residue_move_mask,
        live_rows,
        live_at,
        pair_norm_gain,
        transition_hidden_weight,
        transition_middle_weight,
        transition_back_weight,
        offsets,
        blocks,
    )
    return (single_out, rot_out, trans_out, pair_out)


def solution(mesh):
    placed = (
        P(("batch", "res"), None),
        P(("batch", "res"), "head", None),
        P(None, None, "batch"),
        P(None, "batch"),
        P(),
        P("batch"),
        P(),
        P(None, "head", None),
        P(),
        P("head"),
        P("head"),
        P("head", None, None),
        P(),
        P(),
        P(),
        P(),
        P(),
        P(),
        P(),
        P(),
        P(),
    )
    return jax.shard_map(
        shards,
        mesh=mesh,
        in_specs=placed,
        out_specs=(
            P(("batch", "res"), None),
            P(None, None, ("batch", "res")),
            P(None, ("batch", "res")),
            P(("batch", "res"), "head", None),
        ),
        check_vma=False,
    )
```

```python
import functools
import math

import jax
import jax.numpy as jnp
from jax import lax
from jax.experimental import pallas as pl
from jax.experimental.pallas import tpu as pltpu
from jax.sharding import PartitionSpec as P

HEAD_FEATURES = 16
PQ = 8
PV = 12
STEPS = 8


LOGIT_FACTOR = math.sqrt(1.0 / 3.0)
HIGHEST = lax.Precision.HIGHEST


def rounded(values):
    return lax.optimization_barrier(values.astype(jnp.bfloat16))


def layer_norm(values, gain):
    centre = jnp.mean(values, axis=-1, keepdims=True)
    variance = jnp.mean(jnp.square(values - centre), axis=-1, keepdims=True)
    return (values - centre) * lax.rsqrt(variance + 1e-05) * gain


def to_global(local, rot_cols, trans_cols, npoints):
    rows_here = local.shape[0]
    heads_here = local.shape[1]
    points = local.reshape(rows_here, heads_here, npoints, 3)
    turned = jnp.sum(rot_cols[:, None, None, :, :] * points[:, :, :, None, :], axis=-1)
    return turned + trans_cols[:, None, None, :]


def key_features(projected, rot_cols, trans_cols):
    rows_here = projected.shape[0]
    heads_here = projected.shape[1]
    offset = 3 * HEAD_FEATURES
    key_points = to_global(
        projected[:, :, offset + 3 * PQ : offset + 6 * PQ], rot_cols, trans_cols, PQ
    )
    value_points = to_global(projected[:, :, offset + 6 * PQ :], rot_cols, trans_cols, PV)
    packed_projection = jnp.concatenate(
        [
            projected[:, :, HEAD_FEATURES : 3 * HEAD_FEATURES],
            key_points.reshape(rows_here, heads_here, 3 * PQ),
            value_points.reshape(rows_here, heads_here, 3 * PV),
        ],
        axis=-1,
    )
    return rounded(
        packed_projection.reshape(rows_here, heads_here * (2 * HEAD_FEATURES + 3 * PQ + 3 * PV))
    )


def hat_matrix(vectors):
    comp_x = vectors[:, 0]
    comp_y = vectors[:, 1]
    comp_z = vectors[:, 2]
    zeros_col = jnp.zeros_like(comp_x)
    first_row = jnp.stack([zeros_col, -comp_z, comp_y], -1)
    second_row = jnp.stack([comp_z, zeros_col, -comp_x], -1)
    third_row = jnp.stack([-comp_y, comp_x, zeros_col], -1)
    return jnp.stack([first_row, second_row, third_row], 1)


def frame_step(single_out, frame_velocity_weight, rot_cols, trans_cols, live_rows, step_ratio):
    motion = jnp.dot(single_out, frame_velocity_weight, preferred_element_type=jnp.float32)
    rotvec = step_ratio * jnp.tanh(motion[:, 0:3]) * live_rows[:, None]
    velocity = step_ratio * motion[:, 3:6] * live_rows[:, None]
    angle_sq = jnp.sum(jnp.square(rotvec), -1)
    coef_a = jnp.zeros_like(angle_sq)
    coef_b = jnp.zeros_like(angle_sq)
    coef_c = jnp.zeros_like(angle_sq)
    powers = jnp.ones_like(angle_sq)
    for order in range(8):
        parity = (-1.0) ** order
        coef_a = coef_a + powers * (parity / float(math.factorial(2 * order + 1)))
        coef_b = coef_b + powers * (parity / float(math.factorial(2 * order + 2)))
        coef_c = coef_c + powers * (parity / float(math.factorial(2 * order + 3)))
        powers = powers * angle_sq
    cross_mat = hat_matrix(rotvec)
    cross_sq = jnp.einsum("nab,nbc->nac", cross_mat, cross_mat, precision=HIGHEST)
    identity = jnp.eye(3, dtype=jnp.float32)[None]
    turn = identity + coef_a[:, None, None] * cross_mat + coef_b[:, None, None] * cross_sq
    jacobian = identity + coef_b[:, None, None] * cross_mat + coef_c[:, None, None] * cross_sq
    new_rot = jnp.einsum("nab,nbc->nac", rot_cols, turn, precision=HIGHEST)
    moved = jnp.einsum("nab,nb->na", jacobian, velocity, precision=HIGHEST)
    new_trans = trans_cols + jnp.einsum("nab,nb->na", rot_cols, moved, precision=HIGHEST)
    return (jnp.transpose(new_rot, (1, 2, 0)), jnp.transpose(new_trans))


def local_logit_rows(
    query_values,
    query_flattened,
    packed_projection,
    pair_head_bias,
    within_chain,
    distance_weight,
    chain_offset,
    key_present,
):
    key_scalar = packed_projection[:, :, 0:HEAD_FEATURES]
    key_flat = packed_projection[:, :, 2 * HEAD_FEATURES : 2 * HEAD_FEATURES + 3 * PQ].astype(
        jnp.float32
    )
    scalar_logit_term = jnp.einsum(
        "rhc,nhc->rhn", query_values, key_scalar, preferred_element_type=jnp.float32
    )
    cross_term = jnp.einsum("rhp,nhp->rhn", query_flattened, key_flat, precision=HIGHEST)
    key_square = jnp.transpose(jnp.sum(jnp.square(key_flat), -1))
    point_distance = (
        jnp.sum(jnp.square(query_flattened), -1)[:, :, None] + key_square[None] - 2.0 * cross_term
    )
    point_term_weight = math.sqrt(2.0 / (9.0 * PQ))
    logit_matrix = LOGIT_FACTOR * (
        scalar_logit_term / math.sqrt(HEAD_FEATURES)
        + pair_head_bias
        + chain_offset[None, :, None] * within_chain[:, None, :]
        - (0.5 * point_term_weight * distance_weight)[None, :, None] * point_distance
    )
    return jnp.where(key_present[None, None, :], logit_matrix, -1000000000.0)


def local_points(scalar_out, point_global, rot_own, trans_own, local_output_weight):
    rows_dev = scalar_out.shape[0]
    heads_here = scalar_out.shape[1]
    point_global = point_global.reshape(rows_dev, heads_here, PV, 3)
    centred = point_global - trans_own[:, None, None, :]
    point_local = jnp.sum(rot_own[:, None, None, :, :] * centred[:, :, :, :, None], axis=-2)
    point_norm = jnp.sqrt(jnp.sum(jnp.square(point_local), -1) + 1.0)
    features = jnp.concatenate(
        [scalar_out, point_local.reshape(rows_dev, heads_here, 3 * PV), point_norm], -1
    )
    return jnp.einsum(
        "rhf,hfd->rd", features, local_output_weight.astype(jnp.float32), precision=HIGHEST
    )


def exchange(block, count, step):
    return lax.ppermute(block, "res", [(k, k ^ step) for k in range(count)])


def gather_most(block, count, tied=(), own=None):
    held, offsets = block[None], [0]
    quarter = count // 4
    step = quarter // 2
    while step > 1:
        other = exchange(held, count, step)
        if own is not None and len(held) == 1:
            held = own[None]
        held = jnp.concatenate([held, other], 0)
        offsets = offsets + [o ^ step for o in offsets]
        step //= 2
    held, tied = lax.optimization_barrier((held, tied))
    parts = [held] + [exchange(held, count, k * quarter) for k in (3, 2, 1)]
    held = jnp.concatenate(parts, 0)
    return [o ^ (k * quarter) for k in (0, 3, 2, 1) for o in offsets], held, tied


def gather_blocks(block, count, tied=()):
    if count < 16 or count & (count - 1):
        return None, lax.all_gather(block, "res", axis=0), tied
    offsets, held, tied = gather_most(block, count, tied)
    return offsets, (held, exchange(held, count, 1)), tied


def sorted_blocks(offsets, blocks):
    if offsets is None:
        return blocks
    held, other = blocks
    entries = [held[e] for e in range(len(offsets))] + [other[e] for e in range(len(offsets))]
    every = dict(zip(offsets + [o ^ 1 for o in offsets], entries))
    both = jnp.stack([every[o] for o in range(len(every))])
    index = lax.axis_index("res")
    bit = 1
    while bit < len(every):
        halves = both.reshape((-1, 2, bit) + held.shape[1:])
        both = jnp.where((index & bit) > 0, halves[:, ::-1], halves).reshape(both.shape)
        bit *= 2
    return both


def transition_kernel(
    rows_block,
    rows_part,
    rows_dev,
    offsets,
    live_at,
    live_ref,
    pair_ref,
    left_ref,
    live_row_ref,
    gain_ref,
    hidden_ref,
    middle_ref,
    back_ref,
    *rest,
):
    block_refs, (out_ref, right_ref, live_cols_ref, centring_ref) = rest[:-4], rest[-4:]
    step = pl.program_id(0)
    cols, feats = pair_ref.shape[1:]
    me = lax.axis_index("res")
    col_start = lax.axis_index("head") * cols
    total = right_ref.shape[0]

    @pl.when(step == 0)
    def _():
        at = 0
        for ref in block_refs:
            for e in range(ref.shape[0]):
                value = ref[e].astype(jnp.float32)
                value = value - jnp.mean(value, axis=-1, keepdims=True)
                owner = me ^ offsets[at] if offsets is not None else at
                at += 1
                right_ref[pl.ds(pl.multiple_of(owner * rows_dev, 8), rows_dev), :] = value
        live_row = live_row_ref[pl.ds(live_at, 1), pl.ds(0, total)].astype(jnp.float32)
        wide = jnp.broadcast_to(live_row, (feats, live_row.shape[1]))
        live_cols_ref[...] = jnp.where(jnp.transpose(wide) > 0, 1.0, 0.0)
        across = lax.broadcasted_iota(jnp.int32, (feats, feats), 0)
        down = lax.broadcasted_iota(jnp.int32, (feats, feats), 1)
        centring_ref[...] = (jnp.where(across == down, 1.0, 0.0) - 1.0 / feats).astype(jnp.bfloat16)

    columns = pl.ds(pl.multiple_of(col_start, 8), cols)
    right = right_ref[columns, :][None]
    live_cols = live_cols_ref[columns, :][None]
    left = left_ref[...].astype(jnp.float32)
    left = left - jnp.mean(left, axis=-1, keepdims=True)
    for first in range(0, rows_block, rows_part):
        at = step * rows_block + first
        pair_rows = pair_ref[pl.ds(at, rows_part)]
        pair = pair_rows.reshape(rows_part * cols, feats)
        centred = jnp.dot(pair, centring_ref[...], preferred_element_type=jnp.float32)
        centred = centred.reshape(rows_part, cols, feats)
        centred = centred + left[first : first + rows_part][:, None, :] + right
        variance = jnp.mean(centred * centred, axis=-1, keepdims=True)
        scale = lax.rsqrt(variance + 1e-05)
        gains = [
            gain_ref[...] * jnp.where(live_ref[me * rows_dev + at + r] > 0, 1.0, 0.0)
            for r in range(rows_part)
        ]
        normed = centred * scale * jnp.stack(gains)
        normed = normed.astype(jnp.bfloat16).reshape(rows_part * cols, feats)
        hidden_one = jnp.dot(normed, hidden_ref[...], preferred_element_type=jnp.float32)
        hidden_one = jnp.maximum(hidden_one.astype(jnp.bfloat16), 0)
        hidden_two = jnp.dot(hidden_one, middle_ref[...], preferred_element_type=jnp.float32)
        hidden_two = jnp.maximum(hidden_two.astype(jnp.bfloat16), 0)
        branch = jnp.dot(hidden_two, back_ref[...], preferred_element_type=jnp.float32)
        branch = branch.reshape(rows_part, cols, feats)
        out_ref[pl.ds(first, rows_part)] = (
            pair_rows.astype(jnp.float32) + live_cols * branch
        ).astype(jnp.bfloat16)


def pair_transition(
    pair, left_proj, move_mask, live_rows, live_at, gain, hidden, middle, back, offsets, blocks
):
    rows_dev, cols, feats = pair.shape
    total = move_mask.shape[0]
    rows_part = math.gcd(rows_dev, max(1, 1536 // cols))
    rows_block = rows_part * math.gcd(rows_dev // rows_part, 3)
    left_wide = left_proj.reshape(rows_dev // rows_block, rows_block, feats)
    whole = lambda *shape: pl.BlockSpec(shape, lambda i: (0,) * len(shape))
    kernel = functools.partial(
        transition_kernel, rows_block, rows_part, rows_dev, offsets, live_at
    )
    macs = rows_dev * cols * (2 * feats * feats + 2 * feats * hidden.shape[1] + hidden.shape[1] ** 2)
    return pl.pallas_call(
        kernel,
        grid=(rows_dev // rows_block,),
        in_specs=[
            pl.BlockSpec(memory_space=pltpu.SMEM),
            pl.BlockSpec(memory_space=pltpu.VMEM),
            pl.BlockSpec((None, rows_block, feats), lambda i: (i, 0, 0)),
            whole(*live_rows.shape),
            whole(1, feats),
            whole(*hidden.shape),
            whole(*middle.shape),
            whole(*back.shape),
        ]
        + [whole(*b.shape) for b in blocks],
        out_specs=pl.BlockSpec((rows_block, cols, feats), lambda i: (i, 0, 0)),
        out_shape=jax.ShapeDtypeStruct(pair.shape, pair.dtype),
        scratch_shapes=[
            pltpu.VMEM((total, feats), jnp.float32),
            pltpu.VMEM((total, feats), jnp.float32),
            pltpu.VMEM((feats, feats), jnp.bfloat16),
        ],
        compiler_params=pltpu.CompilerParams(vmem_limit_bytes=32 * 1024 * 1024),
        cost_estimate=pl.CostEstimate(
            flops=2 * macs, bytes_accessed=2 * pair.size * 2, transcendentals=0
        ),
    )(
        move_mask,
        pair,
        left_wide,
        live_rows,
        gain[None],
        hidden,
        middle,
        back,
        *blocks,
    )


def dot(left, right):
    return jnp.dot(left, right, preferred_element_type=jnp.float32)


def dot_rows(left, right, precision=None):
    return lax.dot_general(
        left, right, (((1,), (1,)), ((), ())), preferred_element_type=jnp.float32, precision=precision
    )


def head_mask(heads, lanes):
    head = lax.broadcasted_iota(jnp.int32, (heads, lanes), 0)
    lane = lax.broadcasted_iota(jnp.int32, (heads, lanes), 1)
    return lax.rem(lane, heads) == head


def as_column(row):
    size = row.shape[1]
    return jnp.sum(jnp.where(head_mask(size, size), row, 0.0), axis=1, keepdims=True)


def halves(values):
    high = values.astype(jnp.bfloat16).astype(jnp.float32)
    return jnp.concatenate([high, values - high], 0).astype(jnp.bfloat16)


def point_rows(weight_ref, offset, npoints, coord):
    return jnp.concatenate([weight_ref[offset + 3 * p + coord] for p in range(npoints)], 0)


def turn(parts, rot, shift):
    return [
        rot[c][0] * parts[0] + rot[c][1] * parts[1] + rot[c][2] * parts[2] + shift[c]
        for c in range(3)
    ]


def copy_kernel(source_ref, weight_ref, out_ref, weight_out_ref):
    out_ref[...] = source_ref[...]
    weight_out_ref[...] = weight_ref[...]


def bias_kernel(weight_ref, pair_ref, out_ref, copy_ref, sems):
    pieces = sems.shape[0]
    count = pair_ref.shape[0] // pieces
    copies = [
        pltpu.make_async_copy(
            pair_ref.at[pl.ds(k * count, count)], copy_ref.at[pl.ds(k * count, count)], sems.at[k]
        )
        for k in range(pieces)
    ]
    for copy in copies:
        copy.start()
    for k, copy in enumerate(copies):
        copy.wait()
        for r in range(k * count, (k + 1) * count):
            bias = dot_rows(weight_ref[...], copy_ref[r])
            out_ref[r] = bias.astype(jnp.bfloat16).astype(jnp.float32)


def query_kernel(
    chain_ref,
    bias_ref,
    single_ref,
    weight_ref,
    rot_ref,
    trans_ref,
    rows_ref,
    distance_ref,
    offset_ref,
    query_ref,
    base_ref,
    frame_ref,
    table_ref,
):
    rows, heads, total = bias_ref.shape
    me = lax.axis_index("res")
    table_ref[...] = jnp.zeros_like(table_ref)
    for c in range(3):
        for d in range(3):
            table_ref[pl.ds(3 * c + d, 1), :] = rot_ref[c, pl.ds(d, 1), :]
        table_ref[pl.ds(9 + c, 1), :] = trans_ref[pl.ds(c, 1), :]
    row = lax.broadcasted_iota(jnp.int32, (rows, total), 0)
    column = lax.broadcasted_iota(jnp.int32, (rows, total), 1)
    chosen = jnp.where(column == row + me * rows, 1.0, 0.0)
    frame = dot_rows(chosen, table_ref[...], HIGHEST)
    frame_ref[...] = frame
    rot = [[frame[:, 3 * c + d : 3 * c + d + 1] for d in range(3)] for c in range(3)]
    shift = [frame[:, 9 + c : 10 + c] for c in range(3)]

    weight = 0.5 * math.sqrt(2.0 / (9.0 * PQ)) * as_column(distance_ref[...])
    chain_offset = as_column(offset_ref[...])
    single = single_ref[...]
    scalar_rows = weight_ref[pl.ds(0, HEAD_FEATURES)].reshape(HEAD_FEATURES * heads, -1)
    scalar = dot_rows(single, scalar_rows).astype(jnp.bfloat16).astype(jnp.float32)
    scalar = scalar * (1.0 / math.sqrt(HEAD_FEATURES))
    lanes = scalar.shape[1]
    spread = jnp.where(head_mask(heads, lanes)[None], scalar[:, None, :], 0.0)
    query_ref[:, pl.ds(0, lanes)] = spread.reshape(rows * heads, lanes).astype(jnp.bfloat16)
    points = [
        dot_rows(single, point_rows(weight_ref, 3 * HEAD_FEATURES, PQ, c)) for c in range(3)
    ]
    points = turn(points, rot, shift)
    width = PQ * heads
    square = jnp.zeros((rows, heads, width), jnp.float32)
    for c in range(3):
        spread = jnp.where(head_mask(heads, width)[None], points[c][:, None, :], 0.0)
        square = square + spread * spread
        rest = spread * (2.0 * weight)[None]
        for term in range(3):
            part = rest.astype(jnp.bfloat16)
            rest = rest - part.astype(jnp.float32)
            at = lanes + (3 * term + c) * width
            query_ref[:, pl.ds(at, width)] = part.reshape(rows * heads, width)
    square = jnp.sum(square, axis=-1, keepdims=True)
    own_row = rows_ref[pl.ds(0, 1), pl.ds(0, total)]
    for r in range(rows):
        within = jnp.where(own_row == chain_ref[me * rows + r], 1.0, 0.0)
        base_ref[r] = LOGIT_FACTOR * (bias_ref[r] + chain_offset * within - weight * square[r])


def attention_kernel(
    offsets,
    held_ref,
    other_ref,
    weight_ref,
    query_ref,
    base_ref,
    frame_ref,
    rot_ref,
    trans_ref,
    rows_ref,
    distance_ref,
    pair_ref,
    single_ref,
    local_ref,
    pair_weight_ref,
    gain_ref,
    left_ref,
    right_ref,
    out_ref,
    copy_ref,
    left_out_ref,
    right_out_ref,
    every_ref,
    pair_sum_ref,
):
    rows, total, feats = pair_ref.shape
    heads = weight_ref.shape[1]
    me = lax.axis_index("res")
    for ref, step in ((held_ref, 0), (other_ref, 1)):
        for e, o in enumerate(offsets):
            owner = me ^ (o ^ step)
            every_ref[pl.ds(pl.multiple_of(owner * rows, 8), rows), :] = ref[e].astype(jnp.float32)
    every = every_ref[...].astype(jnp.bfloat16)
    rot = [[rot_ref[c, pl.ds(d, 1), :] for d in range(3)] for c in range(3)]
    shift = [trans_ref[pl.ds(c, 1), :] for c in range(3)]

    scalars, key_points = HEAD_FEATURES * heads, PQ * heads
    offset = 3 * HEAD_FEATURES + 3 * PQ
    weight_rows = [weight_ref[pl.ds(HEAD_FEATURES, 2 * HEAD_FEATURES)].reshape(2 * scalars, -1)]
    weight_rows += [point_rows(weight_ref, offset, PQ, c) for c in range(3)]
    offset = offset + 3 * PQ
    weight_rows += [point_rows(weight_ref, offset, PV, c) for c in range(3)]
    projected = dot_rows(jnp.concatenate(weight_rows, 0), every)
    parts, at = [], 0
    for size in [scalars] * 2 + [key_points] * 3 + [PV * heads] * 3:
        parts.append(projected[at : at + size])
        at += size
    keys = parts[0].astype(jnp.bfloat16)
    points = [p.astype(jnp.bfloat16) for p in turn(parts[2:5], rot, shift)]
    square = sum(jnp.square(p.astype(jnp.float32)) for p in points)
    square = jnp.sum(square.reshape(PQ, heads, total), axis=0)
    keys = jnp.concatenate([keys] + 3 * points, 0)
    weight = 0.5 * LOGIT_FACTOR * math.sqrt(2.0 / (9.0 * PQ)) * as_column(distance_ref[...])
    logits = dot(query_ref[...], keys).reshape(rows, heads, total)
    logits = LOGIT_FACTOR * logits + base_ref[...] - (weight * square)[None]
    present = rows_ref[pl.ds(1, 1), pl.ds(0, total)] > 0
    logits = jnp.where(present[None], logits, -1000000000.0)
    logits = logits.reshape(rows * heads, total)
    exponent = jnp.exp(logits - jnp.max(logits, axis=-1, keepdims=True))
    attention = (exponent / jnp.sum(exponent, axis=-1, keepdims=True)).astype(jnp.bfloat16)

    for r in range(rows):
        pair_sum_ref[pl.ds(r * heads, heads), :] = dot(
            attention[r * heads : (r + 1) * heads], pair_ref[r]
        )

    def own_head(values):
        lanes = values.shape[0]
        mixed = dot_rows(attention, values).reshape(rows, heads, lanes)
        return jnp.sum(jnp.where(head_mask(heads, lanes)[None], mixed, 0.0), axis=1)

    scalar_out = own_head(parts[1].astype(jnp.bfloat16))
    points = [own_head(p.astype(jnp.bfloat16)) for p in turn(parts[5:8], rot, shift)]
    frame = frame_ref[...]
    centred = [points[c] - frame[:, 9 + c : 10 + c] for c in range(3)]
    local = [
        sum(frame[:, 3 * c + d : 3 * c + d + 1] * centred[c] for c in range(3)) for d in range(3)
    ]
    norm = jnp.sqrt(sum(jnp.square(v) for v in local) + 1.0)

    def product(values, rows_of_weight):
        return dot(halves(values), rows_of_weight)

    first = HEAD_FEATURES * heads
    update = product(scalar_out, local_ref[pl.ds(0, HEAD_FEATURES)].reshape(first, -1))
    for c in range(3):
        update = update + product(local[c], point_rows(local_ref, HEAD_FEATURES, PV, c))
    norm_rows = local_ref[pl.ds(HEAD_FEATURES + 3 * PV, PV)].reshape(PV * heads, -1)
    update = update + product(norm, norm_rows)
    pair_sum = jnp.concatenate(
        [pair_sum_ref[pl.ds(h, rows, stride=heads), :] for h in range(heads)], 1
    )
    update = update + product(pair_sum, pair_weight_ref[...])
    values = single_ref[...].astype(jnp.float32) + update[:rows] + update[rows:]
    single_out = layer_norm(values, gain_ref[...][None]).astype(jnp.bfloat16)
    out_ref[...] = single_out
    copy_ref[...] = single_out
    left_out_ref[...] = dot(single_out, left_ref[...]).astype(jnp.bfloat16)
    right_out_ref[...] = dot(single_out, right_ref[...]).astype(jnp.bfloat16)


def frame_kernel(
    rows_ref,
    single_ref,
    velocity_ref,
    rot_ref,
    trans_ref,
    rot_out_ref,
    trans_out_ref,
    table_ref,
):
    rows = single_ref.shape[0]
    total = rot_ref.shape[2]
    me = lax.axis_index("res")
    table_ref[...] = jnp.zeros_like(table_ref)
    for c in range(3):
        for d in range(3):
            table_ref[pl.ds(3 * c + d, 1), :] = rot_ref[c, pl.ds(d, 1), :]
        table_ref[pl.ds(9 + c, 1), :] = trans_ref[pl.ds(c, 1), :]
    table_ref[pl.ds(12, 1), :] = jnp.where(rows_ref[pl.ds(1, 1), pl.ds(0, total)] > 0, 1.0, 0.0)
    row = lax.broadcasted_iota(jnp.int32, (rows, total), 0)
    column = lax.broadcasted_iota(jnp.int32, (rows, total), 1)
    chosen = jnp.where(column == row + me * rows, 1.0, 0.0)
    frame = dot_rows(table_ref[...], chosen, HIGHEST)
    motion = dot_rows(velocity_ref[...], single_ref[...])
    live = frame[12:13]
    ratio = 1.0 / (STEPS - rows_ref[pl.ds(2, 1), :].astype(jnp.float32))[:, :rows]
    x, y, z = [ratio * jnp.tanh(motion[c : c + 1]) * live for c in range(3)]
    velocity = [ratio * motion[3 + c : 4 + c] * live for c in range(3)]
    angle_sq = x * x + y * y + z * z
    coefs = [jnp.zeros_like(angle_sq) for _ in range(3)]
    powers = jnp.ones_like(angle_sq)
    for order in range(8):
        parity = (-1.0) ** order
        coefs = [
            coef + powers * (parity / float(math.factorial(2 * order + 1 + k)))
            for k, coef in enumerate(coefs)
        ]
        powers = powers * angle_sq
    zero = jnp.zeros_like(x)
    cross = [[zero, -z, y], [z, zero, -x], [-y, x, zero]]
    square = [[sum(cross[a][b] * cross[b][c] for b in range(3)) for c in range(3)] for a in range(3)]
    one = [[jnp.ones_like(x) if a == b else zero for b in range(3)] for a in range(3)]

    def series(first, second):
        return [
            [one[a][b] + first * cross[a][b] + second * square[a][b] for b in range(3)]
            for a in range(3)
        ]

    turned, jacobian = series(coefs[0], coefs[1]), series(coefs[1], coefs[2])
    rot = [[frame[3 * a + b : 3 * a + b + 1] for b in range(3)] for a in range(3)]
    moved = [sum(jacobian[a][b] * velocity[b] for b in range(3)) for a in range(3)]
    for a in range(3):
        for c in range(3):
            rot_out_ref[a, pl.ds(c, 1), :] = sum(rot[a][b] * turned[b][c] for b in range(3))
        trans_out_ref[pl.ds(a, 1), :] = frame[9 + a : 10 + a] + sum(
            rot[a][b] * moved[b] for b in range(3)
        )


def stacked_rows(*rows):
    longest = max(row.shape[0] for row in rows)
    wide = [
        row if row.shape[0] in (1, longest) else jnp.pad(row, (0, longest - row.shape[0]))
        for row in rows
    ]
    wide = [jnp.broadcast_to(row, (longest,)) for row in wide]
    at = lax.broadcasted_iota(jnp.int32, (len(rows), longest), 0)
    table = jnp.broadcast_to(wide[0][None], (len(rows), longest))
    for k in range(1, len(rows)):
        table = jnp.where(at == k, wide[k][None], table)
    return table


def in_vmem(count):
    return [pl.BlockSpec(memory_space=pltpu.VMEM)] * count


def attend(
    single,
    pair,
    rotations,
    translations,
    residue_chain_index,
    residue_move_mask,
    timestep,
    single_projection_weight,
    head_bias_weight,
    head_distance_weight,
    chain_logit_offset,
    local_output_weight,
    pair_output_weight,
    single_norm_gain,
    frame_velocity_weight,
    left_pair_weight,
    right_pair_weight,
):
    rows, total, feats = pair.shape
    heads = single_projection_weight.shape[1]
    width = single.shape[1]
    table = stacked_rows(residue_chain_index, residue_move_mask, timestep)
    bias_weight = jnp.transpose(head_bias_weight)
    own_rows, bias_weight = pl.pallas_call(
        copy_kernel,
        grid=(1,),
        in_specs=[
            pl.BlockSpec((rows, width), lambda i: (0, 0)),
            pl.BlockSpec((heads, feats), lambda i: (0, 0)),
        ],
        out_specs=tuple(in_vmem(2)),
        out_shape=(
            jax.ShapeDtypeStruct(single.shape, single.dtype),
            jax.ShapeDtypeStruct(bias_weight.shape, bias_weight.dtype),
        ),
        compiler_params=pltpu.CompilerParams(vmem_limit_bytes=2 * 1024 * 1024),
        cost_estimate=pl.CostEstimate(flops=0, bytes_accessed=10**5, transcendentals=0),
    )(single, bias_weight)
    offsets, held, (table, bias_weight, local_output_weight) = gather_most(
        single, total // rows, (table, bias_weight, local_output_weight), own_rows
    )
    weight = jnp.transpose(single_projection_weight, (2, 1, 0))
    distance = head_distance_weight[None]
    depth = heads * (HEAD_FEATURES + 9 * PQ)
    local_weight = jnp.transpose(local_output_weight, (1, 0, 2))
    bias, pair = pl.pallas_call(
        bias_kernel,
        in_specs=[
            pl.BlockSpec(memory_space=pltpu.VMEM),
            pl.BlockSpec(memory_space=pl.ANY),
        ],
        out_specs=tuple(in_vmem(2)),
        out_shape=(
            jax.ShapeDtypeStruct((rows, heads, total), jnp.float32),
            jax.ShapeDtypeStruct(pair.shape, pair.dtype),
        ),
        scratch_shapes=[pltpu.SemaphoreType.DMA((math.gcd(rows, 3),))],
        compiler_params=pltpu.CompilerParams(vmem_limit_bytes=51200 * 1024),
        cost_estimate=pl.CostEstimate(flops=10**9, bytes_accessed=6 * 10**6, transcendentals=0),
    )(bias_weight, pair)
    held, bias, pair, local_weight = lax.optimization_barrier((held, bias, pair, local_weight))
    other = exchange(held, total // rows, 1)
    query, base, frame = pl.pallas_call(
        query_kernel,
        in_specs=[pl.BlockSpec(memory_space=pltpu.SMEM)] + in_vmem(8),
        out_specs=tuple(in_vmem(3)),
        out_shape=(
            jax.ShapeDtypeStruct((rows * heads, depth), jnp.bfloat16),
            jax.ShapeDtypeStruct((rows, heads, total), jnp.float32),
            jax.ShapeDtypeStruct((rows, 16), jnp.float32),
        ),
        scratch_shapes=[pltpu.VMEM((16, total), jnp.float32)],
        compiler_params=pltpu.CompilerParams(vmem_limit_bytes=24 * 1024 * 1024),
        cost_estimate=pl.CostEstimate(flops=10**9, bytes_accessed=6 * 10**6, transcendentals=0),
    )(
        residue_chain_index,
        bias,
        single,
        weight,
        rotations,
        translations,
        table,
        distance,
        chain_logit_offset[None],
    )
    single_out, single_copy, left_proj, right_proj = pl.pallas_call(
        functools.partial(attention_kernel, offsets),
        in_specs=in_vmem(17),
        out_specs=tuple(in_vmem(4)),
        out_shape=(
            jax.ShapeDtypeStruct((rows, width), jnp.bfloat16),
            jax.ShapeDtypeStruct((rows, width), jnp.bfloat16),
            jax.ShapeDtypeStruct((rows, feats), jnp.bfloat16),
            jax.ShapeDtypeStruct((rows, feats), jnp.bfloat16),
        ),
        scratch_shapes=[
            pltpu.VMEM((total, width), jnp.float32),
            pltpu.VMEM((rows * heads, feats), jnp.float32),
        ],
        compiler_params=pltpu.CompilerParams(vmem_limit_bytes=40 * 1024 * 1024),
        cost_estimate=pl.CostEstimate(flops=2 * 10**9, bytes_accessed=10**7, transcendentals=0),
    )(
        held,
        other,
        weight,
        query,
        base,
        frame,
        rotations,
        translations,
        table,
        distance,
        pair,
        single,
        local_weight,
        pair_output_weight.reshape(heads * feats, width),
        single_norm_gain,
        left_pair_weight,
        right_pair_weight,
    )
    velocity_rows = jnp.transpose(frame_velocity_weight)
    rot_out, trans_out = pl.pallas_call(
        frame_kernel,
        in_specs=in_vmem(5),
        out_specs=tuple(in_vmem(2)),
        out_shape=(
            jax.ShapeDtypeStruct((3, 3, rows), jnp.float32),
            jax.ShapeDtypeStruct((3, rows), jnp.float32),
        ),
        scratch_shapes=[pltpu.VMEM((16, total), jnp.float32)],
        compiler_params=pltpu.CompilerParams(vmem_limit_bytes=4 * 1024 * 1024),
        cost_estimate=pl.CostEstimate(flops=10**6, bytes_accessed=10**5, transcendentals=0),
    )(
        table,
        single_copy,
        velocity_rows,
        rotations,
        translations,
    )
    return single_out, rot_out, trans_out, left_proj, right_proj, table, 1, pair


def attend_split(
    single,
    pair,
    rotations,
    translations,
    residue_chain_index,
    residue_move_mask,
    timestep,
    single_projection_weight,
    head_bias_weight,
    head_distance_weight,
    chain_logit_offset,
    local_output_weight,
    pair_output_weight,
    single_norm_gain,
    frame_velocity_weight,
    left_pair_weight,
    right_pair_weight,
):
    rows_dev = single.shape[0]
    col_count = pair.shape[1]
    total = rotations.shape[2]
    heads_here = single_projection_weight.shape[1]
    row_start = lax.axis_index("res") * rows_dev
    rot_all = jnp.transpose(rotations, (2, 0, 1))
    trans_all = jnp.transpose(translations)
    rot_own = lax.dynamic_slice_in_dim(rot_all, row_start, rows_dev, 0)
    trans_own = lax.dynamic_slice_in_dim(trans_all, row_start, rows_dev, 0)
    own_chain = lax.dynamic_slice_in_dim(residue_chain_index, row_start, rows_dev, 0)
    offset = 3 * HEAD_FEATURES
    feat_count = 2 * HEAD_FEATURES + 3 * PQ + 3 * PV
    count = total // rows_dev
    every_single = sorted_blocks(*gather_blocks(single, count)[:2]).reshape(total, -1)
    every_proj = jnp.einsum(
        "nd,dhf->nhf", every_single, single_projection_weight, preferred_element_type=jnp.float32
    )
    projected = lax.dynamic_slice_in_dim(every_proj, row_start, rows_dev, 0)
    packed_projection = key_features(every_proj, rot_all, trans_all)
    packed_projection = packed_projection.reshape(total, heads_here, feat_count)
    query_values = projected[:, :, 0:HEAD_FEATURES].astype(jnp.bfloat16)
    query_flattened = to_global(
        projected[:, :, offset : offset + 3 * PQ], rot_own, trans_own, PQ
    ).reshape(rows_dev, heads_here, 3 * PQ)
    bias_local = jnp.einsum(
        "rjc,ch->rhj", pair, head_bias_weight, preferred_element_type=jnp.float32
    ).astype(jnp.bfloat16)
    pair_head_bias = lax.all_to_all(
        bias_local, "head", split_axis=1, concat_axis=2, tiled=True
    ).astype(jnp.float32)
    within_chain = (own_chain[:, None] == residue_chain_index[None, :]).astype(jnp.float32)
    logit_matrix = local_logit_rows(
        query_values,
        query_flattened,
        packed_projection,
        pair_head_bias,
        within_chain,
        head_distance_weight,
        chain_logit_offset,
        residue_move_mask > 0,
    )
    peak = jnp.max(logit_matrix, axis=-1, keepdims=True)
    exponent = jnp.exp(logit_matrix - peak)
    attention = rounded(exponent / jnp.sum(exponent, axis=-1, keepdims=True))
    scalar_out = jnp.einsum(
        "rhn,nhc->rhc",
        attention,
        packed_projection[:, :, HEAD_FEATURES : 2 * HEAD_FEATURES],
        preferred_element_type=jnp.float32,
    )
    point_global = jnp.einsum(
        "rhn,nhp->rhp",
        attention.astype(jnp.float32),
        packed_projection[:, :, 2 * HEAD_FEATURES + 3 * PQ :].astype(jnp.float32),
        precision=HIGHEST,
    )
    update_local = local_points(scalar_out, point_global, rot_own, trans_own, local_output_weight)
    attention_cols = lax.all_to_all(attention, "head", split_axis=2, concat_axis=1, tiled=True)
    pair_attended = jnp.einsum(
        "rhj,rjc->rhc", attention_cols, pair, preferred_element_type=jnp.float32
    )
    update_pair = jnp.einsum(
        "rhc,hcd->rd", pair_attended, pair_output_weight.astype(jnp.float32), precision=HIGHEST
    )
    update = lax.psum(update_local + update_pair, "head")
    single_out = layer_norm(single.astype(jnp.float32) + update, single_norm_gain).astype(
        jnp.bfloat16
    )
    live_all = (residue_move_mask > 0).astype(jnp.float32)
    live_own = lax.dynamic_slice_in_dim(live_all, row_start, rows_dev, 0)
    step_ratio = 1.0 / (STEPS - timestep[0]).astype(jnp.float32)
    rot_out, trans_out = frame_step(
        single_out, frame_velocity_weight, rot_own, trans_own, live_own, step_ratio
    )
    left_proj = jnp.dot(single_out, left_pair_weight, preferred_element_type=jnp.float32).astype(
        jnp.bfloat16
    )
    right_proj = jnp.dot(single_out, right_pair_weight, preferred_element_type=jnp.float32).astype(
        jnp.bfloat16
    )
    live_rows = residue_move_mask[None]
    return single_out, rot_out, trans_out, left_proj, right_proj, live_rows, 0, pair


def shards(
    single,
    pair,
    rotations,
    translations,
    residue_chain_index,
    residue_move_mask,
    timestep,
    single_projection_weight,
    head_bias_weight,
    head_distance_weight,
    chain_logit_offset,
    local_output_weight,
    pair_output_weight,
    single_norm_gain,
    frame_velocity_weight,
    left_pair_weight,
    right_pair_weight,
    pair_norm_gain,
    transition_hidden_weight,
    transition_middle_weight,
    transition_back_weight,
):
    rows_dev = single.shape[0]
    count = rotations.shape[2] // rows_dev
    whole_heads = lax.axis_size("head") == 1 and count >= 16 and count & (count - 1) == 0
    single_out, rot_out, trans_out, left_proj, right_proj, live_rows, live_at, pair = (
        attend if whole_heads else attend_split
    )(
        single,
        pair,
        rotations,
        translations,
        residue_chain_index,
        residue_move_mask,
        timestep,
        single_projection_weight,
        head_bias_weight,
        head_distance_weight,
        chain_logit_offset,
        local_output_weight,
        pair_output_weight,
        single_norm_gain,
        frame_velocity_weight,
        left_pair_weight,
        right_pair_weight,
    )
    offsets, blocks, _ = gather_blocks(right_proj, count)
    if offsets is None:
        blocks = (blocks,)
    else:
        offsets = offsets + [o ^ 1 for o in offsets]
    pair_out = pair_transition(
        pair,
        left_proj,
        residue_move_mask,
        live_rows,
        live_at,
        pair_norm_gain,
        transition_hidden_weight,
        transition_middle_weight,
        transition_back_weight,
        offsets,
        blocks,
    )
    return (single_out, rot_out, trans_out, pair_out)


def solution(mesh):
    placed = (
        P(("batch", "res"), None),
        P(("batch", "res"), "head", None),
        P(None, None, "batch"),
        P(None, "batch"),
        P(),
        P("batch"),
        P(),
        P(None, "head", None),
        P(),
        P("head"),
        P("head"),
        P("head", None, None),
        P(),
        P(),
        P(),
        P(),
        P(),
        P(),
        P(),
        P(),
        P(),
    )
    return jax.shard_map(
        shards,
        mesh=mesh,
        in_specs=placed,
        out_specs=(
            P(("batch", "res"), None),
            P(None, None, ("batch", "res")),
            P(None, ("batch", "res")),
            P(("batch", "res"), "head", None),
        ),
        check_vma=False,
    )
```
